32 devices in a mesh: expert: 8 (over z, x), dp: 4 (over y, core).
Axes of the slice: x: 2, y: 2, z: 4, core: 2. Of those that a mesh axis runs over, the one named last changes fastest.
Arguments:
- tokens: bfloat16 [2048, 2048], P(('expert', 'dp')), may hold values from -6 to 6
- routes: int32 [2048, 8], P(('expert', 'dp')), may hold values from 0 to 31, all different within a row; in each aligned block of 64 rows (0 to 63, 64 to 127, ...) at most 20 rows name the same one
- probs: float32 [2048, 8], P(('expert', 'dp')), may hold values from 0.02 to 1
- cotangent: bfloat16 [2048, 2048], P(('expert', 'dp')), may hold values from -6 to 6
- w_gate: bfloat16 [32, 2048, 384], P('expert'), may hold values from -0.125 to 0.125
- w_up: bfloat16 [32, 2048, 384], P('expert'), may hold values from -0.125 to 0.125
- w_down: bfloat16 [32, 2048, 384], P('expert'), may hold values from -0.3125 to 0.3125
Outputs:
- mixed: bfloat16 [2048, 2048], P(('expert', 'dp'))
- token_grad: bfloat16 [2048, 2048], P(('expert', 'dp'))
- prob_grad: float32 [2048, 8], P(('expert', 'dp'))
- gate_grad: bfloat16 [32, 2048, 384], P('expert', 'dp')
- up_grad: bfloat16 [32, 2048, 384], P('expert', 'dp')
- down_grad: bfloat16 [32, 2048, 384], P('expert', 'dp')
The draws below stay inside these ranges and needn't reach their ends.
Inputs may be any that keep to these rules, and one draw needn't show every extreme that they name: `routes`: each row names 8 different experts. Among the 64 rows of one device no expert is named by more than 20 rows, a bound that some block reaches.
All inputs are finite; a program needn't handle non-finite values.
Results may differ from the reference program's by a relative error of at most 0.0095.
Values may be sent and summed in bfloat16 or wider, within the bound.
No kernel may reach another device: no remote copies, remote signals or barrier semaphores. Data moves between devices by JAX's collectives and lax.ppermute only.
A program may use at most 128 MiB of HBM per device.

```python
import math
import jax
import jax.numpy as jnp
import numpy as np
from jax import lax

D = 2048
H = 384
TOP = 8
TOK_DEV = 64
EXPERTS = 32
TOKENS = 2048
CAP = 20
N_EXPERT = 8
N_DP = 4


def level_of(stream_key, dims, cuts, smallest, high):
    gain = 1.0
    for axis_at, shards_of in cuts:
        draws = jax.random.uniform(jax.random.fold_in(jax.random.fold_in(stream_key, 6), axis_at), (shards_of,), jnp.float32, smallest / len(cuts), high / len(cuts))
        gain = gain * jnp.repeat(jnp.exp(draws), dims[axis_at] // shards_of).reshape((-1,) + (1,) * (len(dims) - 1 - axis_at))
    return gain


def deal_out(stream_key, own, number, rows, number_of, top, limit, lean):
    ranking = jax.random.permutation(stream_key, number_of)
    crowded, common = load_shares(number_of, rows * top, limit, lean, True), load_shares(number_of, rows * top, limit, lean, False)
    places = jnp.arange(number_of)

    def named(lengths, rotation):
        used = int((lengths > 0).sum())
        fixed = max(1, used // 4)
        moved = fixed + (places - fixed + rotation * (used - fixed)) % max(1, number_of - fixed)
        return jnp.zeros((number_of,), jnp.int32).at[ranking[jnp.where(places < fixed, places, moved)]].set(jnp.asarray(lengths, jnp.int32))

    lengths = jnp.where(number % 4 == 0, named(crowded, number // 4), named(common, number - number // 4 - 1))
    mixed = jax.random.permutation(jax.random.fold_in(own, 3), number_of)
    source_of, taker = mixed[0:number_of // 2 * 2:2], mixed[1:number_of // 2 * 2:2]
    margin = jnp.minimum(lengths[source_of] - 1, limit - lengths[taker]) // 2
    margin = jnp.where((source_of == ranking[0]) | (taker == ranking[0]) | (lengths[taker] == 0), 0, jnp.maximum(margin, 0))
    moved = jax.random.randint(jax.random.fold_in(own, 4), (number_of // 2,), 0, 1 << 20) % (margin + 1)
    lengths = lengths.at[source_of].add(-moved).at[taker].add(moved)
    labels = jnp.searchsorted(jnp.cumsum(lengths), jnp.arange(rows * top), side="right").astype(jnp.int32)
    listing = labels.reshape(top, rows).T
    listing = listing[jax.random.permutation(jax.random.fold_in(own, 1), rows)]
    rotation = jax.random.randint(jax.random.fold_in(own, 2), (rows, 1), 0, top)
    return jnp.take_along_axis(listing, (jnp.arange(top)[None, :] + rotation) % top, axis=1)


def load_shares(count, total, most, slope, full):
    portions = [(1 << 20) // math.isqrt(standing ** slope) + 1 for standing in range(1, count + 1)]
    largest = most if full else min(most, max(-(-total // count), total * portions[0] // sum(portions)))
    least = 1 if total - largest >= count - 1 else 0
    holding, rest = [largest] + [least] * (count - 1), total - largest - least * (count - 1)
    while rest > 0:
        movable = [i for i in range(1, count) if holding[i] < largest] or [i for i in range(1, count) if holding[i] < most]
        pool, remaining = sum([portions[i] for i in movable]), rest
        for i in movable:
            more = min(most - holding[i], max(1, remaining * portions[i] // pool), rest)
            holding[i] = holding[i] + more
            rest = rest - more
    return np.array(holding)


def normal_values(key, extent, deviation, most, pieces=(), kind=jnp.bfloat16):
    loudness = level_of(key, extent, pieces, -0.22, 0.18) if pieces else 1.0
    values = jax.random.normal(key, extent, jnp.float32) * deviation * loudness
    return jnp.minimum(jnp.maximum(values, -most), most).astype(kind)


def setup_inputs(seed: int = 0) -> dict:
    splits = jax.random.split(jax.random.key(seed), 8)
    tokens = normal_values(splits[0], (TOKENS, D), 1.0, 6.0, ((0, 32),))
    routes_keys = jax.random.split(jax.random.fold_in(splits[1], 1), TOKENS // TOK_DEV)
    routes_turns = jax.random.permutation(jax.random.fold_in(splits[1], 3), TOKENS // TOK_DEV)
    routes = jax.vmap(lambda own, number: deal_out(jax.random.fold_in(splits[1], 2), own, number, TOK_DEV, EXPERTS, TOP, CAP, 2))(routes_keys, routes_turns).reshape((TOKENS, TOP))
    probs = jnp.clip(jnp.exp(math.log(1.0) - 3.912023 * jax.random.uniform(splits[2], (TOKENS, TOP), jnp.float32) ** level_of(splits[2], (TOKENS, TOP), ((0, 32),), -0.2, 0.2)), 0.02, 1.0)
    cotangent = normal_values(splits[3], (TOKENS, D), 1.0, 6.0, ((0, 32),))
    w_gate = normal_values(splits[4], (EXPERTS, D, H), D ** -0.5, 0.125, ((0, 8),))
    w_up = normal_values(splits[5], (EXPERTS, D, H), D ** -0.5, 0.125, ((0, 8),))
    w_down = normal_values(splits[6], (EXPERTS, D, H), H ** -0.5, 0.3125, ((0, 8),))
    return {"tokens": tokens, "routes": routes, "probs": probs, "cotangent": cotangent, "w_gate": w_gate, "w_up": w_up, "w_down": w_down}


def expert_rows(rows_in, upstream, gate_w, up_w, down_w):
    gate_pre = jnp.dot(rows_in, gate_w, preferred_element_type=jnp.float32)
    up_pre = jnp.dot(rows_in, up_w, preferred_element_type=jnp.float32)
    sigmoid_gate = jax.nn.sigmoid(gate_pre)
    active = (gate_pre * sigmoid_gate * up_pre).astype(jnp.bfloat16)
    output = jnp.dot(active, down_w.T, preferred_element_type=jnp.float32).astype(jnp.bfloat16)
    d_active = jnp.dot(upstream, down_w, preferred_element_type=jnp.float32)
    d_gate = (d_active * up_pre * sigmoid_gate * (1.0 + gate_pre * (1.0 - sigmoid_gate))).astype(jnp.bfloat16)
    d_up = (d_active * gate_pre * sigmoid_gate).astype(jnp.bfloat16)
    d_input = (jnp.dot(d_gate, gate_w.T, preferred_element_type=jnp.float32)
               + jnp.dot(d_up, up_w.T, preferred_element_type=jnp.float32)).astype(jnp.bfloat16)
    grad_gate = jnp.dot(rows_in.T, d_gate, preferred_element_type=jnp.float32)
    grad_up = jnp.dot(rows_in.T, d_up, preferred_element_type=jnp.float32)
    grad_down = jnp.dot(upstream.T, active, preferred_element_type=jnp.float32)
    return output, d_input, (grad_gate, grad_up, grad_down)


def round_partial(value):
    return lax.optimization_barrier(value.astype(jnp.bfloat16)).astype(jnp.float32)


def reference(tokens, routes, probs, cotangent, w_gate, w_up, w_down):
    totals = jnp.sum(probs, axis=1, keepdims=True)
    gate_share = probs / totals
    shares_flat = gate_share.reshape(-1)
    flat_expert = routes.reshape(-1).astype(jnp.int32)
    entry_count = TOKENS * TOP
    entry_token = jnp.arange(entry_count, dtype=jnp.int32) // TOP
    replica_of = (entry_token // TOK_DEV) % N_DP
    group_key = (flat_expert * N_DP + replica_of).astype(jnp.int32)
    sort_order = jnp.argsort(group_key, stable=True).astype(jnp.int32)
    group_size = jnp.zeros((EXPERTS * N_DP,), jnp.int32).at[group_key].add(1)
    starts = (jnp.cumsum(group_size) - group_size).astype(jnp.int32)
    row_offset = jnp.arange(N_EXPERT * CAP, dtype=jnp.int32)
    zero_value = jnp.zeros((), jnp.bfloat16)

    def per_expert(state_carry, expert):
        mixed_acc, input_acc, share_acc = state_carry
        gate_w = w_gate[expert]
        up_w = w_up[expert]
        down_w = w_down[expert]
        zero_grad = jnp.zeros((D, H), jnp.float32)
        partials = [zero_grad, zero_grad, zero_grad]
        for replica in range(N_DP):
            group_id = expert * N_DP + replica
            live_row = row_offset < group_size[group_id]
            live_mask = live_row[:, None]
            slot_index = sort_order[jnp.minimum(starts[group_id] + row_offset, entry_count - 1)]
            token_index = slot_index // TOP
            rows_in = jnp.where(live_mask, tokens[token_index], zero_value)
            upstream_row = cotangent[token_index].astype(jnp.float32)
            scaled = (shares_flat[slot_index][:, None] * upstream_row).astype(jnp.bfloat16)
            upstream = jnp.where(live_mask, scaled, zero_value)
            output, d_input, grad_terms = expert_rows(rows_in, upstream, gate_w, up_w, down_w)
            partials = [running + round_partial(addend) for running, addend in zip(partials, grad_terms)]
            out_wide = output.astype(jnp.float32)
            mixed_acc = mixed_acc.at[token_index].add(
                jnp.where(live_mask, shares_flat[slot_index][:, None] * out_wide, 0.0))
            input_acc = input_acc.at[token_index].add(jnp.where(live_mask, d_input.astype(jnp.float32), 0.0))
            share_acc = share_acc.at[slot_index].add(
                jnp.where(live_row, jnp.sum(out_wide * upstream_row, axis=1), 0.0))
        result = tuple(running.astype(jnp.bfloat16) for running in partials)
        return (mixed_acc, input_acc, share_acc), result

    start_state = (jnp.zeros((TOKENS, D), jnp.float32), jnp.zeros((TOKENS, D), jnp.float32),
                   jnp.zeros((entry_count,), jnp.float32))
    final_state, stacked = lax.scan(per_expert, start_state, jnp.arange(EXPERTS, dtype=jnp.int32))
    mixed_acc, input_acc, share_acc = final_state
    share_grad = share_acc.reshape(TOKENS, TOP)
    prob_grad = (share_grad - jnp.sum(gate_share * share_grad, axis=1, keepdims=True)) / totals
    return (mixed_acc.astype(jnp.bfloat16), input_acc.astype(jnp.bfloat16), prob_grad,
            stacked[0], stacked[1], stacked[2])
```

```python
import jax
import jax.numpy as jnp
from jax import lax
from jax.sharding import PartitionSpec as P


F32 = jnp.float32
BF16 = jnp.bfloat16


def swap(value, bit, count):
    return lax.ppermute(value, "dp", [(i, i ^ bit) for i in range(count)])


def bits_of(count):
    bit = count // 2
    while bit:
        yield bit
        bit //= 2


def spread_columns(rows, my_dp, count):
    held = rows[None]
    for bit in bits_of(count):
        mine = jnp.where((my_dp & bit) > 0, 1, 0)
        width = held.shape[-1] // 2
        keep = lax.dynamic_slice_in_dim(held, mine * width, width, 2)
        give = lax.dynamic_slice_in_dim(held, (1 - mine) * width, width, 2)
        got = swap(give, bit, count)
        held = jnp.concatenate([keep, got], axis=0)
    return held


def gather_rows(rows, count):
    held = rows[None]
    for bit in bits_of(count):
        held = jnp.concatenate([held, swap(held, bit, count)], axis=0)
    return held


def order_of(count):
    order = [0]
    for bit in bits_of(count):
        order = order + [k ^ bit for k in order]
    return order


def shards(tokens, routes, probs, cotangent, w_gate, w_up, w_down):
    tok_rows, top = routes.shape
    local = w_gate.shape[0]
    n_exp = lax.axis_size("expert")
    n_dp = lax.axis_size("dp")
    experts = local * n_exp
    cap = 5 * tok_rows * top // (4 * experts) * n_exp
    my_dp = lax.axis_index("dp")
    ids = lax.axis_index("expert") * local + jnp.arange(local, dtype=jnp.int32)

    totals = jnp.sum(probs, axis=1, keepdims=True)
    share = probs / totals
    meta = jnp.concatenate([routes.astype(F32), share], axis=1)
    meta = lax.all_gather(meta, ("dp", "expert"), tiled=True)
    x = lax.all_gather(tokens, "expert", tiled=True)
    c = lax.all_gather(cotangent, "expert", tiled=True)

    meta = meta.reshape(n_dp, n_exp * tok_rows, 2 * top)
    all_routes = meta[:, :, :top].astype(jnp.int32)
    named = all_routes[:, :, :, None] == ids
    hit = jnp.any(named, axis=2)
    rank = jnp.cumsum(hit.astype(jnp.int32), axis=1) - 1
    slot = jnp.where(hit, rank, -1).transpose(0, 2, 1)
    pick_all = (slot[:, :, None, :] == jnp.arange(cap, dtype=jnp.int32)[:, None]).astype(BF16)
    pick_all = pick_all[jnp.array(order_of(n_dp)) ^ my_dp]
    pick = pick_all[0]
    own = lax.dynamic_index_in_dim(meta, my_dp, 0, False)
    own_named = lax.dynamic_index_in_dim(named, my_dp, 0, False)
    token_share = jnp.sum(jnp.where(own_named, own[:, top:, None], 0.0), axis=1)
    row_share = jnp.sum(pick.astype(F32) * token_share.T[:, None, :], axis=2)[:, :, None]

    def dot(spec, a, b):
        return jnp.einsum(spec, a, b, preferred_element_type=F32)

    x_rows = dot("ert,td->erd", pick, x).astype(BF16)
    gate_pre = dot("erd,edh->erh", x_rows, w_gate)
    up_pre = dot("erd,edh->erh", x_rows, w_up)
    sig = jax.nn.sigmoid(gate_pre)
    active = gate_pre * sig * up_pre
    scaled_active = (row_share * active).astype(BF16)
    out = dot("erh,edh->erd", scaled_active, w_down).astype(BF16)
    mixed = dot("ert,erd->td", pick, out).astype(BF16)

    c_rows = dot("ert,td->erd", pick, c).astype(BF16)
    d_raw = dot("erd,edh->erh", c_rows, w_down)
    share_grad = jnp.sum(active * d_raw, axis=2)
    d_active = row_share * d_raw
    d_gate = (d_active * up_pre * sig * (1.0 + gate_pre * (1.0 - sig))).astype(BF16)
    d_up = (d_active * gate_pre * sig).astype(BF16)
    d_input = (dot("erh,edh->erd", d_gate, w_gate) + dot("erh,edh->erd", d_up, w_up)).astype(BF16)
    token_grad = dot("ert,erd->td", pick, d_input).astype(BF16)
    token_sg = jnp.sum(pick.astype(F32) * share_grad[:, :, None], axis=1)
    slot_sg = jnp.sum(jnp.where(own_named, token_sg.T[:, None, :], 0.0), axis=2)

    mixed = lax.psum_scatter(mixed, "expert", scatter_dimension=0, tiled=True)
    token_grad = lax.psum_scatter(token_grad, "expert", scatter_dimension=0, tiled=True)
    slot_sg = lax.psum_scatter(slot_sg, "expert", scatter_dimension=0, tiled=True)
    prob_grad = (slot_sg - jnp.sum(share * slot_sg, axis=1, keepdims=True)) / totals

    x_cols = spread_columns(x, my_dp, n_dp)
    c_cols = spread_columns(c, my_dp, n_dp)
    all_active = gather_rows(scaled_active, n_dp)
    all_gate = gather_rows(d_gate, n_dp)
    all_up = gather_rows(d_up, n_dp)
    x_all = dot("kert,ktd->kerd", pick_all, x_cols).astype(BF16)
    c_all = dot("kert,ktd->kerd", pick_all, c_cols).astype(BF16)
    gate_grad = dot("kerd,kerh->edh", x_all, all_gate).astype(BF16)
    up_grad = dot("kerd,kerh->edh", x_all, all_up).astype(BF16)
    down_grad = dot("kerd,kerh->edh", c_all, all_active).astype(BF16)
    return mixed, token_grad, prob_grad, gate_grad, up_grad, down_grad


def solution(mesh):
    rows = P(("expert", "dp"), None)
    weight = P("expert", None, None)
    grad = P("expert", "dp", None)
    return jax.shard_map(
        shards,
        mesh=mesh,
        in_specs=(rows, rows, rows, rows, weight, weight, weight),
        out_specs=(rows, rows, rows, grad, grad, grad),
        check_vma=False,
    )
```

```python
import jax
import jax.numpy as jnp
from jax import lax
from jax.sharding import PartitionSpec as P


F32 = jnp.float32
BF16 = jnp.bfloat16
LANES = 128


def swap(value, bit, count):
    return lax.ppermute(value, "dp", [(i, i ^ bit) for i in range(count)])


def bits_of(count):
    bit = count // 2
    while bit:
        yield bit
        bit //= 2


def spread_columns(rows, my_dp, count):
    held = rows[None]
    for bit in bits_of(count):
        mine = jnp.where((my_dp & bit) > 0, 1, 0)
        width = held.shape[-1] // 2
        keep = lax.dynamic_slice_in_dim(held, mine * width, width, 2)
        give = lax.dynamic_slice_in_dim(held, (1 - mine) * width, width, 2)
        got = swap(give, bit, count)
        held = jnp.concatenate([keep, got], axis=0)
    return held


def gather_rows(rows, count):
    held = rows[None]
    for bit in bits_of(count):
        held = jnp.concatenate([held, swap(held, bit, count)], axis=0)
    return held


def pair_swap(value, count):
    return lax.ppermute(value, "expert", [(i, i ^ 1) for i in range(count)])


def level_shift(value, hops, count):
    return lax.ppermute(value, "expert", [(i, (i + 2 * hops) % count) for i in range(count)])


def hop_order(levels):
    return sorted(range(1, levels), key=lambda k: abs(2 * k - levels))


def gather_levels(rows, count):
    levels = count // 2
    blocks = [[rows, pair_swap(rows, count)]] + [None] * (levels - 1)
    moved = {k: level_shift(rows, k, count) for k in hop_order(levels)}
    for k in hop_order(levels):
        blocks[k] = [moved[k], pair_swap(moved[k], count)]
    return jnp.concatenate([part for pair in blocks for part in pair], axis=0)


def reduce_levels(rows, count):
    levels = count // 2
    blocks = rows.reshape(levels, 2, -1, rows.shape[-1])
    total = None
    for k in hop_order(levels) + [0]:
        pair = blocks[k, 0].astype(F32) + pair_swap(blocks[k, 1], count).astype(F32)
        if k:
            pair = level_shift(pair.astype(BF16), -k, count).astype(F32)
        total = pair if total is None else total + pair
    return total


def split3(value):
    high = lax.reduce_precision(value, 8, 7)
    rest = value - high
    middle = lax.reduce_precision(rest, 8, 7)
    return [high.astype(BF16), middle.astype(BF16), (rest - middle).astype(BF16)]


def shards(tokens, routes, probs, cotangent, w_gate, w_up, w_down):
    tok_rows, top = routes.shape
    width = tokens.shape[1]
    local = w_gate.shape[0]
    n_exp = lax.axis_size("expert")
    n_dp = lax.axis_size("dp")
    experts = local * n_exp
    cap = 5 * tok_rows * top // (4 * experts) * n_exp
    my_dp = lax.axis_index("dp")
    ids = lax.axis_index("expert") * local + jnp.arange(local, dtype=jnp.int32)

    totals = jnp.sum(probs, axis=1, keepdims=True)
    share = probs / totals
    meta = jnp.concatenate([routes.astype(BF16)] + split3(share), axis=1)
    meta = jnp.pad(meta, ((0, 0), (0, LANES - 4 * top)))
    packed = gather_levels(jnp.concatenate([tokens, meta], axis=1), n_exp)
    c = gather_levels(cotangent, n_exp)

    x = packed[:, :width]
    meta = packed[:, width:].astype(F32)
    all_share = meta[:, top:2 * top] + meta[:, 2 * top:3 * top] + meta[:, 3 * top:4 * top]
    named = meta[:, :top].astype(jnp.int32)[:, :, None] == ids
    hit = jnp.any(named, axis=1)
    rank = jnp.cumsum(hit.astype(jnp.int32), axis=0) - 1
    slot = jnp.where(hit, rank, -1).T
    places = jnp.arange(cap, dtype=jnp.int32)
    pick = (slot[:, None, :] == places[:, None]).astype(BF16)
    token_share = jnp.sum(jnp.where(named, all_share[:, :, None], 0.0), axis=1)
    row_share = jnp.sum(pick.astype(F32) * token_share.T[:, None, :], axis=2)[:, :, None]

    def dot(spec, a, b):
        return jnp.einsum(spec, a, b, preferred_element_type=F32)

    x_rows = dot("ert,td->erd", pick, x).astype(BF16)
    gate_pre = dot("erd,edh->erh", x_rows, w_gate)
    up_pre = dot("erd,edh->erh", x_rows, w_up)
    sig = jax.nn.sigmoid(gate_pre)
    active = gate_pre * sig * up_pre
    scaled_active = (row_share * active).astype(BF16)
    out = dot("erh,edh->erd", scaled_active, w_down).astype(BF16)
    mixed = dot("ert,erd->td", pick, out).astype(BF16)
    mixed = reduce_levels(mixed, n_exp).astype(BF16)

    c_rows = dot("ert,td->erd", pick, c).astype(BF16)
    d_raw = dot("erd,edh->erh", c_rows, w_down)
    share_grad = jnp.sum(active * d_raw, axis=2)
    d_active = row_share * d_raw
    d_gate = (d_active * up_pre * sig * (1.0 + gate_pre * (1.0 - sig))).astype(BF16)
    d_up = (d_active * gate_pre * sig).astype(BF16)
    d_input = (dot("erh,edh->erd", d_gate, w_gate) + dot("erh,edh->erd", d_up, w_up)).astype(BF16)
    token_grad = dot("ert,erd->td", pick, d_input).astype(BF16)
    token_sg = jnp.sum(pick.astype(F32) * share_grad[:, :, None], axis=1)
    slot_sg = jnp.sum(jnp.where(named, token_sg.T[:, None, :], 0.0), axis=2)
    tail = jnp.pad(jnp.concatenate(split3(slot_sg), axis=1), ((0, 0), (0, LANES - 3 * top)))
    back = reduce_levels(jnp.concatenate([token_grad, tail], axis=1), n_exp)
    token_grad = back[:, :width].astype(BF16)
    tail = back[:, width:]
    slot_sg = tail[:, :top] + tail[:, top:2 * top] + tail[:, 2 * top:3 * top]
    prob_grad = (slot_sg - jnp.sum(share * slot_sg, axis=1, keepdims=True)) / totals

    x_cols = spread_columns(x, my_dp, n_dp)
    c_cols = spread_columns(c, my_dp, n_dp)
    all_slot = gather_rows(slot.astype(F32), n_dp)
    all_active = gather_rows(scaled_active, n_dp)
    all_d = gather_rows(jnp.concatenate([d_gate, d_up], axis=2), n_dp)
    hidden = d_gate.shape[2]
    pick_all = (all_slot.astype(jnp.int32)[:, :, None, :] == places[:, None]).astype(BF16)
    x_all = dot("kert,ktd->kerd", pick_all, x_cols).astype(BF16)
    c_all = dot("kert,ktd->kerd", pick_all, c_cols).astype(BF16)
    gate_grad = dot("kerd,kerh->edh", x_all, all_d[..., :hidden]).astype(BF16)
    up_grad = dot("kerd,kerh->edh", x_all, all_d[..., hidden:]).astype(BF16)
    down_grad = dot("kerd,kerh->edh", c_all, all_active).astype(BF16)
    return mixed, token_grad, prob_grad, gate_grad, up_grad, down_grad


def solution(mesh):
    rows = P(("expert", "dp"), None)
    weight = P("expert", None, None)
    grad = P("expert", "dp", None)
    return jax.shard_map(
        shards,
        mesh=mesh,
        in_specs=(rows, rows, rows, rows, weight, weight, weight),
        out_specs=(rows, rows, rows, grad, grad, grad),
        check_vma=False,
    )
```

```python
import functools

import jax
import jax.numpy as jnp
from jax import lax
from jax.experimental import pallas as pl
from jax.experimental.pallas import tpu as pltpu
from jax.sharding import PartitionSpec as P


F32 = jnp.float32
BF16 = jnp.bfloat16
LANES = 128
VMEM_LIMIT = 60 * 1024 * 1024


def round_up(value, unit):
    return -(-value // unit) * unit


def dot(a, b):
    return jnp.dot(a, b, preferred_element_type=F32)


def dot_nt(a, b):
    return lax.dot_general(a, b, (((1,), (1,)), ((), ())), preferred_element_type=F32)


def dot_tn(a, b):
    return lax.dot_general(a, b, (((0,), (0,)), ((), ())), preferred_element_type=F32)


def iota(shape, dim):
    return lax.broadcasted_iota(jnp.int32, shape, dim)


def load_blocks(blocks, held, sems):
    size = blocks[0].shape[0]
    copies = [
        pltpu.make_async_copy(block, held.at[pl.ds(i * size, size), :], sems.at[i])
        for i, block in enumerate(blocks)
    ]
    for copy in copies:
        copy.start()
    for copy in copies:
        copy.wait()


def fill_combine(slots_ref, combine, local, cap_pad):
    places = iota((slots_ref.shape[0], cap_pad), 1).astype(F32)
    for i in range(local):
        hit = slots_ref[:, i:i + 1] == places
        combine[:, i * cap_pad:(i + 1) * cap_pad] = jnp.where(hit, 1.0, 0.0).astype(BF16)


def pick_rows(slots_t_ref, expert, cap):
    row = slots_t_ref[pl.ds(expert, 1), :]
    return row == iota((cap, row.shape[1]), 0).astype(F32)


def store_levels(combine, rows_out, keep_ref, give_refs, tile):
    size, width = keep_ref.shape[1:]
    for start in range(0, width, tile):
        stop = min(start + tile, width)
        part = dot(combine[...], rows_out[:, start:stop]).astype(BF16)
        for k, give_ref in enumerate(give_refs):
            base = 2 * k * size
            keep_ref[k, :, start:stop] = part[base:base + size]
            give_ref[:, start:stop] = part[base + size:base + 2 * size]


def forward_kernel(cfg, first_ref, *refs):
    parts, local, cap, cap_pad, top = cfg
    blocks, refs = refs[:parts], refs[parts:]
    gate_ref, up_ref, down_ref = refs[:3]
    keep_ref, give_refs, refs = refs[3], refs[4:4 + parts // 2], refs[4 + parts // 2:]
    pre_ref, act_ref, info_ref, slots_ref, slots_t_ref = refs[:5]
    held, combine, out_rows, sems = refs[5:]
    expert = pl.program_id(0)
    tokens, width = held.shape[0], gate_ref.shape[1]
    hidden = gate_ref.shape[2]

    @pl.when(expert == 0)
    def _():
        load_blocks(blocks, held, sems)
        meta = held[:, width:].astype(F32).astype(jnp.int32)
        lane = iota(meta.shape, 1)
        hits = jnp.zeros(meta.shape, F32)
        for i in range(local):
            named = (meta == first_ref[0] + i) & (lane < top)
            hit = jnp.sum(jnp.where(named, 1.0, 0.0), axis=1, keepdims=True)
            hits = hits + jnp.where(lane == i, hit, 0.0)
        step = min(tokens, 256)
        below = (iota((step, step), 0) >= iota((step, step), 1)).astype(F32).astype(BF16)
        carry = jnp.zeros((1, LANES), F32)
        for start in range(0, tokens, step):
            part = hits[start:start + step]
            rank = dot(below, part.astype(BF16)) + carry
            carry = rank[step - 1:step]
            slots_ref[start:start + step, :] = jnp.where(part > 0.0, rank - 1.0, -1.0)
        slots_t_ref[...] = jnp.transpose(slots_ref[...])[:slots_t_ref.shape[0]]
        fill_combine(slots_ref, combine, local, cap_pad)
        for i in range(local):
            out_rows[i * cap_pad + cap:(i + 1) * cap_pad, :] = jnp.zeros((cap_pad - cap, width), BF16)

    hit = pick_rows(slots_t_ref, expert, cap)
    pick = jnp.where(hit, 1.0, 0.0)
    token = jnp.sum(jnp.where(hit, iota(hit.shape, 1).astype(F32), 0.0), axis=1, keepdims=True)
    token = jnp.where(jnp.sum(pick, axis=1, keepdims=True) > 0.0, token, -128.0).astype(jnp.int32)
    pick = pick.astype(BF16)
    rows = dot(pick, held[:, :width]).astype(BF16)
    meta = dot(pick, held[:, width:])
    lane = iota(meta.shape, 1)
    named = (meta.astype(jnp.int32) == first_ref[0] + expert) & (lane < top)
    shares = sum(pltpu.roll(meta, LANES - top * (i + 1), 1) for i in range(3))
    share = jnp.sum(jnp.where(named, shares, 0.0), axis=1, keepdims=True)
    info_ref[0] = jnp.where(lane < top, jnp.where(named, 1.0, 0.0), share)

    gate_pre = dot(rows, gate_ref[0])
    up_pre = dot(rows, up_ref[0])
    pre_ref[0, :, :hidden] = gate_pre
    pre_ref[0, :, hidden:] = up_pre
    active = gate_pre * jax.nn.sigmoid(gate_pre) * up_pre
    scaled = (share * active).astype(BF16)
    act_ref[0, :, :hidden] = scaled
    token_pair = jnp.where(lane == 0, token >> 7, jnp.where(lane == 1, token & 127, 0))
    act_ref[0, :, hidden:] = token_pair.astype(F32).astype(BF16)
    out_rows[pl.ds(pl.multiple_of(expert * cap_pad, cap_pad), cap), :] = dot_nt(scaled, down_ref[0]).astype(BF16)

    @pl.when(expert == local - 1)
    def _():
        store_levels(combine, out_rows, keep_ref, give_refs, 512)


def backward_kernel(cfg, *refs):
    parts, local, cap, cap_pad, top = cfg
    blocks, refs = refs[:parts], refs[parts:]
    gate_ref, up_ref, down_ref, pre_ref, info_ref, slots_ref, slots_t_ref = refs[:7]
    keep_ref, give_refs, refs = refs[7], refs[8:8 + parts // 2], refs[8 + parts // 2:]
    grad_ref, held, combine, out_rows, sems = refs
    expert = pl.program_id(0)
    width, hidden = gate_ref.shape[1:]

    @pl.when(expert == 0)
    def _():
        load_blocks(blocks, held, sems)
        fill_combine(slots_ref, combine, local, cap_pad)
        for i in range(local):
            out_rows[i * cap_pad + cap:(i + 1) * cap_pad, :] = jnp.zeros(
                (cap_pad - cap, out_rows.shape[1]), BF16)

    pick = jnp.where(pick_rows(slots_t_ref, expert, cap), 1.0, 0.0).astype(BF16)
    rows = dot(pick, held[...]).astype(BF16)
    info = info_ref[0]
    lane = iota(info.shape, 1)
    share = info[:, top:top + 1]
    gate_pre, up_pre = pre_ref[0, :, :hidden], pre_ref[0, :, hidden:]
    sig = jax.nn.sigmoid(gate_pre)
    silu = gate_pre * sig
    d_raw = dot(rows, down_ref[0])
    share_grad = jnp.sum(silu * up_pre * d_raw, axis=1, keepdims=True)
    d_active = share * d_raw
    d_gate = (d_active * up_pre * sig * (1.0 + gate_pre * (1.0 - sig))).astype(BF16)
    d_up = (d_active * silu).astype(BF16)
    grad_ref[0, :, :hidden] = d_gate
    grad_ref[0, :, hidden:] = d_up
    here = pl.ds(pl.multiple_of(expert * cap_pad, cap_pad), cap)
    out_rows[here, :width] = (dot_nt(d_gate, gate_ref[0]) + dot_nt(d_up, up_ref[0])).astype(BF16)
    placed = jnp.where((lane < top) & (info > 0.0), share_grad, 0.0)
    high = placed.astype(BF16)
    rest = placed - high.astype(F32)
    middle = rest.astype(BF16)
    low = (rest - middle.astype(F32)).astype(BF16)
    tail = high.astype(F32) + pltpu.roll(middle.astype(F32), top, 1) + pltpu.roll(low.astype(F32), 2 * top, 1)
    out_rows[here, width:] = tail.astype(BF16)

    @pl.when(expert == local - 1)
    def _():
        store_levels(combine, out_rows, keep_ref, give_refs, 512)


def weight_kernel(count, cap, x_ref, c_ref, act_ref, grad_ref, gate_ref, up_ref, down_ref, x_rows, c_rows, acts, grads):
    hidden = gate_ref.shape[2]
    tokens = x_ref.shape[1]
    for k in range(count):
        pair = act_ref[k, 0, :, hidden:].astype(F32)
        token = pair[:, 0:1] * 128.0 + pair[:, 1:2]
        pick = jnp.where(token == iota((cap, tokens), 1).astype(F32), 1.0, 0.0).astype(BF16)
        here = slice(k * cap, (k + 1) * cap)
        x_rows[here, :] = dot(pick, x_ref[k]).astype(BF16)
        c_rows[here, :] = dot(pick, c_ref[k]).astype(BF16)
        acts[here, :] = act_ref[k, 0, :, :hidden]
        grads[here, :] = grad_ref[k, 0]
    both = dot_tn(x_rows[...], grads[...])
    gate_ref[0] = both[:, :hidden].astype(BF16)
    up_ref[0] = both[:, hidden:].astype(BF16)
    down_ref[0] = dot_tn(c_rows[...], acts[...]).astype(BF16)


def swap(value, bit, count):
    return lax.ppermute(value, "dp", [(i, i ^ bit) for i in range(count)])


def bits_of(count):
    bit = count // 2
    while bit:
        yield bit
        bit //= 2


def spread_columns(rows, my_dp, count):
    held = rows[None]
    for bit in bits_of(count):
        mine = jnp.where((my_dp & bit) > 0, 1, 0)
        width = held.shape[-1] // 2
        keep = lax.dynamic_slice_in_dim(held, mine * width, width, 2)
        give = lax.dynamic_slice_in_dim(held, (1 - mine) * width, width, 2)
        got = swap(give, bit, count)
        held = jnp.concatenate([keep, got], axis=0)
    return held


def gather_rows(rows, count):
    held = rows[None]
    for bit in bits_of(count):
        held = jnp.concatenate([held, swap(held, bit, count)], axis=0)
    return held


def pair_swap(value, count):
    return lax.ppermute(value, "expert", [(i, i ^ 1) for i in range(count)])


def level_shift(value, hops, count):
    return lax.ppermute(value, "expert", [(i, (i + 2 * hops) % count) for i in range(count)])


def hop_order(levels):
    return sorted(range(1, levels), key=lambda k: abs(2 * k - levels))


def gather_levels(rows, count, after=()):
    levels = count // 2
    rows = lax.optimization_barrier((rows,) + tuple(after))[0]
    moved = {k: level_shift(rows, k, count) for k in hop_order(levels)}
    moved[0] = rows
    blocks = []
    for k in range(levels):
        blocks += [moved[k], pair_swap(moved[k], count)]
    return blocks, [moved[k] for k in range(1, levels)]


def reduce_levels(keep, gives, count):
    total = None
    for k in hop_order(len(gives)) + [0]:
        pair = keep[k].astype(F32) + pair_swap(gives[k], count).astype(F32)
        if k:
            pair = level_shift(pair.astype(BF16), -k, count).astype(F32)
        total = pair if total is None else total + pair
    return total


def split3(value):
    high = lax.reduce_precision(value, 8, 7)
    rest = value - high
    middle = lax.reduce_precision(rest, 8, 7)
    return [high.astype(BF16), middle.astype(BF16), (rest - middle).astype(BF16)]


def shards(tokens, routes, probs, cotangent, w_gate, w_up, w_down):
    tok_rows, top = routes.shape
    local, width, hidden = w_gate.shape
    n_exp = lax.axis_size("expert")
    n_dp = lax.axis_size("dp")
    experts = local * n_exp
    cap = 5 * tok_rows * top // (4 * experts) * n_exp
    cap_pad = round_up(cap, LANES)
    total = n_exp * tok_rows
    levels = n_exp // 2
    wide = width + LANES
    my_dp = lax.axis_index("dp")
    first = (lax.axis_index("expert") * local).astype(jnp.int32).reshape(1)
    cfg = (n_exp, local, cap, cap_pad, top)

    totals = jnp.sum(probs, axis=1, keepdims=True)
    share = probs / totals
    meta = jnp.concatenate([routes.astype(BF16)] + split3(share), axis=1)
    meta = jnp.pad(meta, ((0, 0), (0, LANES - 4 * top)))
    x_blocks, x_moved = gather_levels(jnp.concatenate([tokens, meta], axis=1), n_exp)
    c_blocks, _ = gather_levels(cotangent, n_exp, x_moved)

    any_space = pl.BlockSpec(memory_space=pl.ANY)
    smem = pl.BlockSpec(memory_space=pltpu.SMEM)
    params = pltpu.CompilerParams(dimension_semantics=("arbitrary",), vmem_limit_bytes=VMEM_LIMIT)

    def by_expert(*shape):
        return pl.BlockSpec((1,) + shape, lambda e: (e,) + (0,) * len(shape))

    def whole(*shape):
        return pl.BlockSpec(shape, lambda e: (0,) * len(shape))

    def sds(shape, dtype):
        return jax.ShapeDtypeStruct(shape, dtype)

    def level_outs(columns):
        shapes = [sds((levels, tok_rows, columns), BF16)] + [sds((tok_rows, columns), BF16)] * levels
        return shapes, [whole(*s.shape) for s in shapes]

    weight_specs = [by_expert(width, hidden)] * 3
    slot_rows = round_up(local, 8)
    shapes, specs = level_outs(width)
    forward = pl.pallas_call(
        functools.partial(forward_kernel, cfg),
        grid=(local,),
        in_specs=[smem] + [any_space] * n_exp + weight_specs,
        out_specs=specs + [by_expert(cap, 2 * hidden), by_expert(cap, hidden + LANES), by_expert(cap, LANES),
                           whole(total, LANES), whole(slot_rows, total)],
        out_shape=shapes + [sds((local, cap, 2 * hidden), F32), sds((local, cap, hidden + LANES), BF16),
                            sds((local, cap, LANES), F32), sds((total, LANES), F32), sds((slot_rows, total), F32)],
        scratch_shapes=[
            pltpu.VMEM((total, wide), BF16),
            pltpu.VMEM((total, local * cap_pad), BF16),
            pltpu.VMEM((local * cap_pad, width), BF16),
            pltpu.SemaphoreType.DMA((n_exp,)),
        ],
        compiler_params=params,
        cost_estimate=pl.CostEstimate(flops=12 * 10**9, bytes_accessed=26 * 10**6, transcendentals=0),
        name="forward",
    )
    results = forward(first, *x_blocks, w_gate, w_up, w_down)
    keep, gives = results[0], results[1:1 + levels]
    pre, act, info, slots, slots_t = results[1 + levels:]
    mixed = reduce_levels(keep, gives, n_exp).astype(BF16)

    shapes, specs = level_outs(wide)
    backward = pl.pallas_call(
        functools.partial(backward_kernel, cfg),
        grid=(local,),
        in_specs=[any_space] * n_exp + weight_specs + [
            by_expert(cap, 2 * hidden), by_expert(cap, LANES), whole(total, LANES), whole(slot_rows, total)],
        out_specs=specs + [by_expert(cap, 2 * hidden)],
        out_shape=shapes + [sds((local, cap, 2 * hidden), BF16)],
        scratch_shapes=[
            pltpu.VMEM((total, width), BF16),
            pltpu.VMEM((total, local * cap_pad), BF16),
            pltpu.VMEM((local * cap_pad, wide), BF16),
            pltpu.SemaphoreType.DMA((n_exp,)),
        ],
        compiler_params=params,
        cost_estimate=pl.CostEstimate(flops=12 * 10**9, bytes_accessed=26 * 10**6, transcendentals=0),
        name="backward",
    )
    results = backward(*c_blocks, w_gate, w_up, w_down, pre, info, slots, slots_t)
    keep, gives, grads = results[0], results[1:1 + levels], results[-1]
    back = reduce_levels(keep, gives, n_exp)
    token_grad = back[:, :width].astype(BF16)
    tail = back[:, width:]
    slot_sg = tail[:, :top] + tail[:, top:2 * top] + tail[:, 2 * top:3 * top]
    prob_grad = (slot_sg - jnp.sum(share * slot_sg, axis=1, keepdims=True)) / totals

    x_cols = spread_columns(jnp.concatenate([b[:, :width] for b in x_blocks], axis=0), my_dp, n_dp)
    c_cols = spread_columns(jnp.concatenate(c_blocks, axis=0), my_dp, n_dp)
    all_act = gather_rows(act, n_dp)
    all_grads = gather_rows(grads, n_dp)
    columns = width // n_dp

    def all_by_expert(*shape):
        return pl.BlockSpec((n_dp, 1) + shape, lambda e: (0, e) + (0,) * len(shape))

    weights = pl.pallas_call(
        functools.partial(weight_kernel, n_dp, cap),
        grid=(local,),
        in_specs=[whole(n_dp, total, columns)] * 2 + [all_by_expert(cap, hidden + LANES), all_by_expert(cap, 2 * hidden)],
        out_specs=[by_expert(columns, hidden)] * 3,
        out_shape=[sds((local, columns, hidden), BF16)] * 3,
        scratch_shapes=[pltpu.VMEM((n_dp * cap, columns), BF16)] * 2 + [
            pltpu.VMEM((n_dp * cap, hidden), BF16), pltpu.VMEM((n_dp * cap, 2 * hidden), BF16)],
        compiler_params=params,
        cost_estimate=pl.CostEstimate(flops=8 * 10**9, bytes_accessed=15 * 10**6, transcendentals=0),
        name="weight_grads",
    )
    gate_grad, up_grad, down_grad = weights(x_cols, c_cols, all_act, all_grads)
    return mixed, token_grad, prob_grad, gate_grad, up_grad, down_grad


def solution(mesh):
    rows = P(("expert", "dp"), None)
    weight = P("expert", None, None)
    grad = P("expert", "dp", None)
    return jax.shard_map(
        shards,
        mesh=mesh,
        in_specs=(rows, rows, rows, rows, weight, weight, weight),
        out_specs=(rows, rows, rows, grad, grad, grad),
        check_vma=False,
    )
```

```python
import functools

import jax
import jax.numpy as jnp
from jax import lax
from jax.experimental import pallas as pl
from jax.experimental.pallas import tpu as pltpu
from jax.sharding import PartitionSpec as P


F32 = jnp.float32
BF16 = jnp.bfloat16
LANES = 128
VMEM_LIMIT = 60 * 1024 * 1024


def round_up(value, unit):
    return -(-value // unit) * unit


def dot(a, b):
    return jnp.dot(a, b, preferred_element_type=F32)


def dot_nt(a, b):
    return lax.dot_general(a, b, (((1,), (1,)), ((), ())), preferred_element_type=F32)


def dot_tn(a, b):
    return lax.dot_general(a, b, (((0,), (0,)), ((), ())), preferred_element_type=F32)


def iota(shape, dim):
    return lax.broadcasted_iota(jnp.int32, shape, dim)


def load_blocks(blocks, held, sems):
    copies, start = [], 0
    for i, block in enumerate(blocks):
        size = block.shape[0]
        copies.append(pltpu.make_async_copy(block, held.at[pl.ds(start, size), :], sems.at[i]))
        start += size
    for copy in copies:
        copy.start()
    for copy in copies:
        copy.wait()


def tiles(width, tile=512):
    return [(start, min(start + tile, width)) for start in range(0, width, tile)]


def hidden_kernel(cfg, first_ref, *refs):
    parts, local, cap, cap_pad, top = cfg
    blocks, refs = refs[:parts], refs[parts:]
    gate_ref, up_ref, pre_ref, act_ref, info_ref, pick_ref, combine_ref, held, rows_ref, sems = refs
    expert = pl.program_id(0)
    tokens = held.shape[0]
    width, hidden = gate_ref.shape[1:]

    @pl.when(expert == 0)
    def _():
        load_blocks(blocks, held, sems)
        meta = held[:, width:].astype(F32).astype(jnp.int32)
        lane = iota(meta.shape, 1)
        hits = jnp.zeros(meta.shape, F32)
        for i in range(local):
            named = (meta == first_ref[0] + i) & (lane < top)
            hit = jnp.sum(jnp.where(named, 1.0, 0.0), axis=1, keepdims=True)
            hits = hits + jnp.where(lane == i, hit, 0.0)
        step = min(tokens, 256)
        below = (iota((step, step), 0) >= iota((step, step), 1)).astype(F32).astype(BF16)
        carry = jnp.zeros((1, LANES), F32)
        slots = []
        for start in range(0, tokens, step):
            part = hits[start:start + step]
            rank = dot(below, part.astype(BF16)) + carry
            carry = rank[step - 1:step]
            slots.append(jnp.where(part > 0.0, rank - 1.0, -1.0))
        slots = jnp.concatenate(slots, axis=0)
        slots_t = jnp.transpose(slots)
        places = iota((tokens, cap_pad), 1).astype(F32)
        places_t = iota((cap, tokens), 0).astype(F32)
        for i in range(local):
            hit = slots[:, i:i + 1] == places
            combine_ref[:, i * cap_pad:(i + 1) * cap_pad] = jnp.where(hit, 1.0, 0.0).astype(BF16)
            hit = slots_t[i:i + 1, :] == places_t
            pick_ref[i * cap:(i + 1) * cap, :] = jnp.where(hit, 1.0, 0.0).astype(BF16)
        for start, stop in tiles(held.shape[1]):
            rows_ref[:, start:stop] = dot(pick_ref[...], held[:, start:stop]).astype(BF16)

    here = pl.ds(pl.multiple_of(expert * cap, 16), cap)
    pick = pick_ref[here, :].astype(F32)
    token = jnp.sum(pick * iota(pick.shape, 1).astype(F32), axis=1, keepdims=True)
    token = jnp.where(jnp.sum(pick, axis=1, keepdims=True) > 0.0, token, -128.0).astype(jnp.int32)
    meta = rows_ref[here, width:].astype(F32)
    lane = iota(meta.shape, 1)
    named = (meta.astype(jnp.int32) == first_ref[0] + expert) & (lane < top)
    shares = sum(pltpu.roll(meta, LANES - top * (i + 1), 1) for i in range(3))
    share = jnp.sum(jnp.where(named, shares, 0.0), axis=1, keepdims=True)
    info_ref[0] = jnp.where(lane < top, jnp.where(named, 1.0, 0.0), share)

    rows = rows_ref[here, :width]
    gate_pre = dot(rows, gate_ref[0])
    up_pre = dot(rows, up_ref[0])
    pre_ref[0, :, :hidden] = gate_pre
    pre_ref[0, :, hidden:] = up_pre
    active = gate_pre * jax.nn.sigmoid(gate_pre) * up_pre
    act_ref[0, :, :hidden] = (share * active).astype(BF16)
    token_pair = jnp.where(lane == 0, token >> 7, jnp.where(lane == 1, token & 127, 0))
    act_ref[0, :, hidden:] = token_pair.astype(F32).astype(BF16)


def store_parts(value, here, refs):
    start = 0
    for ref in refs:
        ref[:, here] = value[start:start + ref.shape[0]]
        start += ref.shape[0]


def mixed_kernel(cfg, act_ref, combine_ref, down_ref, *refs):
    local, cap, cap_pad = cfg
    outs, spread = refs[:-1], refs[-1]
    hidden = down_ref.shape[2]
    tile = down_ref.shape[1]
    step = pl.program_id(0)

    @pl.when(step == 0)
    def _():
        for e in range(local):
            here = combine_ref[:, e * cap_pad:e * cap_pad + cap]
            spread[:, e * hidden:(e + 1) * hidden] = dot(here, act_ref[e, :, :hidden]).astype(BF16)

    total = dot_nt(spread[:, :hidden], down_ref[0])
    for e in range(1, local):
        total = total + dot_nt(spread[:, e * hidden:(e + 1) * hidden], down_ref[e])
    store_parts(total.astype(BF16), pl.ds(pl.multiple_of(step * tile, tile), tile), outs)


def grad_kernel(cfg, *refs):
    parts, local, cap, cap_pad, top = cfg
    blocks, refs = refs[:parts], refs[parts:]
    pick_ref, combine_ref, down_ref, pre_ref, info_ref, grad_ref, tail_ref, held, rows_ref, tails, sems = refs
    expert = pl.program_id(0)
    hidden = down_ref.shape[2]

    @pl.when(expert == 0)
    def _():
        load_blocks(blocks, held, sems)
        tails[...] = jnp.zeros(tails.shape, BF16)
        for start, stop in tiles(held.shape[1]):
            rows_ref[:, start:stop] = dot(pick_ref[...], held[:, start:stop]).astype(BF16)

    info = info_ref[0]
    lane = iota(info.shape, 1)
    share = info[:, top:top + 1]
    gate_pre, up_pre = pre_ref[0, :, :hidden], pre_ref[0, :, hidden:]
    sig = jax.nn.sigmoid(gate_pre)
    silu = gate_pre * sig
    d_raw = dot(rows_ref[pl.ds(pl.multiple_of(expert * cap, 16), cap), :], down_ref[0])
    share_grad = jnp.sum(silu * up_pre * d_raw, axis=1, keepdims=True)
    d_active = share * d_raw
    grad_ref[0, :, :hidden] = (d_active * up_pre * sig * (1.0 + gate_pre * (1.0 - sig))).astype(BF16)
    grad_ref[0, :, hidden:] = (d_active * silu).astype(BF16)
    placed = jnp.where((lane < top) & (info > 0.0), share_grad, 0.0)
    high = placed.astype(BF16)
    rest = placed - high.astype(F32)
    middle = rest.astype(BF16)
    low = (rest - middle.astype(F32)).astype(BF16)
    tail = high.astype(F32) + pltpu.roll(middle.astype(F32), top, 1) + pltpu.roll(low.astype(F32), 2 * top, 1)
    tails[pl.ds(pl.multiple_of(expert * cap_pad, cap_pad), cap), :] = tail.astype(BF16)

    @pl.when(expert == local - 1)
    def _():
        tail_ref[...] = dot(combine_ref[...], tails[...]).astype(BF16)


def input_kernel(cfg, grad_ref, combine_ref, tail_ref, gate_ref, up_ref, *refs):
    local, cap, cap_pad = cfg
    outs, rows = refs[:-1], refs[-1]
    tile, hidden = gate_ref.shape[1:]
    step = pl.program_id(0)

    @pl.when(step == 0)
    def _():
        rows[...] = jnp.zeros(rows.shape, BF16)
        width = outs[0].shape[1] - LANES
        store_parts(tail_ref[...], slice(width, width + LANES), outs)

    for e in range(local):
        part = dot_nt(grad_ref[e, :, :hidden], gate_ref[e]) + dot_nt(grad_ref[e, :, hidden:], up_ref[e])
        rows[e * cap_pad:e * cap_pad + cap, :] = part.astype(BF16)
    total = dot(combine_ref[...], rows[...]).astype(BF16)
    store_parts(total, pl.ds(pl.multiple_of(step * tile, tile), tile), outs)


def down_kernel(cap, counts, *refs):
    x_refs, c_refs, act_refs = refs[:counts[0]], refs[counts[0]:counts[1]], refs[counts[1]:counts[2]]
    rows_ref, down_ref, c_rows, acts = refs[counts[2]:]
    hidden = down_ref.shape[2]
    x_parts = [ref.at[k] for ref in x_refs for k in range(ref.shape[0])]
    c_parts = [ref.at[k] for ref in c_refs for k in range(ref.shape[0])]
    act_parts = [ref.at[k, 0] for ref in act_refs for k in range(ref.shape[0])]
    for k, (x_part, c_part, act_part) in enumerate(zip(x_parts, c_parts, act_parts)):
        pair = act_part[:, hidden:].astype(F32)
        token = pair[:, 0:1] * 128.0 + pair[:, 1:2]
        pick = jnp.where(token == iota((cap, x_part.shape[0]), 1).astype(F32), 1.0, 0.0).astype(BF16)
        here = slice(k * cap, (k + 1) * cap)
        rows_ref[0, here, :] = dot(pick, x_part[...]).astype(BF16)
        c_rows[here, :] = dot(pick, c_part[...]).astype(BF16)
        acts[here, :] = act_part[:, :hidden]
    down_ref[0] = dot_tn(c_rows[...], acts[...]).astype(BF16)


def gate_kernel(cap, rows_ref, *refs):
    grad_refs, (gate_ref, up_ref, grads) = refs[:-3], refs[-3:]
    hidden = gate_ref.shape[2]
    parts = [ref.at[k, 0] for ref in grad_refs for k in range(ref.shape[0])]
    for k, part in enumerate(parts):
        grads[k * cap:(k + 1) * cap, :] = part[...]
    both = dot_tn(rows_ref[0], grads[...])
    gate_ref[0] = both[:, :hidden].astype(BF16)
    up_ref[0] = both[:, hidden:].astype(BF16)


def swap(value, bit, count):
    return lax.ppermute(value, "dp", [(i, i ^ bit) for i in range(count)])


def pair_swap(value, count):
    return lax.ppermute(value, "expert", [(i, i ^ 1) for i in range(count)])


def level_shift(value, hops, count):
    return lax.ppermute(value, "expert", [(i, (i + 2 * hops) % count) for i in range(count)])


def fence(*values):
    leaves, tree = jax.tree.flatten(values)
    return jax.tree.unflatten(tree, lax.optimization_barrier(tuple(leaves)))


def split3(value):
    high = lax.reduce_precision(value, 8, 7)
    rest = value - high
    middle = lax.reduce_precision(rest, 8, 7)
    return [high.astype(BF16), middle.astype(BF16), (rest - middle).astype(BF16)]


def shards(tokens, routes, probs, cotangent, w_gate, w_up, w_down):
    tok_rows, top = routes.shape
    local, width, hidden = w_gate.shape
    n_exp = lax.axis_size("expert")
    n_dp = lax.axis_size("dp")
    experts = local * n_exp
    cap = 5 * tok_rows * top // (4 * experts) * n_exp
    cap_pad = round_up(cap, LANES)
    total = n_exp * tok_rows
    levels = n_exp // 2
    line = levels * tok_rows
    wide = width + LANES
    tile = min(width, 512)
    columns = width // n_dp
    far_bit = n_dp // 2
    my_dp = lax.axis_index("dp")
    far = jnp.where((my_dp & far_bit) > 0, 1, 0)
    near = jnp.where((my_dp & 1) > 0, 1, 0)
    first = (lax.axis_index("expert") * local).astype(jnp.int32).reshape(1)
    hops = sorted(range(1, levels), key=lambda k: abs(2 * k - levels))
    mid, rest = hops[0], hops[1:]

    def pair(value):
        return pair_swap(value, n_exp)

    def shift(value, count):
        return level_shift(value, count, n_exp)

    def cut(value, which, parts=2):
        size = value.shape[-1] // parts
        return lax.dynamic_slice_in_dim(value, which * size, size, value.ndim - 1)

    any_space = pl.BlockSpec(memory_space=pl.ANY)
    smem = pl.BlockSpec(memory_space=pltpu.SMEM)
    params = pltpu.CompilerParams(dimension_semantics=("arbitrary",), vmem_limit_bytes=VMEM_LIMIT)

    def by_expert(*shape):
        return pl.BlockSpec((1,) + shape, lambda e: (e,) + (0,) * len(shape))

    def whole(*shape):
        return pl.BlockSpec(shape, lambda e: (0,) * len(shape))

    def sds(shape, dtype):
        return jax.ShapeDtypeStruct(shape, dtype)

    def cost(gflop, mbyte):
        return pl.CostEstimate(flops=gflop * 10**9, bytes_accessed=mbyte * 10**6, transcendentals=0)

    by_columns = pl.BlockSpec((local, tile, hidden), lambda j: (0, j, 0))
    weight_spec = by_expert(width, hidden)
    parts = levels + 3 if rest else levels + 2
    cfg = (parts, local, cap, cap_pad, top)

    totals = jnp.sum(probs, axis=1, keepdims=True)
    share = probs / totals
    meta = jnp.concatenate([routes.astype(BF16)] + split3(share), axis=1)
    meta = jnp.pad(meta, ((0, 0), (0, LANES - 4 * top)))

    x_own = jnp.concatenate([tokens, meta], axis=1)
    x_mid = shift(x_own, mid)
    x_own_pair = pair(x_own)
    x_mid, x_own = fence(x_mid, x_own)
    x_rest = [shift(x_own, k) for k in rest]
    x_mid_pair = pair(x_mid)
    x_rest, x_mid_pair, x_own_pair, cot = fence(x_rest, x_mid_pair, x_own_pair, cotangent)

    x_rest_pair = pair(jnp.concatenate(x_rest, axis=0))
    x_line = jnp.concatenate([x_own, x_mid] + x_rest, axis=0)[:, :width]
    x_far = swap(cut(x_line, 1 - far), far_bit, n_dp)
    c_mid = shift(cot, mid)
    c_own_pair = pair(cot)
    c_mid, cot = fence(c_mid, cot)
    c_rest = [shift(cot, k) for k in rest]
    c_mid_pair = pair(c_mid)
    x_rest_pair, x_far, c_own_pair = fence(x_rest_pair, x_far, c_own_pair)

    x_other = jnp.concatenate([x_own_pair, x_mid_pair, x_rest_pair], axis=0)[:, :width]
    x_far_pair = swap(cut(x_other, 1 - far), far_bit, n_dp)
    pre, act, info, pick, combine = pl.pallas_call(
        functools.partial(hidden_kernel, cfg),
        grid=(local,),
        in_specs=[smem] + [any_space] * parts + [weight_spec] * 2,
        out_specs=[by_expert(cap, 2 * hidden), by_expert(cap, hidden + LANES), by_expert(cap, LANES),
                   whole(local * cap, total), whole(total, local * cap_pad)],
        out_shape=[sds((local, cap, 2 * hidden), F32), sds((local, cap, hidden + LANES), BF16),
                   sds((local, cap, LANES), F32), sds((local * cap, total), BF16), sds((total, local * cap_pad), BF16)],
        scratch_shapes=[
            pltpu.VMEM((total, wide), BF16),
            pltpu.VMEM((local * cap, wide), BF16),
            pltpu.SemaphoreType.DMA((parts,)),
        ],
        compiler_params=params,
        cost_estimate=cost(6, 20),
        name="hidden",
    )(first, x_own, x_mid, *x_rest, x_own_pair, x_mid_pair, x_rest_pair, w_gate, w_up)
    act, c_rest, c_mid_pair, x_far_pair = fence(act, c_rest, c_mid_pair, x_far_pair)

    c_rest_pair = pair(jnp.concatenate(c_rest, axis=0))
    c_line = jnp.concatenate([cot, c_mid] + c_rest, axis=0)
    c_far = swap(cut(c_line, 1 - far), far_bit, n_dp)
    act_far = swap(act[None], far_bit, n_dp)
    x_held = jnp.stack([jnp.concatenate([cut(x_line, far), cut(x_other, far)], axis=0),
                        jnp.concatenate([x_far, x_far_pair], axis=0)])
    x_near = swap(cut(x_held, 1 - near), 1, n_dp)
    level_rows = [line, tok_rows, tok_rows, line - 2 * tok_rows]
    level_specs = [whole(rows, width) for rows in level_rows]
    mixed_keep, mixed_own, mixed_mid, mixed_rest = pl.pallas_call(
        functools.partial(mixed_kernel, (local, cap, cap_pad)),
        grid=(width // tile,),
        in_specs=[whole(local, cap, hidden + LANES), whole(total, local * cap_pad), by_columns],
        out_specs=level_specs,
        out_shape=[sds((rows, width), BF16) for rows in level_rows],
        scratch_shapes=[pltpu.VMEM((total, local * hidden), BF16)],
        compiler_params=params,
        cost_estimate=cost(6, 10),
        name="mixed",
    )(act, combine, w_down)
    c_rest_pair, mixed_keep, mixed_own, mixed_mid, mixed_rest, act_far, x_near = fence(
        c_rest_pair, mixed_keep, mixed_own, mixed_mid, mixed_rest, act_far, x_near)

    def back_rows(keep, got):
        return keep.astype(F32) + got.astype(F32)

    mixed_mid = pair(mixed_mid)
    mixed_rest = pair(mixed_rest)
    act_near = swap(jnp.concatenate([act[None], act_far], axis=0), 1, n_dp)
    c_other = jnp.concatenate([c_own_pair, c_mid_pair, c_rest_pair], axis=0)
    c_far_pair = swap(cut(c_other, 1 - far), far_bit, n_dp)
    grads, tail = pl.pallas_call(
        functools.partial(grad_kernel, cfg),
        grid=(local,),
        in_specs=[any_space] * parts + [whole(local * cap, total), whole(total, local * cap_pad), weight_spec,
                                        by_expert(cap, 2 * hidden), by_expert(cap, LANES)],
        out_specs=[by_expert(cap, 2 * hidden), whole(total, LANES)],
        out_shape=[sds((local, cap, 2 * hidden), BF16), sds((total, LANES), BF16)],
        scratch_shapes=[
            pltpu.VMEM((total, width), BF16),
            pltpu.VMEM((local * cap, width), BF16),
            pltpu.VMEM((local * cap_pad, LANES), BF16),
            pltpu.SemaphoreType.DMA((parts,)),
        ],
        compiler_params=params,
        cost_estimate=cost(6, 12),
        name="hidden_grads",
    )(cot, c_mid, *c_rest, c_own_pair, c_mid_pair, c_rest_pair, pick, combine, w_down, pre, info)
    grads, tail, mixed_mid, mixed_own, c_far = fence(grads, tail, mixed_mid, mixed_own, c_far)

    def send_mid(keep, got):
        return shift(back_rows(keep[tok_rows:2 * tok_rows], got).astype(BF16), -mid)

    def sum_rest(keep, got):
        return back_rows(keep[2 * tok_rows:], got).astype(BF16)

    def send_rest(sums):
        return [shift(sums[i * tok_rows:(i + 1) * tok_rows], -k) for i, k in enumerate(rest)]

    def finish(keep, own, landed):
        return sum([part.astype(F32) for part in landed], back_rows(keep[:tok_rows], own))

    mixed_mid = send_mid(mixed_keep, mixed_mid)
    mixed_own = pair(mixed_own)
    grads_far = swap(grads[None], far_bit, n_dp)
    wide_specs = [whole(rows, wide) for rows in level_rows]
    input_keep, input_own, input_mid, input_rest = pl.pallas_call(
        functools.partial(input_kernel, (local, cap, cap_pad)),
        grid=(width // tile,),
        in_specs=[whole(local, cap, 2 * hidden), whole(total, local * cap_pad), whole(total, LANES),
                  by_columns, by_columns],
        out_specs=wide_specs,
        out_shape=[sds((rows, wide), BF16) for rows in level_rows],
        scratch_shapes=[pltpu.VMEM((local * cap_pad, tile), BF16)],
        compiler_params=params,
        cost_estimate=cost(6, 16),
        name="input_grads",
    )(grads, combine, tail, w_gate, w_up)
    (input_keep, input_own, input_mid, input_rest, mixed_mid, mixed_rest, mixed_own, act_near) = fence(
        input_keep, input_own, input_mid, input_rest, mixed_mid, mixed_rest, mixed_own, act_near)

    mixed_rest = send_rest(sum_rest(mixed_keep, mixed_rest))
    input_mid = pair(input_mid)
    input_rest = pair(input_rest)
    input_mid, input_own = fence(input_mid, input_own)
    input_mid = send_mid(input_keep, input_mid)
    mixed_rest, input_own, c_far_pair = fence(mixed_rest, input_own, c_far_pair)
    input_own = pair(input_own)
    c_held = jnp.stack([jnp.concatenate([cut(c_line, far), cut(c_other, far)], axis=0),
                        jnp.concatenate([c_far, c_far_pair], axis=0)])
    c_near = swap(cut(c_held, 1 - near), 1, n_dp)
    input_rest, c_near = fence(sum_rest(input_keep, input_rest), c_near)
    input_rest = send_rest(input_rest)
    mixed = finish(mixed_keep, mixed_own, [mixed_mid] + mixed_rest).astype(BF16)

    def pieces(*shape):
        return [pl.BlockSpec((n, 1) + shape, lambda e: (0, e) + (0,) * len(shape)) for n in (1, 1, 2)]

    x_pieces, c_pieces = [cut(x_held, near), x_near], [cut(c_held, near), c_near]
    x_rows, down_grad = pl.pallas_call(
        functools.partial(down_kernel, cap, (2, 4, 7)),
        grid=(local,),
        in_specs=[whole(2, total, columns)] * 4 + pieces(cap, hidden + LANES),
        out_specs=[by_expert(n_dp * cap, columns), by_expert(columns, hidden)],
        out_shape=[sds((local, n_dp * cap, columns), BF16), sds((local, columns, hidden), BF16)],
        scratch_shapes=[pltpu.VMEM((n_dp * cap, columns), BF16), pltpu.VMEM((n_dp * cap, hidden), BF16)],
        compiler_params=params,
        cost_estimate=cost(6, 12),
        name="down_grads",
    )(*x_pieces, *c_pieces, act[None], act_far, act_near)

    grads_far, down_grad = fence(grads_far, down_grad)
    grads_near = swap(jnp.concatenate([grads[None], grads_far], axis=0), 1, n_dp)
    gate_grad, up_grad = pl.pallas_call(
        functools.partial(gate_kernel, cap),
        grid=(local,),
        in_specs=[by_expert(n_dp * cap, columns)] + pieces(cap, 2 * hidden),
        out_specs=[by_expert(columns, hidden)] * 2,
        out_shape=[sds((local, columns, hidden), BF16)] * 2,
        scratch_shapes=[pltpu.VMEM((n_dp * cap, 2 * hidden), BF16)],
        compiler_params=params,
        cost_estimate=cost(3, 10),
        name="gate_grads",
    )(x_rows, grads[None], grads_far, grads_near)

    back = finish(input_keep, input_own, [input_mid] + input_rest)
    token_grad = back[:, :width].astype(BF16)
    tail = back[:, width:]
    slot_sg = tail[:, :top] + tail[:, top:2 * top] + tail[:, 2 * top:3 * top]
    prob_grad = (slot_sg - jnp.sum(share * slot_sg, axis=1, keepdims=True)) / totals
    return mixed, token_grad, prob_grad, gate_grad, up_grad, down_grad


def solution(mesh):
    rows = P(("expert", "dp"), None)
    weight = P("expert", None, None)
    grad = P("expert", "dp", None)
    return jax.shard_map(
        shards,
        mesh=mesh,
        in_specs=(rows, rows, rows, rows, weight, weight, weight),
        out_specs=(rows, rows, rows, grad, grad, grad),
        check_vma=False,
    )
```

```python
import functools

import jax
import jax.numpy as jnp
from jax import lax
from jax.experimental import pallas as pl
from jax.experimental.pallas import tpu as pltpu
from jax.sharding import PartitionSpec as P


F32 = jnp.float32
BF16 = jnp.bfloat16
LANES = 128
VMEM_LIMIT = 60 * 1024 * 1024


def round_up(value, unit):
    return -(-value // unit) * unit


def dot(a, b):
    return jnp.dot(a, b, preferred_element_type=F32)


def dot_nt(a, b):
    return lax.dot_general(a, b, (((1,), (1,)), ((), ())), preferred_element_type=F32)


def dot_tn(a, b):
    return lax.dot_general(a, b, (((0,), (0,)), ((), ())), preferred_element_type=F32)


def iota(shape, dim):
    return lax.broadcasted_iota(jnp.int32, shape, dim)


def load_blocks(blocks, held, sems):
    copies, start = [], 0
    for i, block in enumerate(blocks):
        size = block.shape[0]
        copies.append(pltpu.make_async_copy(block, held.at[pl.ds(start, size), :], sems.at[i]))
        start += size
    for copy in copies:
        copy.start()
    for copy in copies:
        copy.wait()


def tiles(width, tile=512):
    return [(start, min(start + tile, width)) for start in range(0, width, tile)]


def half_of(which, width):
    return pl.ds(pl.multiple_of(which * (width // 2), LANES), width // 2)


def hidden_kernel(cfg, first_ref, far_ref, *refs):
    parts, local, cap, cap_pad, top = cfg
    blocks, refs = refs[:parts], refs[parts:]
    gate_ref, up_ref, pre_ref, act_ref, info_ref, pick_ref, combine_ref, keep_ref, held, rows_ref, sems = refs
    expert = pl.program_id(0)
    tokens = held.shape[0]
    width, hidden = gate_ref.shape[1:]

    @pl.when(expert == 0)
    def _():
        load_blocks(blocks, held, sems)
        meta = held[:, width:].astype(F32).astype(jnp.int32)
        lane = iota(meta.shape, 1)
        hits = jnp.zeros(meta.shape, F32)
        for i in range(local):
            named = (meta == first_ref[0] + i) & (lane < top)
            hit = jnp.sum(jnp.where(named, 1.0, 0.0), axis=1, keepdims=True)
            hits = hits + jnp.where(lane == i, hit, 0.0)
        step = min(tokens, 256)
        below = (iota((step, step), 0) >= iota((step, step), 1)).astype(F32).astype(BF16)
        carry = jnp.zeros((1, LANES), F32)
        slots = []
        for start in range(0, tokens, step):
            part = hits[start:start + step]
            rank = dot(below, part.astype(BF16)) + carry
            carry = rank[step - 1:step]
            slots.append(jnp.where(part > 0.0, rank - 1.0, -1.0))
        slots = jnp.concatenate(slots, axis=0)
        slots_t = jnp.transpose(slots)
        places = iota((tokens, cap_pad), 1).astype(F32)
        places_t = iota((cap, tokens), 0).astype(F32)
        for i in range(local):
            hit = slots[:, i:i + 1] == places
            combine_ref[:, i * cap_pad:(i + 1) * cap_pad] = jnp.where(hit, 1.0, 0.0).astype(BF16)
            hit = slots_t[i:i + 1, :] == places_t
            pick_ref[i * cap:(i + 1) * cap, :] = jnp.where(hit, 1.0, 0.0).astype(BF16)
        for start, stop in tiles(held.shape[1]):
            rows_ref[:, start:stop] = dot(pick_ref[...], held[:, start:stop]).astype(BF16)
        keep_ref[...] = held[:, half_of(far_ref[0], width)]

    here = pl.ds(pl.multiple_of(expert * cap, 16), cap)
    pick = pick_ref[here, :].astype(F32)
    token = jnp.sum(pick * iota(pick.shape, 1).astype(F32), axis=1, keepdims=True)
    token = jnp.where(jnp.sum(pick, axis=1, keepdims=True) > 0.0, token, -128.0).astype(jnp.int32)
    meta = rows_ref[here, width:].astype(F32)
    lane = iota(meta.shape, 1)
    named = (meta.astype(jnp.int32) == first_ref[0] + expert) & (lane < top)
    shares = sum(pltpu.roll(meta, LANES - top * (i + 1), 1) for i in range(3))
    share = jnp.sum(jnp.where(named, shares, 0.0), axis=1, keepdims=True)
    info_ref[0] = jnp.where(lane < top, jnp.where(named, 1.0, 0.0), share)

    rows = rows_ref[here, :width]
    gate_pre = dot(rows, gate_ref[0])
    up_pre = dot(rows, up_ref[0])
    pre_ref[0, :, :hidden] = gate_pre
    pre_ref[0, :, hidden:] = up_pre
    active = gate_pre * jax.nn.sigmoid(gate_pre) * up_pre
    act_ref[0, :, :hidden] = (share * active).astype(BF16)
    token_pair = jnp.where(lane == 0, token >> 7, jnp.where(lane == 1, token & 127, 0))
    act_ref[0, :, hidden:] = token_pair.astype(F32).astype(BF16)


def store_parts(value, here, refs):
    start = 0
    for ref in refs:
        ref[:, here] = value[start:start + ref.shape[0]]
        start += ref.shape[0]


def mixed_kernel(cfg, act_ref, combine_ref, down_ref, *refs):
    local, cap, cap_pad = cfg
    outs, spread = refs[:-1], refs[-1]
    hidden = down_ref.shape[2]
    tile = down_ref.shape[1]
    step = pl.program_id(0)

    @pl.when(step == 0)
    def _():
        for e in range(local):
            here = combine_ref[:, e * cap_pad:e * cap_pad + cap]
            spread[:, e * hidden:(e + 1) * hidden] = dot(here, act_ref[e, :, :hidden]).astype(BF16)

    total = dot_nt(spread[:, :hidden], down_ref[0])
    for e in range(1, local):
        total = total + dot_nt(spread[:, e * hidden:(e + 1) * hidden], down_ref[e])
    store_parts(total.astype(BF16), pl.ds(pl.multiple_of(step * tile, tile), tile), outs)


def grad_kernel(cfg, far_ref, *refs):
    parts, local, cap, cap_pad, top = cfg
    blocks, refs = refs[:parts], refs[parts:]
    pick_ref, combine_ref, down_ref, pre_ref, info_ref, d_gate_ref, d_up_ref, tail_ref, keep_ref, give_ref = refs[:10]
    held, rows_ref, tails, sems = refs[10:]
    expert = pl.program_id(0)
    hidden = down_ref.shape[2]

    @pl.when(expert == 0)
    def _():
        load_blocks(blocks, held, sems)
        tails[...] = jnp.zeros(tails.shape, BF16)
        for start, stop in tiles(held.shape[1]):
            rows_ref[:, start:stop] = dot(pick_ref[...], held[:, start:stop]).astype(BF16)
        width = held.shape[1]
        keep_ref[...] = held[:, half_of(far_ref[0], width)]
        give_ref[...] = held[give_ref.shape[0]:, half_of(1 - far_ref[0], width)]

    info = info_ref[0]
    lane = iota(info.shape, 1)
    share = info[:, top:top + 1]
    gate_pre, up_pre = pre_ref[0, :, :hidden], pre_ref[0, :, hidden:]
    sig = jax.nn.sigmoid(gate_pre)
    silu = gate_pre * sig
    d_raw = dot(rows_ref[pl.ds(pl.multiple_of(expert * cap, 16), cap), :], down_ref[0])
    share_grad = jnp.sum(silu * up_pre * d_raw, axis=1, keepdims=True)
    d_active = share * d_raw
    d_gate_ref[0] = (d_active * up_pre * sig * (1.0 + gate_pre * (1.0 - sig))).astype(BF16)
    d_up_ref[0] = (d_active * silu).astype(BF16)
    placed = jnp.where((lane < top) & (info > 0.0), share_grad, 0.0)
    high = placed.astype(BF16)
    rest = placed - high.astype(F32)
    middle = rest.astype(BF16)
    low = (rest - middle.astype(F32)).astype(BF16)
    tail = high.astype(F32) + pltpu.roll(middle.astype(F32), top, 1) + pltpu.roll(low.astype(F32), 2 * top, 1)
    tails[pl.ds(pl.multiple_of(expert * cap_pad, cap_pad), cap), :] = tail.astype(BF16)

    @pl.when(expert == local - 1)
    def _():
        tail_ref[...] = dot(combine_ref[...], tails[...]).astype(BF16)


def input_kernel(cfg, d_gate_ref, d_up_ref, combine_ref, tail_ref, gate_ref, up_ref, *refs):
    local, cap, cap_pad = cfg
    outs, rows = refs[:-1], refs[-1]
    tile, hidden = gate_ref.shape[1:]
    step = pl.program_id(0)

    @pl.when(step == 0)
    def _():
        rows[...] = jnp.zeros(rows.shape, BF16)
        width = outs[0].shape[1] - LANES
        store_parts(tail_ref[...], slice(width, width + LANES), outs)

    for e in range(local):
        part = dot_nt(d_gate_ref[e], gate_ref[e]) + dot_nt(d_up_ref[e], up_ref[e])
        rows[e * cap_pad:e * cap_pad + cap, :] = part.astype(BF16)
    total = dot(combine_ref[...], rows[...]).astype(BF16)
    store_parts(total, pl.ds(pl.multiple_of(step * tile, tile), tile), outs)


def down_kernel(cap, x_ref, near_ref, c_ref, *refs):
    act_refs, (rows_ref, down_ref, c_rows, acts) = refs[:-4], refs[-4:]
    hidden = down_ref.shape[2]
    x_parts = [x_ref.at[0], x_ref.at[1], near_ref.at[0], near_ref.at[1]]
    c_parts = [c_ref.at[0], c_ref.at[1], near_ref.at[2], near_ref.at[3]]
    for k, (x_part, c_part, act_ref) in enumerate(zip(x_parts, c_parts, act_refs)):
        pair = act_ref[0, :, hidden:].astype(F32)
        token = pair[:, 0:1] * 128.0 + pair[:, 1:2]
        pick = jnp.where(token == iota((cap, x_part.shape[0]), 1).astype(F32), 1.0, 0.0).astype(BF16)
        here = slice(k * cap, (k + 1) * cap)
        rows_ref[0, here, :] = dot(pick, x_part[...]).astype(BF16)
        c_rows[here, :] = dot(pick, c_part[...]).astype(BF16)
        acts[here, :] = act_ref[0, :, :hidden]
    down_ref[0] = dot_tn(c_rows[...], acts[...]).astype(BF16)


def gate_kernel(cap, rows_ref, *refs):
    count = (len(refs) - 3) // 2
    gate_ref, up_ref, grads = refs[2 * count:]
    hidden = gate_ref.shape[2]
    for k in range(count):
        grads[k * cap:(k + 1) * cap, :hidden] = refs[k][0]
        grads[k * cap:(k + 1) * cap, hidden:] = refs[count + k][0]
    both = dot_tn(rows_ref[0], grads[...])
    gate_ref[0] = both[:, :hidden].astype(BF16)
    up_ref[0] = both[:, hidden:].astype(BF16)


def cut_kernel(half, plan, word_ref, *refs):
    count = 1 + max(i for i, _, _, _ in plan)
    blocks, outs, sems = refs[:count], refs[count:-1], refs[-1]
    copies = []
    for i, flip, out, row in plan:
        which = 1 - word_ref[0] if flip else word_ref[0]
        here = pl.ds(pl.multiple_of(which * half, LANES), half)
        there = outs[out].at[pl.ds(row, blocks[i].shape[0]), :]
        copies.append(pltpu.make_async_copy(blocks[i].at[:, here], there, sems.at[len(copies)]))
    for copy in copies:
        copy.start()
    for copy in copies:
        copy.wait()


def swap(value, bit, count):
    return lax.ppermute(value, "dp", [(i, i ^ bit) for i in range(count)])


def pair_swap(value, count):
    return lax.ppermute(value, "expert", [(i, i ^ 1) for i in range(count)])


def level_shift(value, hops, count):
    return lax.ppermute(value, "expert", [(i, (i + 2 * hops) % count) for i in range(count)])


def fence(*values):
    leaves, tree = jax.tree.flatten(values)
    return jax.tree.unflatten(tree, lax.optimization_barrier(tuple(leaves)))


def split3(value):
    high = lax.reduce_precision(value, 8, 7)
    rest = value - high
    middle = lax.reduce_precision(rest, 8, 7)
    return [high.astype(BF16), middle.astype(BF16), (rest - middle).astype(BF16)]


def shards(tokens, routes, probs, cotangent, w_gate, w_up, w_down):
    tok_rows, top = routes.shape
    local, width, hidden = w_gate.shape
    n_exp = lax.axis_size("expert")
    n_dp = lax.axis_size("dp")
    experts = local * n_exp
    cap = 5 * tok_rows * top // (4 * experts) * n_exp
    cap_pad = round_up(cap, LANES)
    total = n_exp * tok_rows
    levels = n_exp // 2
    line = levels * tok_rows
    wide = width + LANES
    tile = min(width, 512)
    columns = width // n_dp
    far_bit = n_dp // 2
    my_dp = lax.axis_index("dp")
    far = jnp.where((my_dp & far_bit) > 0, 1, 0)
    near = jnp.where((my_dp & 1) > 0, 1, 0)
    near_word = near.astype(jnp.int32).reshape(1)
    far_word = far.astype(jnp.int32).reshape(1)
    first = (lax.axis_index("expert") * local).astype(jnp.int32).reshape(1)
    hops = sorted(range(1, levels), key=lambda k: abs(2 * k - levels))
    mid, rest = hops[0], hops[1:]

    def pair(value):
        return pair_swap(value, n_exp)

    def shift(value, count):
        return level_shift(value, count, n_exp)

    any_space = pl.BlockSpec(memory_space=pl.ANY)
    smem = pl.BlockSpec(memory_space=pltpu.SMEM)
    params = pltpu.CompilerParams(dimension_semantics=("arbitrary",), vmem_limit_bytes=VMEM_LIMIT)

    def by_expert(*shape):
        return pl.BlockSpec((1,) + shape, lambda e: (e,) + (0,) * len(shape))

    def whole(*shape):
        return pl.BlockSpec(shape, lambda e: (0,) * len(shape))

    def sds(shape, dtype):
        return jax.ShapeDtypeStruct(shape, dtype)

    def cost(gflop, mbyte):
        return pl.CostEstimate(flops=gflop * 10**6, bytes_accessed=mbyte * 10**3, transcendentals=0)

    def cut_blocks(word, blocks, size, wanted, name):
        plan, rows = [], []
        for out, items in enumerate(wanted):
            rows.append(0)
            for i, flip in items:
                plan.append((i, flip, out, rows[out]))
                rows[out] += blocks[i].shape[0]
        return pl.pallas_call(
            functools.partial(cut_kernel, size, plan),
            in_specs=[smem] + [any_space] * len(blocks),
            out_specs=[any_space] * len(wanted),
            out_shape=[sds((n, size), BF16) for n in rows],
            scratch_shapes=[pltpu.SemaphoreType.DMA((len(plan),))],
            cost_estimate=cost(0, 2),
            name=name,
        )(word, *blocks)

    def cut_far(blocks, name):
        return cut_blocks(far_word, blocks, width // 2, [[(i, 1) for i in range(len(blocks))]], name)[0]

    by_columns = pl.BlockSpec((local, tile, hidden), lambda j: (0, j, 0))
    weight_spec = by_expert(width, hidden)
    parts = n_exp
    cfg = (parts, local, cap, cap_pad, top)

    totals = jnp.sum(probs, axis=1, keepdims=True)
    share = probs / totals
    meta = jnp.concatenate([routes.astype(BF16)] + split3(share), axis=1)
    meta = jnp.pad(meta, ((0, 0), (0, LANES - 4 * top)))

    x_own = jnp.concatenate([tokens, meta], axis=1)
    x_mid = shift(x_own, mid)
    x_own_pair = pair(x_own)
    x_mid, x_own, cot = fence(x_mid, x_own, cotangent)
    x_rest = [shift(x_own, k) for k in rest]
    x_mid_pair = pair(x_mid)
    c_own_pair = pair(cot)
    x_rest_pair = [pair(block) for block in x_rest]
    x_landed, cot, x_own_pair, x_mid_pair, c_own_pair = fence(x_rest, cot, x_own_pair, x_mid_pair, c_own_pair)

    c_mid = shift(cot, mid)
    x_far = swap(cut_far([x_own, x_mid] + x_landed, "cut_x"), far_bit, n_dp)
    x_rest_pair, c_mid, cot = fence(x_rest_pair, c_mid, cot)
    c_rest = [shift(cot, k) for k in rest]
    c_mid_pair = pair(c_mid)
    x_far_pair = swap(cut_far([x_own_pair, x_mid_pair] + x_rest_pair, "cut_x_pair"), far_bit, n_dp)
    pre, act, info, pick, combine, x_keep = pl.pallas_call(
        functools.partial(hidden_kernel, cfg),
        grid=(local,),
        in_specs=[smem] * 2 + [any_space] * parts + [weight_spec] * 2,
        out_specs=[by_expert(cap, 2 * hidden), by_expert(cap, hidden + LANES), by_expert(cap, LANES),
                   whole(local * cap, total), whole(total, local * cap_pad), whole(total, width // 2)],
        out_shape=[sds((local, cap, 2 * hidden), F32), sds((local, cap, hidden + LANES), BF16),
                   sds((local, cap, LANES), F32), sds((local * cap, total), BF16), sds((total, local * cap_pad), BF16),
                   sds((total, width // 2), BF16)],
        scratch_shapes=[
            pltpu.VMEM((total, wide), BF16),
            pltpu.VMEM((local * cap, wide), BF16),
            pltpu.SemaphoreType.DMA((parts,)),
        ],
        compiler_params=params,
        cost_estimate=cost(6, 20),
        name="hidden",
    )(first, far_word, x_own, x_mid, *x_rest, x_own_pair, x_mid_pair, *x_rest_pair, w_gate, w_up)
    act, c_rest, c_mid_pair, x_far = fence(act, c_rest, c_mid_pair, x_far)

    c_rest_pair = [pair(block) for block in c_rest]
    act_far = swap(act, far_bit, n_dp)
    c_far = swap(cut_far([cot, c_mid] + c_rest, "cut_c"), far_bit, n_dp)
    level_rows = [line] + [tok_rows] * levels
    level_specs = [whole(rows, width) for rows in level_rows]
    mixed_keep, mixed_own, mixed_mid, *mixed_rest = pl.pallas_call(
        functools.partial(mixed_kernel, (local, cap, cap_pad)),
        grid=(width // tile,),
        in_specs=[whole(local, cap, hidden + LANES), whole(total, local * cap_pad), by_columns],
        out_specs=level_specs,
        out_shape=[sds((rows, width), BF16) for rows in level_rows],
        scratch_shapes=[pltpu.VMEM((total, local * hidden), BF16)],
        compiler_params=params,
        cost_estimate=cost(6, 10),
        name="mixed",
    )(act, combine, w_down)
    c_rest_pair, mixed_keep, mixed_own, mixed_mid, mixed_rest, x_far_pair = fence(
        c_rest_pair, mixed_keep, mixed_own, mixed_mid, mixed_rest, x_far_pair)

    def back_rows(keep, got):
        return keep.astype(F32) + got.astype(F32)

    def sum_back(keep, got, i):
        here = slice((i + 1) * tok_rows, (i + 2) * tok_rows)
        return back_rows(keep[here], got).astype(BF16)

    def finish(keep, own, landed):
        return sum([part.astype(F32) for part in landed], back_rows(keep[:tok_rows], own))

    early = 2
    mixed_got = [pair(block) for block in [mixed_mid] + mixed_rest]
    d_gate, d_up, tail, c_keep, c_give = pl.pallas_call(
        functools.partial(grad_kernel, cfg),
        grid=(local,),
        in_specs=[smem] + [any_space] * parts + [whole(local * cap, total), whole(total, local * cap_pad), weight_spec,
                                                 by_expert(cap, 2 * hidden), by_expert(cap, LANES)],
        out_specs=[by_expert(cap, hidden)] * 2 + [whole(total, LANES), whole(total, width // 2), whole(line, width // 2)],
        out_shape=[sds((local, cap, hidden), BF16)] * 2 + [sds((total, LANES), BF16),
                   sds((total, width // 2), BF16), sds((line, width // 2), BF16)],
        scratch_shapes=[
            pltpu.VMEM((total, width), BF16),
            pltpu.VMEM((local * cap, width), BF16),
            pltpu.VMEM((local * cap_pad, LANES), BF16),
            pltpu.SemaphoreType.DMA((parts,)),
        ],
        compiler_params=params,
        cost_estimate=cost(6, 12),
        name="hidden_grads",
    )(far_word, cot, c_mid, *c_rest, c_own_pair, c_mid_pair, *c_rest_pair, pick, combine, w_down, pre, info)
    d_gate, d_up, tail, c_give, mixed_own, mixed_got[:early], act_far = fence(
        d_gate, d_up, tail, c_give, mixed_own, mixed_got[:early], act_far)

    sums = [sum_back(mixed_keep, got, i) for i, got in enumerate(mixed_got[:early])]
    sums, d_gate, d_up, tail = fence(sums, d_gate, d_up, tail)
    mixed_back = [shift(value, -hops[i]) for i, value in enumerate(sums)]
    c_far_pair = swap(c_give, far_bit, n_dp)
    wide_specs = [whole(rows, wide) for rows in level_rows]
    input_keep, input_own, input_mid, *input_rest = pl.pallas_call(
        functools.partial(input_kernel, (local, cap, cap_pad)),
        grid=(width // tile,),
        in_specs=[whole(local, cap, hidden)] * 2 + [whole(total, local * cap_pad), whole(total, LANES),
                                                    by_columns, by_columns],
        out_specs=wide_specs,
        out_shape=[sds((rows, wide), BF16) for rows in level_rows],
        scratch_shapes=[pltpu.VMEM((local * cap_pad, tile), BF16)],
        compiler_params=params,
        cost_estimate=cost(6, 16),
        name="input_grads",
    )(d_gate, d_up, combine, tail, w_gate, w_up)
    (input_keep, input_own, input_mid, input_rest, mixed_got[early:], mixed_back[0], c_far_pair, c_far, d_gate, d_up) = fence(
        input_keep, input_own, input_mid, input_rest, mixed_got[early:], mixed_back[0], c_far_pair, c_far, d_gate, d_up)

    input_got = [pair(block) for block in [input_mid] + input_rest[:1]]
    mixed_back += [shift(sum_back(mixed_keep, got, early + i), -hops[early + i])
                   for i, got in enumerate(mixed_got[early:])]
    gate_far = swap(d_gate, far_bit, n_dp)
    near_plan = [[(i, 1) for i in range(6)], [(i, 0) for i in range(3)], [(i, 0) for i in range(3, 6)]]
    give, x_keep, c_keep = cut_blocks(
        near_word, [x_keep, x_far, x_far_pair, c_keep, c_far, c_far_pair], columns, near_plan, "cut_near")
    sums = [sum_back(input_keep, got, i) for i, got in enumerate(input_got)]
    sums, input_rest, mixed_back, gate_far, d_up, give = fence(sums, input_rest, mixed_back, gate_far, d_up, give)
    input_back = [shift(value, -hops[i]) for i, value in enumerate(sums)]
    up_far = swap(d_up, far_bit, n_dp)
    input_got = [pair(block) for block in input_rest[1:]]
    got_near = swap(give, 1, n_dp)
    act_near = swap(act, 1, n_dp)
    act_far_near = swap(act_far, 1, n_dp)
    def halves(value):
        return value.reshape(2, total, columns)

    x_rows, down_grad = pl.pallas_call(
        functools.partial(down_kernel, cap),
        grid=(local,),
        in_specs=[whole(2, total, columns), whole(4, total, columns), whole(2, total, columns)] + [by_expert(cap, hidden + LANES)] * 4,
        out_specs=[by_expert(n_dp * cap, columns), by_expert(columns, hidden)],
        out_shape=[sds((local, n_dp * cap, columns), BF16), sds((local, columns, hidden), BF16)],
        scratch_shapes=[pltpu.VMEM((n_dp * cap, columns), BF16), pltpu.VMEM((n_dp * cap, hidden), BF16)],
        compiler_params=params,
        cost_estimate=cost(6, 12),
        name="down_grads",
    )(halves(x_keep), got_near.reshape(4, total, columns), halves(c_keep), act, act_far, act_near, act_far_near)

    gate_near, up_near = swap(d_gate, 1, n_dp), swap(d_up, 1, n_dp)
    gate_far_near = swap(gate_far, 1, n_dp)
    sums, input_back, input_own, mixed_own, up_far, x_rows = fence(
        [sum_back(input_keep, got, 2 + i) for i, got in enumerate(input_got)],
        input_back, input_own, mixed_own, up_far, x_rows)
    input_back += [shift(value, -hops[2 + i]) for i, value in enumerate(sums)]
    mixed_own = pair(mixed_own)
    input_own = pair(input_own)
    mixed = finish(mixed_keep, mixed_own, mixed_back).astype(BF16)
    up_far_near = swap(up_far, 1, n_dp)
    gate_grad, up_grad = pl.pallas_call(
        functools.partial(gate_kernel, cap),
        grid=(local,),
        in_specs=[by_expert(n_dp * cap, columns)] + [by_expert(cap, hidden)] * 8,
        out_specs=[by_expert(columns, hidden)] * 2,
        out_shape=[sds((local, columns, hidden), BF16)] * 2,
        scratch_shapes=[pltpu.VMEM((n_dp * cap, 2 * hidden), BF16)],
        compiler_params=params,
        cost_estimate=cost(3, 10),
        name="gate_grads",
    )(x_rows, d_gate, gate_far, gate_near, gate_far_near, d_up, up_far, up_near, up_far_near)

    back = finish(input_keep, input_own, input_back)
    token_grad = back[:, :width].astype(BF16)
    tail = back[:, width:]
    slot_sg = tail[:, :top] + tail[:, top:2 * top] + tail[:, 2 * top:3 * top]
    prob_grad = (slot_sg - jnp.sum(share * slot_sg, axis=1, keepdims=True)) / totals
    return mixed, token_grad, prob_grad, gate_grad, up_grad, down_grad


def solution(mesh):
    rows = P(("expert", "dp"), None)
    weight = P("expert", None, None)
    grad = P("expert", "dp", None)
    return jax.shard_map(
        shards,
        mesh=mesh,
        in_specs=(rows, rows, rows, rows, weight, weight, weight),
        out_specs=(rows, rows, rows, grad, grad, grad),
        check_vma=False,
    )
```

```python
import functools

import jax
import jax.numpy as jnp
from jax import lax
from jax.experimental import pallas as pl
from jax.experimental.pallas import tpu as pltpu
from jax.sharding import PartitionSpec as P


F32 = jnp.float32
BF16 = jnp.bfloat16
LANES = 128
VMEM_LIMIT = 60 * 1024 * 1024


def round_up(value, unit):
    return -(-value // unit) * unit


def dot(a, b):
    return jnp.dot(a, b, preferred_element_type=F32)


def dot_nt(a, b):
    return lax.dot_general(a, b, (((1,), (1,)), ((), ())), preferred_element_type=F32)


def dot_tn(a, b):
    return lax.dot_general(a, b, (((0,), (0,)), ((), ())), preferred_element_type=F32)


def iota(shape, dim):
    return lax.broadcasted_iota(jnp.int32, shape, dim)


def load_blocks(blocks, held, sems):
    copies, start = [], 0
    for i, block in enumerate(blocks):
        size = block.shape[0]
        copies.append(pltpu.make_async_copy(block, held.at[pl.ds(start, size), :], sems.at[i]))
        start += size
    for copy in copies:
        copy.start()
    for copy in copies:
        copy.wait()


def tiles(width, tile=512):
    return [(start, min(start + tile, width)) for start in range(0, width, tile)]


def half_of(which, width):
    return pl.ds(pl.multiple_of(which * (width // 2), LANES), width // 2)


def hidden_kernel(cfg, first_ref, far_ref, *refs):
    parts, local, cap, cap_pad, top = cfg
    blocks, refs = refs[:parts], refs[parts:]
    gate_ref, up_ref, pre_ref, act_ref, info_ref, pick_ref, combine_ref, keep_ref, held, rows_ref, sems = refs
    expert = pl.program_id(0)
    tokens = held.shape[0]
    width, hidden = gate_ref.shape[1:]

    @pl.when(expert == 0)
    def _():
        load_blocks(blocks, held, sems)
        meta = held[:, width:].astype(F32).astype(jnp.int32)
        lane = iota(meta.shape, 1)
        hits = jnp.zeros(meta.shape, F32)
        for i in range(local):
            named = (meta == first_ref[0] + i) & (lane < top)
            hit = jnp.sum(jnp.where(named, 1.0, 0.0), axis=1, keepdims=True)
            hits = hits + jnp.where(lane == i, hit, 0.0)
        step = min(tokens, 256)
        below = (iota((step, step), 0) >= iota((step, step), 1)).astype(F32).astype(BF16)
        carry = jnp.zeros((1, LANES), F32)
        slots = []
        for start in range(0, tokens, step):
            part = hits[start:start + step]
            rank = dot(below, part.astype(BF16)) + carry
            carry = rank[step - 1:step]
            slots.append(jnp.where(part > 0.0, rank - 1.0, -1.0))
        slots = jnp.concatenate(slots, axis=0)
        slots_t = jnp.transpose(slots)
        places = iota((tokens, cap_pad), 1).astype(F32)
        places_t = iota((cap, tokens), 0).astype(F32)
        for i in range(local):
            hit = slots[:, i:i + 1] == places
            combine_ref[:, i * cap_pad:(i + 1) * cap_pad] = jnp.where(hit, 1.0, 0.0).astype(BF16)
            hit = slots_t[i:i + 1, :] == places_t
            pick_ref[i * cap:(i + 1) * cap, :] = jnp.where(hit, 1.0, 0.0).astype(BF16)
        for start, stop in tiles(held.shape[1]):
            rows_ref[:, start:stop] = dot(pick_ref[...], held[:, start:stop]).astype(BF16)
        keep_ref[...] = held[:, half_of(far_ref[0], width)]

    here = pl.ds(pl.multiple_of(expert * cap, 16), cap)
    pick = pick_ref[here, :].astype(F32)
    token = jnp.sum(pick * iota(pick.shape, 1).astype(F32), axis=1, keepdims=True)
    token = jnp.where(jnp.sum(pick, axis=1, keepdims=True) > 0.0, token, -128.0).astype(jnp.int32)
    meta = rows_ref[here, width:].astype(F32)
    lane = iota(meta.shape, 1)
    named = (meta.astype(jnp.int32) == first_ref[0] + expert) & (lane < top)
    shares = sum(pltpu.roll(meta, LANES - top * (i + 1), 1) for i in range(3))
    share = jnp.sum(jnp.where(named, shares, 0.0), axis=1, keepdims=True)
    info_ref[0] = jnp.where(lane < top, jnp.where(named, 1.0, 0.0), share)

    rows = rows_ref[here, :width]
    gate_pre = dot(rows, gate_ref[0])
    up_pre = dot(rows, up_ref[0])
    pre_ref[0, :, :hidden] = gate_pre
    pre_ref[0, :, hidden:] = up_pre
    active = gate_pre * jax.nn.sigmoid(gate_pre) * up_pre
    act_ref[0, :, :hidden] = (share * active).astype(BF16)
    token_pair = jnp.where(lane == 0, token >> 7, jnp.where(lane == 1, token & 127, 0))
    act_ref[0, :, hidden:] = token_pair.astype(F32).astype(BF16)


def store_parts(value, here, refs):
    start = 0
    for ref in refs:
        ref[:, here] = value[start:start + ref.shape[0]]
        start += ref.shape[0]


def mixed_kernel(cfg, act_ref, combine_ref, down_ref, *refs):
    local, cap, cap_pad = cfg
    outs, spread = refs[:-1], refs[-1]
    hidden = down_ref.shape[2]
    tile = down_ref.shape[1]
    step = pl.program_id(0)

    @pl.when(step == 0)
    def _():
        for e in range(local):
            here = combine_ref[:, e * cap_pad:e * cap_pad + cap]
            spread[:, e * hidden:(e + 1) * hidden] = dot(here, act_ref[e, :, :hidden]).astype(BF16)

    total = dot_nt(spread[:, :hidden], down_ref[0])
    for e in range(1, local):
        total = total + dot_nt(spread[:, e * hidden:(e + 1) * hidden], down_ref[e])
    store_parts(total.astype(BF16), pl.ds(pl.multiple_of(step * tile, tile), tile), outs)


def grad_kernel(cfg, far_ref, *refs):
    parts, local, cap, cap_pad, top = cfg
    blocks, refs = refs[:parts], refs[parts:]
    pick_ref, combine_ref, down_ref, pre_ref, info_ref, d_gate_ref, d_up_ref, tail_ref, keep_ref, give_ref = refs[:10]
    held, rows_ref, tails, sems = refs[10:]
    expert = pl.program_id(0)
    hidden = down_ref.shape[2]

    @pl.when(expert == 0)
    def _():
        load_blocks(blocks, held, sems)
        tails[...] = jnp.zeros(tails.shape, BF16)
        for start, stop in tiles(held.shape[1]):
            rows_ref[:, start:stop] = dot(pick_ref[...], held[:, start:stop]).astype(BF16)
        width = held.shape[1]
        keep_ref[...] = held[:, half_of(far_ref[0], width)]
        give_ref[...] = held[give_ref.shape[0]:, half_of(1 - far_ref[0], width)]

    info = info_ref[0]
    lane = iota(info.shape, 1)
    share = info[:, top:top + 1]
    gate_pre, up_pre = pre_ref[0, :, :hidden], pre_ref[0, :, hidden:]
    sig = jax.nn.sigmoid(gate_pre)
    silu = gate_pre * sig
    d_raw = dot(rows_ref[pl.ds(pl.multiple_of(expert * cap, 16), cap), :], down_ref[0])
    share_grad = jnp.sum(silu * up_pre * d_raw, axis=1, keepdims=True)
    d_active = share * d_raw
    d_gate_ref[0] = (d_active * up_pre * sig * (1.0 + gate_pre * (1.0 - sig))).astype(BF16)
    d_up_ref[0] = (d_active * silu).astype(BF16)
    placed = jnp.where((lane < top) & (info > 0.0), share_grad, 0.0)
    high = placed.astype(BF16)
    rest = placed - high.astype(F32)
    middle = rest.astype(BF16)
    low = (rest - middle.astype(F32)).astype(BF16)
    tail = high.astype(F32) + pltpu.roll(middle.astype(F32), top, 1) + pltpu.roll(low.astype(F32), 2 * top, 1)
    tails[pl.ds(pl.multiple_of(expert * cap_pad, cap_pad), cap), :] = tail.astype(BF16)

    @pl.when(expert == local - 1)
    def _():
        tail_ref[...] = dot(combine_ref[...], tails[...]).astype(BF16)


def input_kernel(cfg, d_gate_ref, d_up_ref, combine_ref, tail_ref, gate_ref, up_ref, *refs):
    local, cap, cap_pad = cfg
    outs, rows = refs[:-1], refs[-1]
    tile, hidden = gate_ref.shape[1:]
    step = pl.program_id(0)

    @pl.when(step == 0)
    def _():
        rows[...] = jnp.zeros(rows.shape, BF16)
        width = outs[0].shape[1] - LANES
        store_parts(tail_ref[...], slice(width, width + LANES), outs)

    for e in range(local):
        part = dot_nt(d_gate_ref[e], gate_ref[e]) + dot_nt(d_up_ref[e], up_ref[e])
        rows[e * cap_pad:e * cap_pad + cap, :] = part.astype(BF16)
    total = dot(combine_ref[...], rows[...]).astype(BF16)
    store_parts(total, pl.ds(pl.multiple_of(step * tile, tile), tile), outs)


def down_kernel(cap, x_ref, near_ref, c_ref, *refs):
    act_refs, (rows_ref, down_ref, c_rows, acts) = refs[:-4], refs[-4:]
    hidden = down_ref.shape[2]
    x_parts = [x_ref.at[0], x_ref.at[1], near_ref.at[0], near_ref.at[1]]
    c_parts = [c_ref.at[0], c_ref.at[1], near_ref.at[2], near_ref.at[3]]
    for k, (x_part, c_part, act_ref) in enumerate(zip(x_parts, c_parts, act_refs)):
        pair = act_ref[0, :, hidden:].astype(F32)
        token = pair[:, 0:1] * 128.0 + pair[:, 1:2]
        pick = jnp.where(token == iota((cap, x_part.shape[0]), 1).astype(F32), 1.0, 0.0).astype(BF16)
        here = slice(k * cap, (k + 1) * cap)
        rows_ref[0, here, :] = dot(pick, x_part[...]).astype(BF16)
        c_rows[here, :] = dot(pick, c_part[...]).astype(BF16)
        acts[here, :] = act_ref[0, :, :hidden]
    down_ref[0] = dot_tn(c_rows[...], acts[...]).astype(BF16)


def gate_kernel(cap, rows_ref, *refs):
    count = (len(refs) - 3) // 2
    gate_ref, up_ref, grads = refs[2 * count:]
    hidden = gate_ref.shape[2]
    for k in range(count):
        grads[k * cap:(k + 1) * cap, :hidden] = refs[k][0]
        grads[k * cap:(k + 1) * cap, hidden:] = refs[count + k][0]
    both = dot_tn(rows_ref[0], grads[...])
    gate_ref[0] = both[:, :hidden].astype(BF16)
    up_ref[0] = both[:, hidden:].astype(BF16)


def cut_kernel(half, plan, word_ref, *refs):
    count = 1 + max(i for i, _, _, _ in plan)
    blocks, outs, sems = refs[:count], refs[count:-1], refs[-1]
    copies = []
    for i, flip, out, row in plan:
        which = 1 - word_ref[0] if flip else word_ref[0]
        here = pl.ds(pl.multiple_of(which * half, LANES), half)
        there = outs[out].at[pl.ds(row, blocks[i].shape[0]), :]
        copies.append(pltpu.make_async_copy(blocks[i].at[:, here], there, sems.at[len(copies)]))
    for copy in copies:
        copy.start()
    for copy in copies:
        copy.wait()


def swap(value, bit, count):
    return lax.ppermute(value, "dp", [(i, i ^ bit) for i in range(count)])


def pair_swap(value, count):
    return lax.ppermute(value, "expert", [(i, i ^ 1) for i in range(count)])


def level_shift(value, hops, count):
    return lax.ppermute(value, "expert", [(i, (i + 2 * hops) % count) for i in range(count)])


def fence(*values):
    leaves, tree = jax.tree.flatten(values)
    return jax.tree.unflatten(tree, lax.optimization_barrier(tuple(leaves)))


def split3(value):
    high = lax.reduce_precision(value, 8, 7)
    rest = value - high
    middle = lax.reduce_precision(rest, 8, 7)
    return [high.astype(BF16), middle.astype(BF16), (rest - middle).astype(BF16)]


def shards(tokens, routes, probs, cotangent, w_gate, w_up, w_down):
    tok_rows, top = routes.shape
    local, width, hidden = w_gate.shape
    n_exp = lax.axis_size("expert")
    n_dp = lax.axis_size("dp")
    experts = local * n_exp
    cap = 5 * tok_rows * top // (4 * experts) * n_exp
    cap_pad = round_up(cap, LANES)
    total = n_exp * tok_rows
    levels = n_exp // 2
    line = levels * tok_rows
    wide = width + LANES
    tile = min(width, 512)
    columns = width // n_dp
    far_bit = n_dp // 2
    my_dp = lax.axis_index("dp")
    far = jnp.where((my_dp & far_bit) > 0, 1, 0)
    near = jnp.where((my_dp & 1) > 0, 1, 0)
    near_word = near.astype(jnp.int32).reshape(1)
    far_word = far.astype(jnp.int32).reshape(1)
    first = (lax.axis_index("expert") * local).astype(jnp.int32).reshape(1)
    hops = sorted(range(1, levels), key=lambda k: abs(2 * k - levels))
    mid, rest = hops[0], hops[1:]

    def pair(value):
        return pair_swap(value, n_exp)

    def shift(value, count):
        return level_shift(value, count, n_exp)

    any_space = pl.BlockSpec(memory_space=pl.ANY)
    smem = pl.BlockSpec(memory_space=pltpu.SMEM)
    params = pltpu.CompilerParams(dimension_semantics=("arbitrary",), vmem_limit_bytes=VMEM_LIMIT)

    def by_expert(*shape):
        return pl.BlockSpec((1,) + shape, lambda e: (e,) + (0,) * len(shape))

    def whole(*shape):
        return pl.BlockSpec(shape, lambda e: (0,) * len(shape))

    def sds(shape, dtype):
        return jax.ShapeDtypeStruct(shape, dtype)

    def cost(gflop, mbyte):
        return pl.CostEstimate(flops=gflop * 10**6, bytes_accessed=mbyte * 10**3, transcendentals=0)

    def cut_blocks(word, blocks, size, wanted, name):
        plan, rows = [], []
        for out, items in enumerate(wanted):
            rows.append(0)
            for i, flip in items:
                plan.append((i, flip, out, rows[out]))
                rows[out] += blocks[i].shape[0]
        return pl.pallas_call(
            functools.partial(cut_kernel, size, plan),
            in_specs=[smem] + [any_space] * len(blocks),
            out_specs=[pl.BlockSpec(memory_space=pltpu.VMEM)] * len(wanted),
            out_shape=[sds((n, size), BF16) for n in rows],
            scratch_shapes=[pltpu.SemaphoreType.DMA((len(plan),))],
            compiler_params=pltpu.CompilerParams(vmem_limit_bytes=VMEM_LIMIT),
            cost_estimate=cost(0, 2),
            name=name,
        )(word, *blocks)

    def cut_far(blocks, name):
        return cut_blocks(far_word, blocks, width // 2, [[(i, 1) for i in range(len(blocks))]], name)[0]

    by_columns = pl.BlockSpec((local, tile, hidden), lambda j: (0, j, 0))
    weight_spec = by_expert(width, hidden)
    parts = n_exp
    cfg = (parts, local, cap, cap_pad, top)

    totals = jnp.sum(probs, axis=1, keepdims=True)
    share = probs / totals
    meta = jnp.concatenate([routes.astype(BF16)] + split3(share), axis=1)
    meta = jnp.pad(meta, ((0, 0), (0, LANES - 4 * top)))

    x_own = jnp.concatenate([tokens, meta], axis=1)
    x_mid = shift(x_own, mid)
    x_own_pair = pair(x_own)
    c_own_pair = pair(cotangent)
    x_mid, x_own, cot, x_own_pair, c_own_pair = fence(x_mid, x_own, cotangent, x_own_pair, c_own_pair)
    x_rest = [shift(x_own, k) for k in rest]
    x_mid_pair = pair(x_mid)
    x_rest_pair = [pair(block) for block in x_rest]
    x_landed, cot, x_mid_pair = fence(x_rest, cot, x_mid_pair)

    c_mid = shift(cot, mid)
    x_far = swap(cut_far([x_own, x_mid] + x_landed, "cut_x"), far_bit, n_dp)
    x_rest_pair, c_mid, cot = fence(x_rest_pair, c_mid, cot)
    c_rest = [shift(cot, k) for k in rest]
    c_mid_pair = pair(c_mid)
    x_far_pair = swap(cut_far([x_own_pair, x_mid_pair] + x_rest_pair, "cut_x_pair"), far_bit, n_dp)
    pre, act, info, pick, combine, x_keep = pl.pallas_call(
        functools.partial(hidden_kernel, cfg),
        grid=(local,),
        in_specs=[smem] * 2 + [any_space] * parts + [weight_spec] * 2,
        out_specs=[by_expert(cap, 2 * hidden), by_expert(cap, hidden + LANES), by_expert(cap, LANES),
                   whole(local * cap, total), whole(total, local * cap_pad), whole(total, width // 2)],
        out_shape=[sds((local, cap, 2 * hidden), F32), sds((local, cap, hidden + LANES), BF16),
                   sds((local, cap, LANES), F32), sds((local * cap, total), BF16), sds((total, local * cap_pad), BF16),
                   sds((total, width // 2), BF16)],
        scratch_shapes=[
            pltpu.VMEM((total, wide), BF16),
            pltpu.VMEM((local * cap, wide), BF16),
            pltpu.SemaphoreType.DMA((parts,)),
        ],
        compiler_params=params,
        cost_estimate=cost(6, 20),
        name="hidden",
    )(first, far_word, x_own, x_mid, *x_rest, x_own_pair, x_mid_pair, *x_rest_pair, w_gate, w_up)
    act, c_rest, c_mid_pair, x_far = fence(act, c_rest, c_mid_pair, x_far)

    c_rest_pair = [pair(block) for block in c_rest]
    act_far = swap(act, far_bit, n_dp)
    c_far = swap(cut_far([cot, c_mid] + c_rest, "cut_c"), far_bit, n_dp)
    level_rows = [line] + [tok_rows] * levels
    level_specs = [whole(rows, width) for rows in level_rows]
    mixed_keep, mixed_own, mixed_mid, *mixed_rest = pl.pallas_call(
        functools.partial(mixed_kernel, (local, cap, cap_pad)),
        grid=(width // tile,),
        in_specs=[whole(local, cap, hidden + LANES), whole(total, local * cap_pad), by_columns],
        out_specs=level_specs,
        out_shape=[sds((rows, width), BF16) for rows in level_rows],
        scratch_shapes=[pltpu.VMEM((total, local * hidden), BF16)],
        compiler_params=params,
        cost_estimate=cost(6, 10),
        name="mixed",
    )(act, combine, w_down)
    c_rest_pair, mixed_keep, mixed_own, mixed_mid, mixed_rest, x_far_pair = fence(
        c_rest_pair, mixed_keep, mixed_own, mixed_mid, mixed_rest, x_far_pair)

    def back_rows(keep, got):
        return keep.astype(F32) + got.astype(F32)

    def sum_back(keep, got, i):
        here = slice((i + 1) * tok_rows, (i + 2) * tok_rows)
        return back_rows(keep[here], got).astype(BF16)

    def finish(keep, own, landed):
        return sum([part.astype(F32) for part in landed], back_rows(keep[:tok_rows], own))

    early = 2
    mixed_got = [pair(block) for block in [mixed_mid] + mixed_rest]
    d_gate, d_up, tail, c_keep, c_give = pl.pallas_call(
        functools.partial(grad_kernel, cfg),
        grid=(local,),
        in_specs=[smem] + [any_space] * parts + [whole(local * cap, total), whole(total, local * cap_pad), weight_spec,
                                                 by_expert(cap, 2 * hidden), by_expert(cap, LANES)],
        out_specs=[by_expert(cap, hidden)] * 2 + [whole(total, LANES), whole(total, width // 2), whole(line, width // 2)],
        out_shape=[sds((local, cap, hidden), BF16)] * 2 + [sds((total, LANES), BF16),
                   sds((total, width // 2), BF16), sds((line, width // 2), BF16)],
        scratch_shapes=[
            pltpu.VMEM((total, width), BF16),
            pltpu.VMEM((local * cap, width), BF16),
            pltpu.VMEM((local * cap_pad, LANES), BF16),
            pltpu.SemaphoreType.DMA((parts,)),
        ],
        compiler_params=params,
        cost_estimate=cost(6, 12),
        name="hidden_grads",
    )(far_word, cot, c_mid, *c_rest, c_own_pair, c_mid_pair, *c_rest_pair, pick, combine, w_down, pre, info)
    d_gate, d_up, tail, c_give, mixed_own, mixed_got[:early], act_far = fence(
        d_gate, d_up, tail, c_give, mixed_own, mixed_got[:early], act_far)

    sums = [sum_back(mixed_keep, got, i) for i, got in enumerate(mixed_got[:early])]
    sums, d_gate, d_up, tail = fence(sums, d_gate, d_up, tail)
    mixed_back = [shift(value, -hops[i]) for i, value in enumerate(sums)]
    c_far_pair = swap(c_give, far_bit, n_dp)
    wide_specs = [whole(rows, wide) for rows in level_rows]
    input_keep, input_own, input_mid, *input_rest = pl.pallas_call(
        functools.partial(input_kernel, (local, cap, cap_pad)),
        grid=(width // tile,),
        in_specs=[whole(local, cap, hidden)] * 2 + [whole(total, local * cap_pad), whole(total, LANES),
                                                    by_columns, by_columns],
        out_specs=wide_specs,
        out_shape=[sds((rows, wide), BF16) for rows in level_rows],
        scratch_shapes=[pltpu.VMEM((local * cap_pad, tile), BF16)],
        compiler_params=params,
        cost_estimate=cost(6, 16),
        name="input_grads",
    )(d_gate, d_up, combine, tail, w_gate, w_up)
    (input_keep, input_own, input_mid, input_rest, mixed_got[early:], mixed_back[0], c_far_pair, c_far, d_gate, d_up) = fence(
        input_keep, input_own, input_mid, input_rest, mixed_got[early:], mixed_back[0], c_far_pair, c_far, d_gate, d_up)

    input_got = [pair(block) for block in [input_mid] + input_rest[:1]]
    mixed_back += [shift(sum_back(mixed_keep, got, early + i), -hops[early + i])
                   for i, got in enumerate(mixed_got[early:])]
    gate_far = swap(d_gate, far_bit, n_dp)
    near_plan = [[(i, 1) for i in range(6)], [(i, 0) for i in range(3)], [(i, 0) for i in range(3, 6)]]
    give, x_keep, c_keep = cut_blocks(
        near_word, [x_keep, x_far, x_far_pair, c_keep, c_far, c_far_pair], columns, near_plan, "cut_near")
    sums = [sum_back(input_keep, got, i) for i, got in enumerate(input_got)]
    sums, input_rest, mixed_back, gate_far, d_up, give = fence(sums, input_rest, mixed_back, gate_far, d_up, give)
    input_back = [shift(value, -hops[i]) for i, value in enumerate(sums)]
    up_far = swap(d_up, far_bit, n_dp)
    input_got = [pair(block) for block in input_rest[1:]]
    got_near = swap(give, 1, n_dp)
    act_near = swap(act, 1, n_dp)
    act_far_near = swap(act_far, 1, n_dp)
    def halves(value):
        return value.reshape(2, total, columns)

    x_rows, down_grad = pl.pallas_call(
        functools.partial(down_kernel, cap),
        grid=(local,),
        in_specs=[whole(2, total, columns), whole(4, total, columns), whole(2, total, columns)] + [by_expert(cap, hidden + LANES)] * 4,
        out_specs=[by_expert(n_dp * cap, columns), by_expert(columns, hidden)],
        out_shape=[sds((local, n_dp * cap, columns), BF16), sds((local, columns, hidden), BF16)],
        scratch_shapes=[pltpu.VMEM((n_dp * cap, columns), BF16), pltpu.VMEM((n_dp * cap, hidden), BF16)],
        compiler_params=params,
        cost_estimate=cost(6, 12),
        name="down_grads",
    )(halves(x_keep), got_near.reshape(4, total, columns), halves(c_keep), act, act_far, act_near, act_far_near)

    gate_near, up_near = swap(d_gate, 1, n_dp), swap(d_up, 1, n_dp)
    gate_far_near = swap(gate_far, 1, n_dp)
    sums, input_back, input_own, mixed_own, up_far, x_rows = fence(
        [sum_back(input_keep, got, 2 + i) for i, got in enumerate(input_got)],
        input_back, input_own, mixed_own, up_far, x_rows)
    input_back += [shift(value, -hops[2 + i]) for i, value in enumerate(sums)]
    mixed_own = pair(mixed_own)
    input_own = pair(input_own)
    mixed = finish(mixed_keep, mixed_own, mixed_back).astype(BF16)
    up_far_near = swap(up_far, 1, n_dp)
    gate_grad, up_grad = pl.pallas_call(
        functools.partial(gate_kernel, cap),
        grid=(local,),
        in_specs=[by_expert(n_dp * cap, columns)] + [by_expert(cap, hidden)] * 8,
        out_specs=[by_expert(columns, hidden)] * 2,
        out_shape=[sds((local, columns, hidden), BF16)] * 2,
        scratch_shapes=[pltpu.VMEM((n_dp * cap, 2 * hidden), BF16)],
        compiler_params=params,
        cost_estimate=cost(3, 10),
        name="gate_grads",
    )(x_rows, d_gate, gate_far, gate_near, gate_far_near, d_up, up_far, up_near, up_far_near)

    back = finish(input_keep, input_own, input_back)
    token_grad = back[:, :width].astype(BF16)
    tail = back[:, width:]
    slot_sg = tail[:, :top] + tail[:, top:2 * top] + tail[:, 2 * top:3 * top]
    prob_grad = (slot_sg - jnp.sum(share * slot_sg, axis=1, keepdims=True)) / totals
    return mixed, token_grad, prob_grad, gate_grad, up_grad, down_grad


def solution(mesh):
    rows = P(("expert", "dp"), None)
    weight = P("expert", None, None)
    grad = P("expert", "dp", None)
    return jax.shard_map(
        shards,
        mesh=mesh,
        in_specs=(rows, rows, rows, rows, weight, weight, weight),
        out_specs=(rows, rows, rows, grad, grad, grad),
        check_vma=False,
    )
```

```python
import functools

import jax
import jax.numpy as jnp
from jax import lax
from jax.experimental import pallas as pl
from jax.experimental.pallas import tpu as pltpu
from jax.sharding import PartitionSpec as P


F32 = jnp.float32
BF16 = jnp.bfloat16
LANES = 128
VMEM_LIMIT = 60 * 1024 * 1024


def round_up(value, unit):
    return -(-value // unit) * unit


def dot(a, b):
    return jnp.dot(a, b, preferred_element_type=F32)


def dot_nt(a, b):
    return lax.dot_general(a, b, (((1,), (1,)), ((), ())), preferred_element_type=F32)


def dot_tn(a, b):
    return lax.dot_general(a, b, (((0,), (0,)), ((), ())), preferred_element_type=F32)


def iota(shape, dim):
    return lax.broadcasted_iota(jnp.int32, shape, dim)


def load_blocks(blocks, held, sems):
    copies, start = [], 0
    for i, block in enumerate(blocks):
        size = block.shape[0]
        copies.append(pltpu.make_async_copy(block, held.at[pl.ds(start, size), :], sems.at[i]))
        start += size
    for copy in copies:
        copy.start()
    for copy in copies:
        copy.wait()


def tiles(width, tile=512):
    return [(start, min(start + tile, width)) for start in range(0, width, tile)]


def half_of(which, width):
    return pl.ds(pl.multiple_of(which * (width // 2), LANES), width // 2)


def hidden_kernel(cfg, first_ref, far_ref, *refs):
    parts, local, cap, cap_pad, top = cfg
    blocks, refs = refs[:parts], refs[parts:]
    gate_ref, up_ref, pre_ref, act_ref, info_ref, pick_ref, combine_ref, keep_ref, give_ref = refs[:9]
    held, rows_ref, sems = refs[9:]
    expert = pl.program_id(0)
    tokens = held.shape[0]
    width, hidden = gate_ref.shape[1:]

    @pl.when(expert == 0)
    def _():
        load_blocks(blocks, held, sems)
        meta = held[:, width:].astype(F32).astype(jnp.int32)
        lane = iota(meta.shape, 1)
        hits = jnp.zeros(meta.shape, F32)
        for i in range(local):
            named = (meta == first_ref[0] + i) & (lane < top)
            hit = jnp.sum(jnp.where(named, 1.0, 0.0), axis=1, keepdims=True)
            hits = hits + jnp.where(lane == i, hit, 0.0)
        step = min(tokens, 256)
        below = (iota((step, step), 0) >= iota((step, step), 1)).astype(F32).astype(BF16)
        carry = jnp.zeros((1, LANES), F32)
        slots = []
        for start in range(0, tokens, step):
            part = hits[start:start + step]
            rank = dot(below, part.astype(BF16)) + carry
            carry = rank[step - 1:step]
            slots.append(jnp.where(part > 0.0, rank - 1.0, -1.0))
        slots = jnp.concatenate(slots, axis=0)
        slots_t = jnp.transpose(slots)
        places = iota((tokens, cap_pad), 1).astype(F32)
        places_t = iota((cap, tokens), 0).astype(F32)
        for i in range(local):
            hit = slots[:, i:i + 1] == places
            combine_ref[:, i * cap_pad:(i + 1) * cap_pad] = jnp.where(hit, 1.0, 0.0).astype(BF16)
            hit = slots_t[i:i + 1, :] == places_t
            pick_ref[i * cap:(i + 1) * cap, :] = jnp.where(hit, 1.0, 0.0).astype(BF16)
        for start, stop in tiles(held.shape[1]):
            rows_ref[:, start:stop] = dot(pick_ref[...], held[:, start:stop]).astype(BF16)
        keep_ref[...] = held[:, half_of(far_ref[0], width)]
        give_ref[...] = held[give_ref.shape[0]:, half_of(1 - far_ref[0], width)]

    here = pl.ds(pl.multiple_of(expert * cap, 16), cap)
    pick = pick_ref[here, :].astype(F32)
    token = jnp.sum(pick * iota(pick.shape, 1).astype(F32), axis=1, keepdims=True)
    token = jnp.where(jnp.sum(pick, axis=1, keepdims=True) > 0.0, token, -128.0).astype(jnp.int32)
    meta = rows_ref[here, width:].astype(F32)
    lane = iota(meta.shape, 1)
    named = (meta.astype(jnp.int32) == first_ref[0] + expert) & (lane < top)
    shares = sum(pltpu.roll(meta, LANES - top * (i + 1), 1) for i in range(3))
    share = jnp.sum(jnp.where(named, shares, 0.0), axis=1, keepdims=True)
    info_ref[0] = jnp.where(lane < top, jnp.where(named, 1.0, 0.0), share)

    rows = rows_ref[here, :width]
    gate_pre = dot(rows, gate_ref[0])
    up_pre = dot(rows, up_ref[0])
    pre_ref[0, :, :hidden] = gate_pre
    pre_ref[0, :, hidden:] = up_pre
    active = gate_pre * jax.nn.sigmoid(gate_pre) * up_pre
    act_ref[0, :, :hidden] = (share * active).astype(BF16)
    token_pair = jnp.where(lane == 0, token >> 7, jnp.where(lane == 1, token & 127, 0))
    act_ref[0, :, hidden:] = token_pair.astype(F32).astype(BF16)


def store_parts(value, here, refs):
    keep_ref, mid_ref, rest_ref = refs
    line, size = keep_ref.shape[0], mid_ref.shape[0]
    keep_ref[:, here] = value[:line]
    mid_ref[:, here] = value[line + size:line + 2 * size]
    rest_ref[:line - 2 * size, here] = value[line + 2 * size:]
    rest_ref[line - 2 * size:, here] = value[line:line + size]


def mixed_kernel(cfg, far_ref, act_ref, combine_ref, down_ref, *refs):
    levels, local, cap, cap_pad = cfg
    blocks, refs = refs[:levels], refs[levels:]
    outs, give_ref, spread, sems = refs[:-3], refs[-3], refs[-2], refs[-1]
    size = blocks[0].shape[0]
    here = half_of(1 - far_ref[0], blocks[0].shape[1])
    copies = [pltpu.make_async_copy(block.at[:, here], give_ref.at[pl.ds(i * size, size), :], sems.at[i])
              for i, block in enumerate(blocks)]
    hidden = down_ref.shape[2]
    tile = down_ref.shape[1]
    step = pl.program_id(0)

    @pl.when(step == 0)
    def _():
        for copy in copies:
            copy.start()
        for e in range(local):
            here = combine_ref[:, e * cap_pad:e * cap_pad + cap]
            spread[:, e * hidden:(e + 1) * hidden] = dot(here, act_ref[e, :, :hidden]).astype(BF16)

    total = dot_nt(spread[:, :hidden], down_ref[0])
    for e in range(1, local):
        total = total + dot_nt(spread[:, e * hidden:(e + 1) * hidden], down_ref[e])
    store_parts(total.astype(BF16), pl.ds(pl.multiple_of(step * tile, tile), tile), outs)

    @pl.when(step == pl.num_programs(0) - 1)
    def _():
        for copy in copies:
            copy.wait()


def grad_kernel(cfg, far_ref, *refs):
    parts, local, cap, cap_pad, top = cfg
    blocks, refs = refs[:parts], refs[parts:]
    pick_ref, combine_ref, down_ref, pre_ref, info_ref, d_gate_ref, d_up_ref, tail_ref, keep_ref, give_ref = refs[:10]
    held, rows_ref, tails, sems = refs[10:]
    expert = pl.program_id(0)
    hidden = down_ref.shape[2]

    @pl.when(expert == 0)
    def _():
        load_blocks(blocks, held, sems)
        tails[...] = jnp.zeros(tails.shape, BF16)
        for start, stop in tiles(held.shape[1]):
            rows_ref[:, start:stop] = dot(pick_ref[...], held[:, start:stop]).astype(BF16)
        width = held.shape[1]
        keep_ref[...] = held[:, half_of(far_ref[0], width)]
        give_ref[...] = held[give_ref.shape[0]:, half_of(1 - far_ref[0], width)]

    info = info_ref[0]
    lane = iota(info.shape, 1)
    share = info[:, top:top + 1]
    gate_pre, up_pre = pre_ref[0, :, :hidden], pre_ref[0, :, hidden:]
    sig = jax.nn.sigmoid(gate_pre)
    silu = gate_pre * sig
    d_raw = dot(rows_ref[pl.ds(pl.multiple_of(expert * cap, 16), cap), :], down_ref[0])
    share_grad = jnp.sum(silu * up_pre * d_raw, axis=1, keepdims=True)
    d_active = share * d_raw
    d_gate_ref[0] = (d_active * up_pre * sig * (1.0 + gate_pre * (1.0 - sig))).astype(BF16)
    d_up_ref[0] = (d_active * silu).astype(BF16)
    placed = jnp.where((lane < top) & (info > 0.0), share_grad, 0.0)
    high = placed.astype(BF16)
    rest = placed - high.astype(F32)
    middle = rest.astype(BF16)
    low = (rest - middle.astype(F32)).astype(BF16)
    tail = high.astype(F32) + pltpu.roll(middle.astype(F32), top, 1) + pltpu.roll(low.astype(F32), 2 * top, 1)
    tails[pl.ds(pl.multiple_of(expert * cap_pad, cap_pad), cap), :] = tail.astype(BF16)

    @pl.when(expert == local - 1)
    def _():
        tail_ref[...] = dot(combine_ref[...], tails[...]).astype(BF16)


def input_kernel(cfg, d_gate_ref, d_up_ref, combine_ref, tail_ref, gate_ref, up_ref, *refs):
    local, cap, cap_pad = cfg
    outs, rows = refs[:-1], refs[-1]
    tile, hidden = gate_ref.shape[1:]
    step = pl.program_id(0)

    @pl.when(step == 0)
    def _():
        rows[...] = jnp.zeros(rows.shape, BF16)
        width = outs[0].shape[1] - LANES
        store_parts(tail_ref[...], slice(width, width + LANES), outs)

    for e in range(local):
        part = dot_nt(d_gate_ref[e], gate_ref[e]) + dot_nt(d_up_ref[e], up_ref[e])
        rows[e * cap_pad:e * cap_pad + cap, :] = part.astype(BF16)
    total = dot(combine_ref[...], rows[...]).astype(BF16)
    store_parts(total, pl.ds(pl.multiple_of(step * tile, tile), tile), outs)


def store_halves(part, near_ref, both, keep_ref, give_ref):
    both[...] = part.astype(BF16)
    size = keep_ref.shape[1]
    keep_ref[0] = both[pl.ds(pl.multiple_of(near_ref[0] * size, 16), size), :]
    give_ref[0] = both[pl.ds(pl.multiple_of((1 - near_ref[0]) * size, 16), size), :]


def down_kernel(cap, near_ref, pick_ref, *refs):
    x_refs, c_refs, (act_ref, act_far_ref, rows_ref, keep_ref, give_ref, c_rows, acts, both) = refs[:3], refs[3:6], refs[6:]
    hidden = acts.shape[1]
    line = x_refs[1].shape[0]
    acts[:cap, :] = act_ref[0, :, :hidden]
    acts[cap:, :] = act_far_ref[0, :, :hidden]
    pair = act_far_ref[0, :, hidden:].astype(F32)
    token = pair[:, 0:1] * 128.0 + pair[:, 1:2]
    pick = pick_ref[...]
    pick_far = jnp.where(token == iota(pick.shape, 1).astype(F32), 1.0, 0.0).astype(BF16)
    for (own, far, far_pair), rows in ((x_refs, rows_ref.at[0]), (c_refs, c_rows)):
        rows[:cap, :] = dot(pick, own[...]).astype(BF16)
        rows[cap:, :] = (dot(pick_far[:, :line], far[...]) + dot(pick_far[:, line:], far_pair[...])).astype(BF16)
    store_halves(dot_tn(c_rows[...], acts[...]), near_ref, both, keep_ref, give_ref)


def partial_kernel(cap, near_ref, rows_ref, own_ref, far_ref, keep_ref, give_ref, grads, both):
    grads[:cap, :] = own_ref[0]
    grads[cap:, :] = far_ref[0]
    store_halves(dot_tn(rows_ref[0], grads[...]), near_ref, both, keep_ref, give_ref)


def cut_kernel(half, plan, word_ref, *refs):
    count = 1 + max(i for i, _, _, _ in plan)
    blocks, outs, sems = refs[:count], refs[count:-1], refs[-1]
    copies = []
    for i, flip, out, row in plan:
        which = 1 - word_ref[0] if flip else word_ref[0]
        here = pl.ds(pl.multiple_of(which * half, LANES), half)
        there = outs[out].at[pl.ds(row, blocks[i].shape[0]), :]
        copies.append(pltpu.make_async_copy(blocks[i].at[:, here], there, sems.at[len(copies)]))
    for copy in copies:
        copy.start()
    for copy in copies:
        copy.wait()


def swap(value, bit, count):
    return lax.ppermute(value, "dp", [(i, i ^ bit) for i in range(count)])


def pair_swap(value, count):
    return lax.ppermute(value, "expert", [(i, i ^ 1) for i in range(count)])


def level_shift(value, hops, count):
    return lax.ppermute(value, "expert", [(i, (i + 2 * hops) % count) for i in range(count)])


def fence(*values):
    leaves, tree = jax.tree.flatten(values)
    return jax.tree.unflatten(tree, lax.optimization_barrier(tuple(leaves)))


def split3(value):
    high = lax.reduce_precision(value, 8, 7)
    rest = value - high
    middle = lax.reduce_precision(rest, 8, 7)
    return [high.astype(BF16), middle.astype(BF16), (rest - middle).astype(BF16)]


def shards(tokens, routes, probs, cotangent, w_gate, w_up, w_down):
    tok_rows, top = routes.shape
    local, width, hidden = w_gate.shape
    n_exp = lax.axis_size("expert")
    n_dp = lax.axis_size("dp")
    experts = local * n_exp
    cap = 5 * tok_rows * top // (4 * experts) * n_exp
    cap_pad = round_up(cap, LANES)
    total = n_exp * tok_rows
    levels = n_exp // 2
    line = levels * tok_rows
    wide = width + LANES
    tile = min(width, 512)
    columns = width // n_dp
    half = width // 2
    far_bit = n_dp // 2
    my_dp = lax.axis_index("dp")
    far = jnp.where((my_dp & far_bit) > 0, 1, 0)
    near = jnp.where((my_dp & 1) > 0, 1, 0)
    near_word = near.astype(jnp.int32).reshape(1)
    far_word = far.astype(jnp.int32).reshape(1)
    first = (lax.axis_index("expert") * local).astype(jnp.int32).reshape(1)
    hops = sorted(range(1, levels), key=lambda k: abs(2 * k - levels))
    mid, rest = hops[0], hops[1:]

    def pair(value):
        return pair_swap(value, n_exp)

    def shift(value, count):
        return level_shift(value, count, n_exp)

    any_space = pl.BlockSpec(memory_space=pl.ANY)
    smem = pl.BlockSpec(memory_space=pltpu.SMEM)
    params = pltpu.CompilerParams(dimension_semantics=("arbitrary",), vmem_limit_bytes=VMEM_LIMIT)

    def by_expert(*shape):
        return pl.BlockSpec((1,) + shape, lambda e: (e,) + (0,) * len(shape))

    def whole(*shape):
        return pl.BlockSpec(shape, lambda e: (0,) * len(shape))

    def sds(shape, dtype):
        return jax.ShapeDtypeStruct(shape, dtype)

    def cost(gflop, mbyte):
        return pl.CostEstimate(flops=gflop * 10**6, bytes_accessed=mbyte * 10**3, transcendentals=0)

    def cut_blocks(word, blocks, size, wanted, name):
        plan, rows = [], []
        for out, items in enumerate(wanted):
            rows.append(0)
            for i, flip in items:
                plan.append((i, flip, out, rows[out]))
                rows[out] += blocks[i].shape[0]
        return pl.pallas_call(
            functools.partial(cut_kernel, size, plan),
            in_specs=[smem] + [any_space] * len(blocks),
            out_specs=[pl.BlockSpec(memory_space=pltpu.VMEM)] * len(wanted),
            out_shape=[sds((n, size), BF16) for n in rows],
            scratch_shapes=[pltpu.SemaphoreType.DMA((len(plan),))],
            compiler_params=pltpu.CompilerParams(vmem_limit_bytes=VMEM_LIMIT),
            cost_estimate=cost(0, 2),
            name=name,
        )(word, *blocks)

    def cut_far(blocks, name):
        return cut_blocks(far_word, blocks, width // 2, [[(i, 1) for i in range(len(blocks))]], name)[0]

    by_columns = pl.BlockSpec((local, tile, hidden), lambda j: (0, j, 0))
    weight_spec = by_expert(width, hidden)
    parts = n_exp
    cfg = (parts, local, cap, cap_pad, top)

    totals = jnp.sum(probs, axis=1, keepdims=True)
    share = probs / totals
    meta = jnp.concatenate([routes.astype(BF16)] + split3(share), axis=1)
    meta = jnp.pad(meta, ((0, 0), (0, LANES - 4 * top)))

    x_own = jnp.concatenate([tokens, meta], axis=1)
    x_mid = shift(x_own, mid)
    x_own_pair = pair(x_own)
    c_own_pair = pair(cotangent)
    x_mid, x_own, cot, x_own_pair, c_own_pair = fence(x_mid, x_own, cotangent, x_own_pair, c_own_pair)
    x_rest = [shift(x_own, k) for k in rest]
    x_mid_pair = pair(x_mid)
    x_rest_pair = [pair(block) for block in x_rest]
    x_landed, cot, x_mid_pair = fence(x_rest, cot, x_mid_pair)

    c_mid = shift(cot, mid)
    x_far = swap(cut_far([x_own, x_mid] + x_landed, "cut_x"), far_bit, n_dp)
    x_rest_pair, c_mid, cot = fence(x_rest_pair, c_mid, cot)
    c_rest = [shift(cot, k) for k in rest]
    c_mid_pair = pair(c_mid)
    pre, act, info, pick, combine, x_keep, x_give = pl.pallas_call(
        functools.partial(hidden_kernel, cfg),
        grid=(local,),
        in_specs=[smem] * 2 + [any_space] * parts + [weight_spec] * 2,
        out_specs=[by_expert(cap, 2 * hidden), by_expert(cap, hidden + LANES), by_expert(cap, LANES),
                   whole(local * cap, total), whole(total, local * cap_pad), whole(total, half), whole(line, half)],
        out_shape=[sds((local, cap, 2 * hidden), F32), sds((local, cap, hidden + LANES), BF16),
                   sds((local, cap, LANES), F32), sds((local * cap, total), BF16), sds((total, local * cap_pad), BF16),
                   sds((total, half), BF16), sds((line, half), BF16)],
        scratch_shapes=[
            pltpu.VMEM((total, wide), BF16),
            pltpu.VMEM((local * cap, wide), BF16),
            pltpu.SemaphoreType.DMA((parts,)),
        ],
        compiler_params=params,
        cost_estimate=cost(6, 20),
        name="hidden",
    )(first, far_word, x_own, x_mid, *x_rest, x_own_pair, x_mid_pair, *x_rest_pair, w_gate, w_up)
    act, c_rest, c_mid_pair, x_far = fence(act, c_rest, c_mid_pair, x_far)

    c_rest_pair = [pair(block) for block in c_rest]
    act_far = swap(act, far_bit, n_dp)
    x_far_pair = swap(x_give, far_bit, n_dp)
    level_rows = [line, tok_rows, line - tok_rows]
    level_specs = [whole(rows, width) for rows in level_rows]
    mixed_keep, mixed_mid, mixed_rest, c_give = pl.pallas_call(
        functools.partial(mixed_kernel, (levels, local, cap, cap_pad)),
        grid=(width // tile,),
        in_specs=[smem, whole(local, cap, hidden + LANES), whole(total, local * cap_pad), by_columns] + [any_space] * levels,
        out_specs=level_specs + [whole(line, half)],
        out_shape=[sds((rows, width), BF16) for rows in level_rows] + [sds((line, half), BF16)],
        scratch_shapes=[pltpu.VMEM((total, local * hidden), BF16), pltpu.SemaphoreType.DMA((levels,))],
        compiler_params=params,
        cost_estimate=cost(6, 10),
        name="mixed",
    )(far_word, act, combine, w_down, cot, c_mid, *c_rest)
    c_rest_pair, mixed_keep, mixed_mid, mixed_rest, c_give, x_far_pair = fence(
        c_rest_pair, mixed_keep, mixed_mid, mixed_rest, c_give, x_far_pair)

    def back_rows(keep, got):
        return keep.astype(F32) + got.astype(F32)

    def sum_mid(keep, got):
        return back_rows(keep[tok_rows:2 * tok_rows], got).astype(BF16)

    def sum_rest(keep, got):
        return back_rows(keep[2 * tok_rows:], got[:line - 2 * tok_rows]).astype(BF16)

    def send_rest(sums):
        return [shift(sums[i * tok_rows:(i + 1) * tok_rows], -k) for i, k in enumerate(rest)]

    def finish(keep, got, landed):
        return sum([part.astype(F32) for part in landed], back_rows(keep[:tok_rows], got[line - 2 * tok_rows:]))

    mixed_mid, mixed_rest = pair(mixed_mid), pair(mixed_rest)
    c_far = swap(c_give, far_bit, n_dp)
    d_gate, d_up, tail, c_keep, c_give = pl.pallas_call(
        functools.partial(grad_kernel, cfg),
        grid=(local,),
        in_specs=[smem] + [any_space] * parts + [whole(local * cap, total), whole(total, local * cap_pad), weight_spec,
                                                 by_expert(cap, 2 * hidden), by_expert(cap, LANES)],
        out_specs=[by_expert(cap, hidden)] * 2 + [whole(total, LANES), whole(total, half), whole(line, half)],
        out_shape=[sds((local, cap, hidden), BF16)] * 2 + [sds((total, LANES), BF16),
                   sds((total, half), BF16), sds((line, half), BF16)],
        scratch_shapes=[
            pltpu.VMEM((total, width), BF16),
            pltpu.VMEM((local * cap, width), BF16),
            pltpu.VMEM((local * cap_pad, LANES), BF16),
            pltpu.SemaphoreType.DMA((parts,)),
        ],
        compiler_params=params,
        cost_estimate=cost(6, 12),
        name="hidden_grads",
    )(far_word, cot, c_mid, *c_rest, c_own_pair, c_mid_pair, *c_rest_pair, pick, combine, w_down, pre, info)
    mixed_mid, d_gate, d_up, tail, c_give, act_far = fence(
        sum_mid(mixed_keep, mixed_mid), d_gate, d_up, tail, c_give, act_far)

    mixed_back = [shift(mixed_mid, -mid)]
    c_far_pair = swap(c_give, far_bit, n_dp)
    gate_far = swap(d_gate, far_bit, n_dp)
    wide_specs = [whole(rows, wide) for rows in level_rows]
    input_keep, input_mid, input_rest = pl.pallas_call(
        functools.partial(input_kernel, (local, cap, cap_pad)),
        grid=(width // tile,),
        in_specs=[whole(local, cap, hidden)] * 2 + [whole(total, local * cap_pad), whole(total, LANES),
                                                    by_columns, by_columns],
        out_specs=wide_specs,
        out_shape=[sds((rows, wide), BF16) for rows in level_rows],
        scratch_shapes=[pltpu.VMEM((local * cap_pad, tile), BF16)],
        compiler_params=params,
        cost_estimate=cost(6, 16),
        name="input_grads",
    )(d_gate, d_up, combine, tail, w_gate, w_up)
    mixed_sums, input_keep, input_mid, input_rest, mixed_back, c_far, d_up = fence(
        sum_rest(mixed_keep, mixed_rest), input_keep, input_mid, input_rest, mixed_back, c_far, d_up)

    mixed_back += send_rest(mixed_sums)
    input_mid, input_rest = pair(input_mid), pair(input_rest)
    up_far = swap(d_up, far_bit, n_dp)
    input_mid, mixed_back, c_far_pair, x_keep = fence(sum_mid(input_keep, input_mid), mixed_back, c_far_pair, x_keep)

    input_back = [shift(input_mid, -mid)]
    partial_specs = [by_expert(columns, hidden)] * 2
    partial_shapes = [sds((local, columns, hidden), BF16)] * 2
    x_rows, down_keep, down_give = pl.pallas_call(
        functools.partial(down_kernel, cap),
        grid=(local,),
        in_specs=[smem, pl.BlockSpec((cap, total), lambda e: (e, 0))] + [whole(total, half), whole(line, half), whole(line, half)] * 2
        + [by_expert(cap, hidden + LANES)] * 2,
        out_specs=[by_expert(2 * cap, half)] + partial_specs,
        out_shape=[sds((local, 2 * cap, half), BF16)] + partial_shapes,
        scratch_shapes=[pltpu.VMEM((2 * cap, half), BF16), pltpu.VMEM((2 * cap, hidden), BF16), pltpu.VMEM((half, hidden), BF16)],
        compiler_params=params,
        cost_estimate=cost(6, 12),
        name="down_grads",
    )(near_word, pick, x_keep, x_far, x_far_pair, c_keep, c_far, c_far_pair, act, act_far)
    input_sums, input_back, x_rows, down_keep, down_give, gate_far = fence(
        sum_rest(input_keep, input_rest), input_back, x_rows, down_keep, down_give, gate_far)

    input_back += send_rest(input_sums)
    down_got = swap(down_give, 1, n_dp)

    def partial_grads(grads, grads_far, name):
        return pl.pallas_call(
            functools.partial(partial_kernel, cap),
            grid=(local,),
            in_specs=[smem, by_expert(2 * cap, half)] + [by_expert(cap, hidden)] * 2,
            out_specs=partial_specs,
            out_shape=partial_shapes,
            scratch_shapes=[pltpu.VMEM((2 * cap, hidden), BF16), pltpu.VMEM((half, hidden), BF16)],
            compiler_params=params,
            cost_estimate=cost(3, 10),
            name=name,
        )(near_word, x_rows, grads, grads_far)

    gate_keep, gate_give = partial_grads(d_gate, gate_far, "gate_grads")
    gate_got = swap(gate_give, 1, n_dp)
    up_keep, up_give = partial_grads(d_up, up_far, "up_grads")
    up_got = swap(up_give, 1, n_dp)
    down_grad = back_rows(down_keep, down_got).astype(BF16)
    gate_grad = back_rows(gate_keep, gate_got).astype(BF16)
    up_grad = back_rows(up_keep, up_got).astype(BF16)

    mixed = finish(mixed_keep, mixed_rest, mixed_back).astype(BF16)
    back = finish(input_keep, input_rest, input_back)
    token_grad = back[:, :width].astype(BF16)
    tail = back[:, width:]
    slot_sg = tail[:, :top] + tail[:, top:2 * top] + tail[:, 2 * top:3 * top]
    prob_grad = (slot_sg - jnp.sum(share * slot_sg, axis=1, keepdims=True)) / totals
    return mixed, token_grad, prob_grad, gate_grad, up_grad, down_grad


def solution(mesh):
    rows = P(("expert", "dp"), None)
    weight = P("expert", None, None)
    grad = P("expert", "dp", None)
    return jax.shard_map(
        shards,
        mesh=mesh,
        in_specs=(rows, rows, rows, rows, weight, weight, weight),
        out_specs=(rows, rows, rows, grad, grad, grad),
        check_vma=False,
    )
```

```python
import functools

import jax
import jax.numpy as jnp
from jax import lax
from jax.experimental import pallas as pl
from jax.experimental.pallas import tpu as pltpu
from jax.sharding import PartitionSpec as P


F32 = jnp.float32
BF16 = jnp.bfloat16
LANES = 128
VMEM_LIMIT = 60 * 1024 * 1024


def round_up(value, unit):
    return -(-value // unit) * unit


def dot(a, b):
    return jnp.dot(a, b, preferred_element_type=F32)


def dot_nt(a, b):
    return lax.dot_general(a, b, (((1,), (1,)), ((), ())), preferred_element_type=F32)


def dot_tn(a, b):
    return lax.dot_general(a, b, (((0,), (0,)), ((), ())), preferred_element_type=F32)


def iota(shape, dim):
    return lax.broadcasted_iota(jnp.int32, shape, dim)


def load_blocks(blocks, held, sems):
    copies, start = [], 0
    for i, block in enumerate(blocks):
        size = block.shape[0]
        copies.append(pltpu.make_async_copy(block, held.at[pl.ds(start, size), :], sems.at[i]))
        start += size
    for copy in copies:
        copy.start()
    for copy in copies:
        copy.wait()


def tiles(width, tile=512):
    return [(start, min(start + tile, width)) for start in range(0, width, tile)]


def half_of(which, width):
    return pl.ds(pl.multiple_of(which * (width // 2), LANES), width // 2)


def hidden_kernel(cfg, first_ref, far_ref, *refs):
    parts, local, cap, cap_pad, top = cfg
    blocks, refs = refs[:parts], refs[parts:]
    gate_ref, up_ref, pre_ref, act_ref, info_ref, pick_ref, combine_ref, keep_ref, give_ref = refs[:9]
    held, rows_ref, sems = refs[9:]
    expert = pl.program_id(0)
    tokens = held.shape[0]
    width, hidden = gate_ref.shape[1:]

    @pl.when(expert == 0)
    def _():
        load_blocks(blocks, held, sems)
        meta = held[:, width:].astype(F32).astype(jnp.int32)
        lane = iota(meta.shape, 1)
        hits = jnp.zeros(meta.shape, F32)
        for i in range(local):
            named = (meta == first_ref[0] + i) & (lane < top)
            hit = jnp.sum(jnp.where(named, 1.0, 0.0), axis=1, keepdims=True)
            hits = hits + jnp.where(lane == i, hit, 0.0)
        step = min(tokens, 256)
        below = (iota((step, step), 0) >= iota((step, step), 1)).astype(F32).astype(BF16)
        carry = jnp.zeros((1, LANES), F32)
        slots = []
        for start in range(0, tokens, step):
            part = hits[start:start + step]
            rank = dot(below, part.astype(BF16)) + carry
            carry = rank[step - 1:step]
            slots.append(jnp.where(part > 0.0, rank - 1.0, -1.0))
        slots = jnp.concatenate(slots, axis=0)
        slots_t = jnp.transpose(slots)
        places = iota((tokens, cap_pad), 1).astype(F32)
        places_t = iota((cap, tokens), 0).astype(F32)
        for i in range(local):
            hit = slots[:, i:i + 1] == places
            combine_ref[:, i * cap_pad:(i + 1) * cap_pad] = jnp.where(hit, 1.0, 0.0).astype(BF16)
            hit = slots_t[i:i + 1, :] == places_t
            pick_ref[i * cap:(i + 1) * cap, :] = jnp.where(hit, 1.0, 0.0).astype(BF16)
        for start, stop in tiles(held.shape[1]):
            rows_ref[:, start:stop] = dot(pick_ref[...], held[:, start:stop]).astype(BF16)
        keep_ref[...] = held[:, half_of(far_ref[0], width)]
        give_ref[...] = held[give_ref.shape[0]:, half_of(1 - far_ref[0], width)]

    here = pl.ds(pl.multiple_of(expert * cap, 16), cap)
    pick = pick_ref[here, :].astype(F32)
    token = jnp.sum(pick * iota(pick.shape, 1).astype(F32), axis=1, keepdims=True)
    token = jnp.where(jnp.sum(pick, axis=1, keepdims=True) > 0.0, token, -128.0).astype(jnp.int32)
    meta = rows_ref[here, width:].astype(F32)
    lane = iota(meta.shape, 1)
    named = (meta.astype(jnp.int32) == first_ref[0] + expert) & (lane < top)
    shares = sum(pltpu.roll(meta, LANES - top * (i + 1), 1) for i in range(3))
    share = jnp.sum(jnp.where(named, shares, 0.0), axis=1, keepdims=True)
    info_ref[0] = jnp.where(lane < top, jnp.where(named, 1.0, 0.0), share)

    rows = rows_ref[here, :width]
    gate_pre = dot(rows, gate_ref[0])
    up_pre = dot(rows, up_ref[0])
    pre_ref[0, :, :hidden] = gate_pre
    pre_ref[0, :, hidden:] = up_pre
    active = gate_pre * jax.nn.sigmoid(gate_pre) * up_pre
    act_ref[0, :, :hidden] = (share * active).astype(BF16)
    token_pair = jnp.where(lane == 0, token >> 7, jnp.where(lane == 1, token & 127, 0))
    act_ref[0, :, hidden:] = token_pair.astype(F32).astype(BF16)


def store_parts(value, here, refs):
    keep_ref, mid_ref, rest_ref = refs
    line, size = keep_ref.shape[0], mid_ref.shape[0]
    keep_ref[:, here] = value[:line]
    mid_ref[:, here] = value[line + size:line + 2 * size]
    rest_ref[:line - 2 * size, here] = value[line + 2 * size:]
    rest_ref[line - 2 * size:, here] = value[line:line + size]


def mixed_kernel(cfg, far_ref, act_ref, combine_ref, down_ref, *refs):
    levels, local, cap, cap_pad = cfg
    blocks, refs = refs[:levels], refs[levels:]
    outs, give_ref, spread, sems = refs[:-3], refs[-3], refs[-2], refs[-1]
    size = blocks[0].shape[0]
    here = half_of(1 - far_ref[0], blocks[0].shape[1])
    copies = [pltpu.make_async_copy(block.at[:, here], give_ref.at[pl.ds(i * size, size), :], sems.at[i])
              for i, block in enumerate(blocks)]
    hidden = down_ref.shape[2]
    tile = down_ref.shape[1]
    step = pl.program_id(0)

    @pl.when(step == 0)
    def _():
        for copy in copies:
            copy.start()
        for e in range(local):
            here = combine_ref[:, e * cap_pad:e * cap_pad + cap]
            spread[:, e * hidden:(e + 1) * hidden] = dot(here, act_ref[e, :, :hidden]).astype(BF16)

    total = dot_nt(spread[:, :hidden], down_ref[0])
    for e in range(1, local):
        total = total + dot_nt(spread[:, e * hidden:(e + 1) * hidden], down_ref[e])
    store_parts(total.astype(BF16), pl.ds(pl.multiple_of(step * tile, tile), tile), outs)

    @pl.when(step == pl.num_programs(0) - 1)
    def _():
        for copy in copies:
            copy.wait()


def grad_kernel(cfg, far_ref, *refs):
    parts, local, cap, cap_pad, top = cfg
    blocks, refs = refs[:parts], refs[parts:]
    pick_ref, combine_ref, down_ref, pre_ref, info_ref, d_gate_ref, d_up_ref, tail_ref, keep_ref, give_ref = refs[:10]
    held, rows_ref, tails, sems = refs[10:]
    expert = pl.program_id(0)
    hidden = down_ref.shape[2]

    @pl.when(expert == 0)
    def _():
        load_blocks(blocks, held, sems)
        tails[...] = jnp.zeros(tails.shape, BF16)
        for start, stop in tiles(held.shape[1]):
            rows_ref[:, start:stop] = dot(pick_ref[...], held[:, start:stop]).astype(BF16)
        width = held.shape[1]
        keep_ref[...] = held[:, half_of(far_ref[0], width)]
        give_ref[...] = held[give_ref.shape[0]:, half_of(1 - far_ref[0], width)]

    info = info_ref[0]
    lane = iota(info.shape, 1)
    share = info[:, top:top + 1]
    gate_pre, up_pre = pre_ref[0, :, :hidden], pre_ref[0, :, hidden:]
    sig = jax.nn.sigmoid(gate_pre)
    silu = gate_pre * sig
    d_raw = dot(rows_ref[pl.ds(pl.multiple_of(expert * cap, 16), cap), :], down_ref[0])
    share_grad = jnp.sum(silu * up_pre * d_raw, axis=1, keepdims=True)
    d_active = share * d_raw
    d_gate_ref[0] = (d_active * up_pre * sig * (1.0 + gate_pre * (1.0 - sig))).astype(BF16)
    d_up_ref[0] = (d_active * silu).astype(BF16)
    placed = jnp.where((lane < top) & (info > 0.0), share_grad, 0.0)
    high = placed.astype(BF16)
    rest = placed - high.astype(F32)
    middle = rest.astype(BF16)
    low = (rest - middle.astype(F32)).astype(BF16)
    tail = high.astype(F32) + pltpu.roll(middle.astype(F32), top, 1) + pltpu.roll(low.astype(F32), 2 * top, 1)
    tails[pl.ds(pl.multiple_of(expert * cap_pad, cap_pad), cap), :] = tail.astype(BF16)

    @pl.when(expert == local - 1)
    def _():
        tail_ref[...] = dot(combine_ref[...], tails[...]).astype(BF16)


def input_kernel(cfg, d_gate_ref, d_up_ref, combine_ref, tail_ref, gate_ref, up_ref, *refs):
    local, cap, cap_pad = cfg
    outs, rows = refs[:-1], refs[-1]
    tile, hidden = gate_ref.shape[1:]
    step = pl.program_id(0)

    @pl.when(step == 0)
    def _():
        rows[...] = jnp.zeros(rows.shape, BF16)
        width = outs[0].shape[1] - LANES
        store_parts(tail_ref[...], slice(width, width + LANES), outs)

    for e in range(local):
        part = dot_nt(d_gate_ref[e], gate_ref[e]) + dot_nt(d_up_ref[e], up_ref[e])
        rows[e * cap_pad:e * cap_pad + cap, :] = part.astype(BF16)
    total = dot(combine_ref[...], rows[...]).astype(BF16)
    store_parts(total, pl.ds(pl.multiple_of(step * tile, tile), tile), outs)


def store_halves(part, near_ref, both, keep_ref, give_ref):
    both[...] = part.astype(BF16)
    size = keep_ref.shape[1]
    keep_ref[0] = both[pl.ds(pl.multiple_of(near_ref[0] * size, 16), size), :]
    give_ref[0] = both[pl.ds(pl.multiple_of((1 - near_ref[0]) * size, 16), size), :]


def down_kernel(cap, near_ref, pick_ref, *refs):
    x_refs, c_refs, (act_ref, act_far_ref, rows_ref, keep_ref, give_ref, c_rows, acts, both) = refs[:3], refs[3:6], refs[6:]
    hidden = acts.shape[1]
    line = x_refs[1].shape[0]
    acts[:cap, :] = act_ref[0, :, :hidden]
    acts[cap:, :] = act_far_ref[0, :, :hidden]
    pair = act_far_ref[0, :, hidden:].astype(F32)
    token = pair[:, 0:1] * 128.0 + pair[:, 1:2]
    pick = pick_ref[...]
    pick_far = jnp.where(token == iota(pick.shape, 1).astype(F32), 1.0, 0.0).astype(BF16)
    for (own, far, far_pair), rows in ((x_refs, rows_ref.at[0]), (c_refs, c_rows)):
        rows[:cap, :] = dot(pick, own[...]).astype(BF16)
        rows[cap:, :] = (dot(pick_far[:, :line], far[...]) + dot(pick_far[:, line:], far_pair[...])).astype(BF16)
    store_halves(dot_tn(c_rows[...], acts[...]), near_ref, both, keep_ref, give_ref)


def partial_kernel(cap, near_ref, rows_ref, own_ref, far_ref, keep_ref, give_ref, grads, both):
    grads[:cap, :] = own_ref[0]
    grads[cap:, :] = far_ref[0]
    store_halves(dot_tn(rows_ref[0], grads[...]), near_ref, both, keep_ref, give_ref)


def cut_kernel(half, plan, word_ref, *refs):
    count = 1 + max(i for i, _, _, _ in plan)
    blocks, outs, sems = refs[:count], refs[count:-1], refs[-1]
    copies = []
    for i, flip, out, row in plan:
        which = 1 - word_ref[0] if flip else word_ref[0]
        here = pl.ds(pl.multiple_of(which * half, LANES), half)
        there = outs[out].at[pl.ds(row, blocks[i].shape[0]), :]
        copies.append(pltpu.make_async_copy(blocks[i].at[:, here], there, sems.at[len(copies)]))
    for copy in copies:
        copy.start()
    for copy in copies:
        copy.wait()


def swap(value, bit, count):
    return lax.ppermute(value, "dp", [(i, i ^ bit) for i in range(count)])


def pair_swap(value, count):
    return lax.ppermute(value, "expert", [(i, i ^ 1) for i in range(count)])


def level_shift(value, hops, count):
    return lax.ppermute(value, "expert", [(i, (i + 2 * hops) % count) for i in range(count)])


def fence(*values):
    leaves, tree = jax.tree.flatten(values)
    return jax.tree.unflatten(tree, lax.optimization_barrier(tuple(leaves)))


def split3(value):
    high = lax.reduce_precision(value, 8, 7)
    rest = value - high
    middle = lax.reduce_precision(rest, 8, 7)
    return [high.astype(BF16), middle.astype(BF16), (rest - middle).astype(BF16)]


def shards(tokens, routes, probs, cotangent, w_gate, w_up, w_down):
    tok_rows, top = routes.shape
    local, width, hidden = w_gate.shape
    n_exp = lax.axis_size("expert")
    n_dp = lax.axis_size("dp")
    experts = local * n_exp
    cap = 5 * tok_rows * top // (4 * experts) * n_exp
    cap_pad = round_up(cap, LANES)
    total = n_exp * tok_rows
    levels = n_exp // 2
    line = levels * tok_rows
    wide = width + LANES
    tile = min(width, 512)
    columns = width // n_dp
    half = width // 2
    far_bit = n_dp // 2
    my_dp = lax.axis_index("dp")
    far = jnp.where((my_dp & far_bit) > 0, 1, 0)
    near = jnp.where((my_dp & 1) > 0, 1, 0)
    near_word = near.astype(jnp.int32).reshape(1)
    far_word = far.astype(jnp.int32).reshape(1)
    first = (lax.axis_index("expert") * local).astype(jnp.int32).reshape(1)
    hops = sorted(range(1, levels), key=lambda k: abs(2 * k - levels))
    mid, rest = hops[0], hops[1:]

    def pair(value):
        return pair_swap(value, n_exp)

    def shift(value, count):
        return level_shift(value, count, n_exp)

    any_space = pl.BlockSpec(memory_space=pl.ANY)
    smem = pl.BlockSpec(memory_space=pltpu.SMEM)
    params = pltpu.CompilerParams(dimension_semantics=("arbitrary",), vmem_limit_bytes=VMEM_LIMIT)

    def by_expert(*shape):
        return pl.BlockSpec((1,) + shape, lambda e: (e,) + (0,) * len(shape))

    def whole(*shape):
        return pl.BlockSpec(shape, lambda e: (0,) * len(shape))

    def sds(shape, dtype):
        return jax.ShapeDtypeStruct(shape, dtype)

    def cost(gflop, mbyte):
        return pl.CostEstimate(flops=gflop * 10**6, bytes_accessed=mbyte * 10**3, transcendentals=0)

    def cut_blocks(word, blocks, size, wanted, name):
        plan, rows = [], []
        for out, items in enumerate(wanted):
            rows.append(0)
            for i, flip in items:
                plan.append((i, flip, out, rows[out]))
                rows[out] += blocks[i].shape[0]
        return pl.pallas_call(
            functools.partial(cut_kernel, size, plan),
            in_specs=[smem] + [any_space] * len(blocks),
            out_specs=[pl.BlockSpec(memory_space=pltpu.VMEM)] * len(wanted),
            out_shape=[sds((n, size), BF16) for n in rows],
            scratch_shapes=[pltpu.SemaphoreType.DMA((len(plan),))],
            compiler_params=pltpu.CompilerParams(vmem_limit_bytes=VMEM_LIMIT),
            cost_estimate=cost(0, 2),
            name=name,
        )(word, *blocks)

    def cut_far(blocks, name):
        return cut_blocks(far_word, blocks, width // 2, [[(i, 1) for i in range(len(blocks))]], name)[0]

    by_columns = pl.BlockSpec((local, tile, hidden), lambda j: (0, j, 0))
    weight_spec = by_expert(width, hidden)
    parts = n_exp
    cfg = (parts, local, cap, cap_pad, top)

    totals = jnp.sum(probs, axis=1, keepdims=True)
    share = probs / totals
    meta = jnp.concatenate([routes.astype(BF16)] + split3(share), axis=1)
    meta = jnp.pad(meta, ((0, 0), (0, LANES - 4 * top)))

    x_own = jnp.concatenate([tokens, meta], axis=1)
    x_mid = shift(x_own, mid)
    x_own_pair = pair(x_own)
    c_own_pair = pair(cotangent)
    x_mid, x_own, cot, x_own_pair, c_own_pair = fence(x_mid, x_own, cotangent, x_own_pair, c_own_pair)
    x_rest = [shift(x_own, k) for k in rest]
    x_mid_pair = pair(x_mid)
    x_rest_pair = [pair(block) for block in x_rest]
    x_landed, cot, x_mid_pair = fence(x_rest, cot, x_mid_pair)

    c_mid = shift(cot, mid)
    c_rest = [shift(cot, k) for k in rest]
    x_far = swap(cut_far([x_own, x_mid] + x_landed, "cut_x"), far_bit, n_dp)
    x_rest_pair, c_mid = fence(x_rest_pair, c_mid)
    c_mid_pair = pair(c_mid)
    pre, act, info, pick, combine, x_keep, x_give = pl.pallas_call(
        functools.partial(hidden_kernel, cfg),
        grid=(local,),
        in_specs=[smem] * 2 + [any_space] * parts + [weight_spec] * 2,
        out_specs=[by_expert(cap, 2 * hidden), by_expert(cap, hidden + LANES), by_expert(cap, LANES),
                   whole(local * cap, total), whole(total, local * cap_pad), whole(total, half), whole(line, half)],
        out_shape=[sds((local, cap, 2 * hidden), F32), sds((local, cap, hidden + LANES), BF16),
                   sds((local, cap, LANES), F32), sds((local * cap, total), BF16), sds((total, local * cap_pad), BF16),
                   sds((total, half), BF16), sds((line, half), BF16)],
        scratch_shapes=[
            pltpu.VMEM((total, wide), BF16),
            pltpu.VMEM((local * cap, wide), BF16),
            pltpu.SemaphoreType.DMA((parts,)),
        ],
        compiler_params=params,
        cost_estimate=cost(6, 20),
        name="hidden",
    )(first, far_word, x_own, x_mid, *x_rest, x_own_pair, x_mid_pair, *x_rest_pair, w_gate, w_up)
    act, c_rest, c_mid_pair, x_far = fence(act, c_rest, c_mid_pair, x_far)

    c_rest_pair = [pair(block) for block in c_rest]
    act_far = swap(act, far_bit, n_dp)
    x_far_pair = swap(x_give, far_bit, n_dp)
    level_rows = [line, tok_rows, line - tok_rows]
    level_specs = [whole(rows, width) for rows in level_rows]
    mixed_keep, mixed_mid, mixed_rest, c_give = pl.pallas_call(
        functools.partial(mixed_kernel, (levels, local, cap, cap_pad)),
        grid=(width // tile,),
        in_specs=[smem, whole(local, cap, hidden + LANES), whole(total, local * cap_pad), by_columns] + [any_space] * levels,
        out_specs=level_specs + [whole(line, half)],
        out_shape=[sds((rows, width), BF16) for rows in level_rows] + [sds((line, half), BF16)],
        scratch_shapes=[pltpu.VMEM((total, local * hidden), BF16), pltpu.SemaphoreType.DMA((levels,))],
        compiler_params=params,
        cost_estimate=cost(6, 10),
        name="mixed",
    )(far_word, act, combine, w_down, cot, c_mid, *c_rest)
    c_rest_pair, mixed_keep, mixed_mid, mixed_rest, c_give, x_far_pair = fence(
        c_rest_pair, mixed_keep, mixed_mid, mixed_rest, c_give, x_far_pair)

    def back_rows(keep, got):
        return keep.astype(F32) + got.astype(F32)

    def sum_mid(keep, got):
        return back_rows(keep[tok_rows:2 * tok_rows], got).astype(BF16)

    def sum_rest(keep, got):
        return back_rows(keep[2 * tok_rows:], got[:line - 2 * tok_rows]).astype(BF16)

    def send_rest(sums):
        return [shift(sums[i * tok_rows:(i + 1) * tok_rows], -k) for i, k in enumerate(rest)]

    def finish(keep, got, landed):
        return sum([part.astype(F32) for part in landed], back_rows(keep[:tok_rows], got[line - 2 * tok_rows:]))

    mixed_mid = pair(mixed_mid)
    c_far = swap(c_give, far_bit, n_dp)
    d_gate, d_up, tail, c_keep, c_give = pl.pallas_call(
        functools.partial(grad_kernel, cfg),
        grid=(local,),
        in_specs=[smem] + [any_space] * parts + [whole(local * cap, total), whole(total, local * cap_pad), weight_spec,
                                                 by_expert(cap, 2 * hidden), by_expert(cap, LANES)],
        out_specs=[by_expert(cap, hidden)] * 2 + [whole(total, LANES), whole(total, half), whole(line, half)],
        out_shape=[sds((local, cap, hidden), BF16)] * 2 + [sds((total, LANES), BF16),
                   sds((total, half), BF16), sds((line, half), BF16)],
        scratch_shapes=[
            pltpu.VMEM((total, width), BF16),
            pltpu.VMEM((local * cap, width), BF16),
            pltpu.VMEM((local * cap_pad, LANES), BF16),
            pltpu.SemaphoreType.DMA((parts,)),
        ],
        compiler_params=params,
        cost_estimate=cost(6, 12),
        name="hidden_grads",
    )(far_word, cot, c_mid, *c_rest, c_own_pair, c_mid_pair, *c_rest_pair, pick, combine, w_down, pre, info)
    mixed_mid, mixed_rest, d_gate, d_up, tail, c_give, act_far = fence(
        sum_mid(mixed_keep, mixed_mid), mixed_rest, d_gate, d_up, tail, c_give, act_far)
    mixed_rest = pair(mixed_rest)

    mixed_back = [shift(mixed_mid, -mid)]
    c_far_pair = swap(c_give, far_bit, n_dp)
    wide_specs = [whole(rows, wide) for rows in level_rows]
    input_keep, input_mid, input_rest = pl.pallas_call(
        functools.partial(input_kernel, (local, cap, cap_pad)),
        grid=(width // tile,),
        in_specs=[whole(local, cap, hidden)] * 2 + [whole(total, local * cap_pad), whole(total, LANES),
                                                    by_columns, by_columns],
        out_specs=wide_specs,
        out_shape=[sds((rows, wide), BF16) for rows in level_rows],
        scratch_shapes=[pltpu.VMEM((local * cap_pad, tile), BF16)],
        compiler_params=params,
        cost_estimate=cost(6, 16),
        name="input_grads",
    )(d_gate, d_up, combine, tail, w_gate, w_up)
    mixed_sums, input_keep, input_mid, input_rest, mixed_back, c_far, d_up = fence(
        sum_rest(mixed_keep, mixed_rest), input_keep, input_mid, input_rest, mixed_back, c_far, d_up)

    mixed_back += send_rest(mixed_sums)
    input_mid, input_rest = pair(input_mid), pair(input_rest)
    input_mid, mixed_back, c_far_pair, x_keep, d_gate = fence(
        sum_mid(input_keep, input_mid), mixed_back, c_far_pair, x_keep, d_gate)

    input_back = [shift(input_mid, -mid)]
    gate_far = swap(d_gate, far_bit, n_dp)
    up_far = swap(d_up, far_bit, n_dp)
    partial_specs = [by_expert(columns, hidden)] * 2
    partial_shapes = [sds((local, columns, hidden), BF16)] * 2
    x_rows, down_keep, down_give = pl.pallas_call(
        functools.partial(down_kernel, cap),
        grid=(local,),
        in_specs=[smem, pl.BlockSpec((cap, total), lambda e: (e, 0))] + [whole(total, half), whole(line, half), whole(line, half)] * 2
        + [by_expert(cap, hidden + LANES)] * 2,
        out_specs=[by_expert(2 * cap, half)] + partial_specs,
        out_shape=[sds((local, 2 * cap, half), BF16)] + partial_shapes,
        scratch_shapes=[pltpu.VMEM((2 * cap, half), BF16), pltpu.VMEM((2 * cap, hidden), BF16), pltpu.VMEM((half, hidden), BF16)],
        compiler_params=params,
        cost_estimate=cost(6, 12),
        name="down_grads",
    )(near_word, pick, x_keep, x_far, x_far_pair, c_keep, c_far, c_far_pair, act, act_far)
    input_sums, input_back, x_rows, down_keep, down_give, gate_far = fence(
        sum_rest(input_keep, input_rest), input_back, x_rows, down_keep, down_give, gate_far)

    input_back += send_rest(input_sums)
    down_got = swap(down_give, 1, n_dp)

    def partial_grads(grads, grads_far, name):
        return pl.pallas_call(
            functools.partial(partial_kernel, cap),
            grid=(local,),
            in_specs=[smem, by_expert(2 * cap, half)] + [by_expert(cap, hidden)] * 2,
            out_specs=partial_specs,
            out_shape=partial_shapes,
            scratch_shapes=[pltpu.VMEM((2 * cap, hidden), BF16), pltpu.VMEM((half, hidden), BF16)],
            compiler_params=params,
            cost_estimate=cost(3, 10),
            name=name,
        )(near_word, x_rows, grads, grads_far)

    gate_keep, gate_give = partial_grads(d_gate, gate_far, "gate_grads")
    gate_got = swap(gate_give, 1, n_dp)
    up_far, input_back, gate_keep, down_got = fence(up_far, input_back, gate_keep, down_got)
    up_keep, up_give = partial_grads(d_up, up_far, "up_grads")
    up_got = swap(up_give, 1, n_dp)
    down_grad = back_rows(down_keep, down_got).astype(BF16)
    gate_grad = back_rows(gate_keep, gate_got).astype(BF16)
    up_grad = back_rows(up_keep, up_got).astype(BF16)

    mixed = finish(mixed_keep, mixed_rest, mixed_back).astype(BF16)
    back = finish(input_keep, input_rest, input_back)
    token_grad = back[:, :width].astype(BF16)
    tail = back[:, width:]
    slot_sg = tail[:, :top] + tail[:, top:2 * top] + tail[:, 2 * top:3 * top]
    prob_grad = (slot_sg - jnp.sum(share * slot_sg, axis=1, keepdims=True)) / totals
    return mixed, token_grad, prob_grad, gate_grad, up_grad, down_grad


def solution(mesh):
    rows = P(("expert", "dp"), None)
    weight = P("expert", None, None)
    grad = P("expert", "dp", None)
    return jax.shard_map(
        shards,
        mesh=mesh,
        in_specs=(rows, rows, rows, rows, weight, weight, weight),
        out_specs=(rows, rows, rows, grad, grad, grad),
        check_vma=False,
    )
```

```python
import functools

import jax
import jax.numpy as jnp
from jax import lax
from jax.experimental import pallas as pl
from jax.experimental.pallas import tpu as pltpu
from jax.sharding import PartitionSpec as P


F32 = jnp.float32
BF16 = jnp.bfloat16
LANES = 128
VMEM_LIMIT = 60 * 1024 * 1024


def round_up(value, unit):
    return -(-value // unit) * unit


def dot(a, b):
    return jnp.dot(a, b, preferred_element_type=F32)


def dot_nt(a, b):
    return lax.dot_general(a, b, (((1,), (1,)), ((), ())), preferred_element_type=F32)


def dot_tn(a, b):
    return lax.dot_general(a, b, (((0,), (0,)), ((), ())), preferred_element_type=F32)


def iota(shape, dim):
    return lax.broadcasted_iota(jnp.int32, shape, dim)


def load_blocks(blocks, held, sems):
    copies, start = [], 0
    for i, block in enumerate(blocks):
        size = block.shape[0]
        copies.append(pltpu.make_async_copy(block, held.at[pl.ds(start, size), :], sems.at[i]))
        start += size
    for copy in copies:
        copy.start()
    for copy in copies:
        copy.wait()


def tiles(width, tile=512):
    return [(start, min(start + tile, width)) for start in range(0, width, tile)]


def half_of(which, width):
    return pl.ds(pl.multiple_of(which * (width // 2), LANES), width // 2)


def hidden_kernel(cfg, first_ref, far_ref, *refs):
    parts, local, cap, cap_pad, top = cfg
    blocks, refs = refs[:parts], refs[parts:]
    gate_ref, up_ref, pre_ref, act_ref, info_ref, pick_ref, combine_ref, keep_ref = refs[:8]
    held, rows_ref, sems = refs[8:]
    expert = pl.program_id(0)
    tokens = held.shape[0]
    width, hidden = gate_ref.shape[1:]

    @pl.when(expert == 0)
    def _():
        load_blocks(blocks, held, sems)
        meta = held[:, width:].astype(F32).astype(jnp.int32)
        lane = iota(meta.shape, 1)
        hits = jnp.zeros(meta.shape, F32)
        for i in range(local):
            named = (meta == first_ref[0] + i) & (lane < top)
            hit = jnp.sum(jnp.where(named, 1.0, 0.0), axis=1, keepdims=True)
            hits = hits + jnp.where(lane == i, hit, 0.0)
        step = min(tokens, 256)
        below = (iota((step, step), 0) >= iota((step, step), 1)).astype(F32).astype(BF16)
        carry = jnp.zeros((1, LANES), F32)
        slots = []
        for start in range(0, tokens, step):
            part = hits[start:start + step]
            rank = dot(below, part.astype(BF16)) + carry
            carry = rank[step - 1:step]
            slots.append(jnp.where(part > 0.0, rank - 1.0, -1.0))
        slots = jnp.concatenate(slots, axis=0)
        slots_t = jnp.transpose(slots)
        places = iota((tokens, cap_pad), 1).astype(F32)
        places_t = iota((cap, tokens), 0).astype(F32)
        for i in range(local):
            hit = slots[:, i:i + 1] == places
            combine_ref[:, i * cap_pad:(i + 1) * cap_pad] = jnp.where(hit, 1.0, 0.0).astype(BF16)
            hit = slots_t[i:i + 1, :] == places_t
            pick_ref[i * cap:(i + 1) * cap, :] = jnp.where(hit, 1.0, 0.0).astype(BF16)
        for start, stop in tiles(held.shape[1]):
            rows_ref[:, start:stop] = dot(pick_ref[...], held[:, start:stop]).astype(BF16)
        keep_ref[...] = held[:, half_of(far_ref[0], width)]

    here = pl.ds(pl.multiple_of(expert * cap, 16), cap)
    pick = pick_ref[here, :].astype(F32)
    token = jnp.sum(pick * iota(pick.shape, 1).astype(F32), axis=1, keepdims=True)
    token = jnp.where(jnp.sum(pick, axis=1, keepdims=True) > 0.0, token, -128.0).astype(jnp.int32)
    meta = rows_ref[here, width:].astype(F32)
    lane = iota(meta.shape, 1)
    named = (meta.astype(jnp.int32) == first_ref[0] + expert) & (lane < top)
    shares = sum(pltpu.roll(meta, LANES - top * (i + 1), 1) for i in range(3))
    share = jnp.sum(jnp.where(named, shares, 0.0), axis=1, keepdims=True)
    info_ref[0] = jnp.where(lane < top, jnp.where(named, 1.0, 0.0), share)

    rows = rows_ref[here, :width]
    gate_pre = dot(rows, gate_ref[0])
    up_pre = dot(rows, up_ref[0])
    pre_ref[0, :, :hidden] = gate_pre
    pre_ref[0, :, hidden:] = up_pre
    active = gate_pre * jax.nn.sigmoid(gate_pre) * up_pre
    act_ref[0, :, :hidden] = (share * active).astype(BF16)
    token_pair = jnp.where(lane == 0, token >> 7, jnp.where(lane == 1, token & 127, 0))
    act_ref[0, :, hidden:] = token_pair.astype(F32).astype(BF16)


def store_parts(plan, value, here, refs):
    refs[0][:, here] = value[:refs[0].shape[0]]
    line, size = refs[0].shape[0], refs[0].shape[0] // sum(len(items) for items in plan)
    for ref, items in zip(refs[1:], plan):
        for i, block in enumerate(items):
            start = line + block * size
            ref[i * size:(i + 1) * size, here] = value[start:start + size]


def mixed_kernel(cfg, far_ref, act_ref, combine_ref, down_ref, *refs):
    plan, levels, local, cap, cap_pad = cfg
    blocks, refs = refs[:levels], refs[levels:]
    outs, give_ref, spread, sems = refs[:-3], refs[-3], refs[-2], refs[-1]
    size = blocks[0].shape[0]
    here = half_of(1 - far_ref[0], blocks[0].shape[1])
    copies = [pltpu.make_async_copy(block.at[:, here], give_ref.at[pl.ds(i * size, size), :], sems.at[i])
              for i, block in enumerate(blocks)]
    hidden = down_ref.shape[2]
    tile = down_ref.shape[1]
    step = pl.program_id(0)

    @pl.when(step == 0)
    def _():
        for copy in copies:
            copy.start()
        for e in range(local):
            here = combine_ref[:, e * cap_pad:e * cap_pad + cap]
            spread[:, e * hidden:(e + 1) * hidden] = dot(here, act_ref[e, :, :hidden]).astype(BF16)

    total = dot_nt(spread[:, :hidden], down_ref[0])
    for e in range(1, local):
        total = total + dot_nt(spread[:, e * hidden:(e + 1) * hidden], down_ref[e])
    store_parts(plan, total.astype(BF16), pl.ds(pl.multiple_of(step * tile, tile), tile), outs)

    @pl.when(step == pl.num_programs(0) - 1)
    def _():
        for copy in copies:
            copy.wait()


def grad_kernel(cfg, far_ref, *refs):
    parts, local, cap, cap_pad, top = cfg
    blocks, refs = refs[:parts], refs[parts:]
    pick_ref, combine_ref, down_ref, pre_ref, info_ref, d_gate_ref, d_up_ref, tail_ref, keep_ref, give_ref = refs[:10]
    held, rows_ref, tails, sems = refs[10:]
    expert = pl.program_id(0)
    hidden = down_ref.shape[2]

    @pl.when(expert == 0)
    def _():
        load_blocks(blocks, held, sems)
        tails[...] = jnp.zeros(tails.shape, BF16)
        for start, stop in tiles(held.shape[1]):
            rows_ref[:, start:stop] = dot(pick_ref[...], held[:, start:stop]).astype(BF16)
        width = held.shape[1]
        keep_ref[...] = held[:, half_of(far_ref[0], width)]
        give_ref[...] = held[give_ref.shape[0]:, half_of(1 - far_ref[0], width)]

    info = info_ref[0]
    lane = iota(info.shape, 1)
    share = info[:, top:top + 1]
    gate_pre, up_pre = pre_ref[0, :, :hidden], pre_ref[0, :, hidden:]
    sig = jax.nn.sigmoid(gate_pre)
    silu = gate_pre * sig
    d_raw = dot(rows_ref[pl.ds(pl.multiple_of(expert * cap, 16), cap), :], down_ref[0])
    share_grad = jnp.sum(silu * up_pre * d_raw, axis=1, keepdims=True)
    d_active = share * d_raw
    d_gate_ref[0] = (d_active * up_pre * sig * (1.0 + gate_pre * (1.0 - sig))).astype(BF16)
    d_up_ref[0] = (d_active * silu).astype(BF16)
    placed = jnp.where((lane < top) & (info > 0.0), share_grad, 0.0)
    high = placed.astype(BF16)
    rest = placed - high.astype(F32)
    middle = rest.astype(BF16)
    low = (rest - middle.astype(F32)).astype(BF16)
    tail = high.astype(F32) + pltpu.roll(middle.astype(F32), top, 1) + pltpu.roll(low.astype(F32), 2 * top, 1)
    tails[pl.ds(pl.multiple_of(expert * cap_pad, cap_pad), cap), :] = tail.astype(BF16)

    @pl.when(expert == local - 1)
    def _():
        tail_ref[...] = dot(combine_ref[...], tails[...]).astype(BF16)


def input_kernel(cfg, d_gate_ref, d_up_ref, combine_ref, tail_ref, gate_ref, up_ref, *refs):
    plan, local, cap, cap_pad = cfg
    outs, rows = refs[:-1], refs[-1]
    tile, hidden = gate_ref.shape[1:]
    step = pl.program_id(0)

    @pl.when(step == 0)
    def _():
        rows[...] = jnp.zeros(rows.shape, BF16)
        width = outs[0].shape[1] - LANES
        store_parts(plan, tail_ref[...], slice(width, width + LANES), outs)

    for e in range(local):
        part = dot_nt(d_gate_ref[e], gate_ref[e]) + dot_nt(d_up_ref[e], up_ref[e])
        rows[e * cap_pad:e * cap_pad + cap, :] = part.astype(BF16)
    total = dot(combine_ref[...], rows[...]).astype(BF16)
    store_parts(plan, total, pl.ds(pl.multiple_of(step * tile, tile), tile), outs)


def store_halves(part, near_ref, both, keep_ref, give_ref):
    both[...] = part.astype(BF16)
    size = keep_ref.shape[1]
    keep_ref[0] = both[pl.ds(pl.multiple_of(near_ref[0] * size, 16), size), :]
    give_ref[0] = both[pl.ds(pl.multiple_of((1 - near_ref[0]) * size, 16), size), :]


def down_kernel(cap, near_ref, pick_ref, *refs):
    x_refs, c_refs, (act_ref, act_far_ref, rows_ref, keep_ref, give_ref, c_rows, acts, both) = refs[:3], refs[3:6], refs[6:]
    hidden = acts.shape[1]
    line = x_refs[1].shape[0]
    acts[:cap, :] = act_ref[0, :, :hidden]
    acts[cap:, :] = act_far_ref[0, :, :hidden]
    pair = act_far_ref[0, :, hidden:].astype(F32)
    token = pair[:, 0:1] * 128.0 + pair[:, 1:2]
    pick = pick_ref[...]
    pick_far = jnp.where(token == iota(pick.shape, 1).astype(F32), 1.0, 0.0).astype(BF16)
    for (own, far, far_pair), rows in ((x_refs, rows_ref.at[0]), (c_refs, c_rows)):
        rows[:cap, :] = dot(pick, own[...]).astype(BF16)
        rows[cap:, :] = (dot(pick_far[:, :line], far[...]) + dot(pick_far[:, line:], far_pair[...])).astype(BF16)
    store_halves(dot_tn(c_rows[...], acts[...]), near_ref, both, keep_ref, give_ref)


def partial_kernel(cap, near_ref, rows_ref, own_ref, far_ref, keep_ref, give_ref, grads, both):
    grads[:cap, :] = own_ref[0]
    grads[cap:, :] = far_ref[0]
    store_halves(dot_tn(rows_ref[0], grads[...]), near_ref, both, keep_ref, give_ref)


def cut_kernel(half, plan, word_ref, *refs):
    count = 1 + max(i for i, _, _, _ in plan)
    blocks, outs, sems = refs[:count], refs[count:-1], refs[-1]
    copies = []
    for i, flip, out, row in plan:
        which = 1 - word_ref[0] if flip else word_ref[0]
        here = pl.ds(pl.multiple_of(which * half, LANES), half)
        there = outs[out].at[pl.ds(row, blocks[i].shape[0]), :]
        copies.append(pltpu.make_async_copy(blocks[i].at[:, here], there, sems.at[len(copies)]))
    for copy in copies:
        copy.start()
    for copy in copies:
        copy.wait()


def swap(value, bit, count):
    return lax.ppermute(value, "dp", [(i, i ^ bit) for i in range(count)])


def exchange(value, bit, count):
    return lax.ppermute(value, "expert", [(i, i ^ bit) for i in range(count)])


def fence(*values):
    leaves, tree = jax.tree.flatten(values)
    return jax.tree.unflatten(tree, lax.optimization_barrier(tuple(leaves)))


def split3(value):
    high = lax.reduce_precision(value, 8, 7)
    rest = value - high
    middle = lax.reduce_precision(rest, 8, 7)
    return [high.astype(BF16), middle.astype(BF16), (rest - middle).astype(BF16)]


def shards(tokens, routes, probs, cotangent, w_gate, w_up, w_down):
    tok_rows, top = routes.shape
    local, width, hidden = w_gate.shape
    n_exp = lax.axis_size("expert")
    n_dp = lax.axis_size("dp")
    experts = local * n_exp
    cap = 5 * tok_rows * top // (4 * experts) * n_exp
    cap_pad = round_up(cap, LANES)
    total = n_exp * tok_rows
    levels = n_exp // 2
    line = levels * tok_rows
    wide = width + LANES
    tile = min(width, 512)
    columns = width // n_dp
    half = width // 2
    far_bit = n_dp // 2
    my_dp = lax.axis_index("dp")
    far = jnp.where((my_dp & far_bit) > 0, 1, 0)
    near = jnp.where((my_dp & 1) > 0, 1, 0)
    near_word = near.astype(jnp.int32).reshape(1)
    far_word = far.astype(jnp.int32).reshape(1)
    first = (lax.axis_index("expert") * local).astype(jnp.int32).reshape(1)
    line_blocks = list(range(0, n_exp, 2))
    sides = [k for k in line_blocks if k & 2 and k > 2]
    folds = [k ^ 2 for k in sides]
    groups = [sides, folds, [2, 0]]
    plan = [[k // 2 for k in group] for group in groups]
    upper_bits = [1 << i for i in range(2, n_exp.bit_length() - 1)]

    def send(value, bit):
        return exchange(value, bit, n_exp)

    def gather_upper(value):
        blocks = {0: value}
        for bit in reversed(upper_bits):
            blocks.update({k | bit: send(block, bit) for k, block in list(blocks.items())})
        return blocks

    any_space = pl.BlockSpec(memory_space=pl.ANY)
    smem = pl.BlockSpec(memory_space=pltpu.SMEM)
    params = pltpu.CompilerParams(dimension_semantics=("arbitrary",), vmem_limit_bytes=VMEM_LIMIT)

    def by_expert(*shape):
        return pl.BlockSpec((1,) + shape, lambda e: (e,) + (0,) * len(shape))

    def whole(*shape):
        return pl.BlockSpec(shape, lambda e: (0,) * len(shape))

    def sds(shape, dtype):
        return jax.ShapeDtypeStruct(shape, dtype)

    def cost(gflop, mbyte):
        return pl.CostEstimate(flops=gflop * 10**6, bytes_accessed=mbyte * 10**3, transcendentals=0)

    def cut_blocks(word, blocks, size, wanted, name):
        plan, rows = [], []
        for out, items in enumerate(wanted):
            rows.append(0)
            for i, flip in items:
                plan.append((i, flip, out, rows[out]))
                rows[out] += blocks[i].shape[0]
        return pl.pallas_call(
            functools.partial(cut_kernel, size, plan),
            in_specs=[smem] + [any_space] * len(blocks),
            out_specs=[pl.BlockSpec(memory_space=pltpu.VMEM)] * len(wanted),
            out_shape=[sds((n, size), BF16) for n in rows],
            scratch_shapes=[pltpu.SemaphoreType.DMA((len(plan),))],
            compiler_params=pltpu.CompilerParams(vmem_limit_bytes=VMEM_LIMIT),
            cost_estimate=cost(0, 2),
            name=name,
        )(word, *blocks)

    def cut_far(blocks, name):
        return cut_blocks(far_word, blocks, width // 2, [[(i, 1) for i in range(len(blocks))]], name)[0]

    by_columns = pl.BlockSpec((local, tile, hidden), lambda j: (0, j, 0))
    weight_spec = by_expert(width, hidden)
    parts = n_exp
    cfg = (parts, local, cap, cap_pad, top)

    totals = jnp.sum(probs, axis=1, keepdims=True)
    share = probs / totals
    meta = jnp.concatenate([routes.astype(BF16)] + split3(share), axis=1)
    meta = jnp.pad(meta, ((0, 0), (0, LANES - 4 * top)))

    x_own = jnp.concatenate([tokens, meta], axis=1)
    x_line = gather_upper(x_own)
    x_line[2] = send(x_own, 2)
    x_pair = {k: send(x_line[k], 1) for k in (0, 2)}
    x_line, x_pair, cot = fence(x_line, x_pair, cotangent)

    x_line.update({k | 2: send(x_line[k], 2) for k in folds})
    x_pair.update({k: send(x_line[k], 1) for k in folds})
    c_line = gather_upper(cot)
    c_line[2] = send(cot, 2)
    c_pair = {0: send(cot, 1)}
    x_line, c_line, x_pair, c_pair = fence(x_line, c_line, x_pair, c_pair)
    x_pair.update({k: send(x_line[k], 1) for k in sides})
    x_far = swap(cut_far([x_line[k] for k in line_blocks], "cut_x"), far_bit, n_dp)
    x_pair, c_line = fence(x_pair, c_line)

    c_line.update({k | 2: send(c_line[k], 2) for k in folds})
    c_pair.update({k: send(c_line[k], 1) for k in [2] + folds})
    x_far_pair = swap(cut_far([x_pair[k] for k in line_blocks], "cut_x_pair"), far_bit, n_dp)
    pre, act, info, pick, combine, x_keep = pl.pallas_call(
        functools.partial(hidden_kernel, cfg),
        grid=(local,),
        in_specs=[smem] * 2 + [any_space] * parts + [weight_spec] * 2,
        out_specs=[by_expert(cap, 2 * hidden), by_expert(cap, hidden + LANES), by_expert(cap, LANES),
                   whole(local * cap, total), whole(total, local * cap_pad), whole(total, half)],
        out_shape=[sds((local, cap, 2 * hidden), F32), sds((local, cap, hidden + LANES), BF16),
                   sds((local, cap, LANES), F32), sds((local * cap, total), BF16), sds((total, local * cap_pad), BF16),
                   sds((total, half), BF16)],
        scratch_shapes=[
            pltpu.VMEM((total, wide), BF16),
            pltpu.VMEM((local * cap, wide), BF16),
            pltpu.SemaphoreType.DMA((parts,)),
        ],
        compiler_params=params,
        cost_estimate=cost(6, 20),
        name="hidden",
    )(first, far_word, *[x_line[k] for k in line_blocks], *[x_pair[k] for k in line_blocks], w_gate, w_up)
    act, c_line, c_pair, x_far = fence(act, c_line, c_pair, x_far)

    c_pair.update({k: send(c_line[k], 1) for k in sides})
    act_far = swap(act, far_bit, n_dp)
    level_rows = [line] + [len(group) * tok_rows for group in groups]
    level_specs = [whole(rows, width) for rows in level_rows]
    mixed_keep, *mixed_out, c_give = pl.pallas_call(
        functools.partial(mixed_kernel, (plan, levels, local, cap, cap_pad)),
        grid=(width // tile,),
        in_specs=[smem, whole(local, cap, hidden + LANES), whole(total, local * cap_pad), by_columns] + [any_space] * levels,
        out_specs=level_specs + [whole(line, half)],
        out_shape=[sds((rows, width), BF16) for rows in level_rows] + [sds((line, half), BF16)],
        scratch_shapes=[pltpu.VMEM((total, local * hidden), BF16), pltpu.SemaphoreType.DMA((levels,))],
        compiler_params=params,
        cost_estimate=cost(6, 10),
        name="mixed",
    )(far_word, act, combine, w_down, *[c_line[k] for k in line_blocks])
    c_pair, mixed_keep, mixed_out, c_give, x_far_pair = fence(c_pair, mixed_keep, mixed_out, c_give, x_far_pair)

    def back_rows(keep, got):
        return keep.astype(F32) + got.astype(F32)

    def pair_sums(keep, got, group):
        mine = jnp.concatenate([keep[k // 2 * tok_rows:(k // 2 + 1) * tok_rows] for k in group], axis=0)
        return back_rows(mine, got)

    def fold_upper(sums):
        blocks = {k: sums[i * tok_rows:(i + 1) * tok_rows] for i, k in enumerate(folds)}
        landed = []
        for bit in upper_bits:
            for k in [k for k in blocks if k & bit]:
                got = send(blocks.pop(k).astype(BF16), bit)
                if k == bit:
                    landed.append(got)
                else:
                    blocks[k ^ bit] = back_rows(blocks[k ^ bit], got)
        return landed

    def finish(sums, landed):
        return sum([part.astype(F32) for part in landed], sums[tok_rows:].astype(F32))

    mixed_got = [send(part, 1) for part in mixed_out[:2]]
    c_far = swap(c_give, far_bit, n_dp)
    d_gate, d_up, tail, c_keep, c_give = pl.pallas_call(
        functools.partial(grad_kernel, cfg),
        grid=(local,),
        in_specs=[smem] + [any_space] * parts + [whole(local * cap, total), whole(total, local * cap_pad), weight_spec,
                                                 by_expert(cap, 2 * hidden), by_expert(cap, LANES)],
        out_specs=[by_expert(cap, hidden)] * 2 + [whole(total, LANES), whole(total, half), whole(line, half)],
        out_shape=[sds((local, cap, hidden), BF16)] * 2 + [sds((total, LANES), BF16),
                   sds((total, half), BF16), sds((line, half), BF16)],
        scratch_shapes=[
            pltpu.VMEM((total, width), BF16),
            pltpu.VMEM((local * cap, width), BF16),
            pltpu.VMEM((local * cap_pad, LANES), BF16),
            pltpu.SemaphoreType.DMA((parts,)),
        ],
        compiler_params=params,
        cost_estimate=cost(6, 12),
        name="hidden_grads",
    )(far_word, *[c_line[k] for k in line_blocks], *[c_pair[k] for k in line_blocks], pick, combine, w_down, pre, info)
    mixed_sides, mixed_got, mixed_out, d_gate, d_up, tail, c_give, act_far = fence(
        pair_sums(mixed_keep, mixed_got[0], sides).astype(BF16), mixed_got, mixed_out, d_gate, d_up, tail, c_give, act_far)

    mixed_sides = send(mixed_sides, 2)
    mixed_got.append(send(mixed_out[2], 1))
    c_far_pair = swap(c_give, far_bit, n_dp)
    gate_far = swap(d_gate, far_bit, n_dp)
    wide_specs = [whole(rows, wide) for rows in level_rows]
    input_keep, *input_out = pl.pallas_call(
        functools.partial(input_kernel, (plan, local, cap, cap_pad)),
        grid=(width // tile,),
        in_specs=[whole(local, cap, hidden)] * 2 + [whole(total, local * cap_pad), whole(total, LANES),
                                                    by_columns, by_columns],
        out_specs=wide_specs,
        out_shape=[sds((rows, wide), BF16) for rows in level_rows],
        scratch_shapes=[pltpu.VMEM((local * cap_pad, tile), BF16)],
        compiler_params=params,
        cost_estimate=cost(6, 16),
        name="input_grads",
    )(d_gate, d_up, combine, tail, w_gate, w_up)
    input_keep, input_out, mixed_sides, mixed_got, c_far, d_up = fence(
        input_keep, input_out, mixed_sides, mixed_got, c_far, d_up)

    input_got = [send(part, 1) for part in input_out[:2]]
    mixed_landed = fold_upper(back_rows(pair_sums(mixed_keep, mixed_got[1], folds), mixed_sides))
    mixed_ends = pair_sums(mixed_keep, mixed_got[2], [2, 0])
    mixed_landed.append(send(mixed_ends[:tok_rows].astype(BF16), 2))
    input_sides, input_out = fence(pair_sums(input_keep, input_got[0], sides).astype(BF16), input_out)
    input_sides = send(input_sides, 2)
    input_folds, c_far_pair, mixed_landed, d_up, x_keep = fence(
        back_rows(pair_sums(input_keep, input_got[1], folds), input_sides).astype(BF16), c_far_pair, mixed_landed, d_up, x_keep)
    input_landed = fold_upper(input_folds)
    input_got.append(send(input_out[2], 1))
    up_far = swap(d_up, far_bit, n_dp)
    partial_specs = [by_expert(columns, hidden)] * 2
    partial_shapes = [sds((local, columns, hidden), BF16)] * 2
    x_rows, down_keep, down_give = pl.pallas_call(
        functools.partial(down_kernel, cap),
        grid=(local,),
        in_specs=[smem, pl.BlockSpec((cap, total), lambda e: (e, 0))] + [whole(total, half), whole(line, half), whole(line, half)] * 2
        + [by_expert(cap, hidden + LANES)] * 2,
        out_specs=[by_expert(2 * cap, half)] + partial_specs,
        out_shape=[sds((local, 2 * cap, half), BF16)] + partial_shapes,
        scratch_shapes=[pltpu.VMEM((2 * cap, half), BF16), pltpu.VMEM((2 * cap, hidden), BF16), pltpu.VMEM((half, hidden), BF16)],
        compiler_params=params,
        cost_estimate=cost(6, 12),
        name="down_grads",
    )(near_word, pick, x_keep, x_far, x_far_pair, c_keep, c_far, c_far_pair, act, act_far)
    input_ends, input_landed, x_rows, down_keep, down_give, gate_far = fence(
        pair_sums(input_keep, input_got[2], [2, 0]), input_landed, x_rows, down_keep, down_give, gate_far)

    input_landed.append(send(input_ends[:tok_rows].astype(BF16), 2))
    down_got = swap(down_give, 1, n_dp)

    def partial_grads(grads, grads_far, name):
        return pl.pallas_call(
            functools.partial(partial_kernel, cap),
            grid=(local,),
            in_specs=[smem, by_expert(2 * cap, half)] + [by_expert(cap, hidden)] * 2,
            out_specs=partial_specs,
            out_shape=partial_shapes,
            scratch_shapes=[pltpu.VMEM((2 * cap, hidden), BF16), pltpu.VMEM((half, hidden), BF16)],
            compiler_params=params,
            cost_estimate=cost(3, 10),
            name=name,
        )(near_word, x_rows, grads, grads_far)

    gate_keep, gate_give = partial_grads(d_gate, gate_far, "gate_grads")
    gate_got = swap(gate_give, 1, n_dp)
    down_grad = back_rows(down_keep, down_got).astype(BF16)
    gate_grad = back_rows(gate_keep, gate_got).astype(BF16)
    up_far, input_landed, gate_grad, down_grad = fence(up_far, input_landed, gate_grad, down_grad)
    up_keep, up_give = partial_grads(d_up, up_far, "up_grads")
    up_got = swap(up_give, 1, n_dp)
    up_grad = back_rows(up_keep, up_got).astype(BF16)

    mixed = finish(mixed_ends, mixed_landed).astype(BF16)
    back = finish(input_ends, input_landed)
    token_grad = back[:, :width].astype(BF16)
    tail = back[:, width:]
    slot_sg = tail[:, :top] + tail[:, top:2 * top] + tail[:, 2 * top:3 * top]
    prob_grad = (slot_sg - jnp.sum(share * slot_sg, axis=1, keepdims=True)) / totals
    return mixed, token_grad, prob_grad, gate_grad, up_grad, down_grad


def solution(mesh):
    rows = P(("expert", "dp"), None)
    weight = P("expert", None, None)
    grad = P("expert", "dp", None)
    return jax.shard_map(
        shards,
        mesh=mesh,
        in_specs=(rows, rows, rows, rows, weight, weight, weight),
        out_specs=(rows, rows, rows, grad, grad, grad),
        check_vma=False,
    )
```

```python
import functools

import jax
import jax.numpy as jnp
from jax import lax
from jax.experimental import pallas as pl
from jax.experimental.pallas import tpu as pltpu
from jax.sharding import PartitionSpec as P


F32 = jnp.float32
BF16 = jnp.bfloat16
LANES = 128
VMEM_LIMIT = 60 * 1024 * 1024


def round_up(value, unit):
    return -(-value // unit) * unit


def dot(a, b):
    return jnp.dot(a, b, preferred_element_type=F32)


def dot_nt(a, b):
    return lax.dot_general(a, b, (((1,), (1,)), ((), ())), preferred_element_type=F32)


def dot_tn(a, b):
    return lax.dot_general(a, b, (((0,), (0,)), ((), ())), preferred_element_type=F32)


def iota(shape, dim):
    return lax.broadcasted_iota(jnp.int32, shape, dim)


def load_blocks(blocks, held, sems):
    copies, start = [], 0
    for i, block in enumerate(blocks):
        size = block.shape[0]
        copies.append(pltpu.make_async_copy(block, held.at[pl.ds(start, size), :], sems.at[i]))
        start += size
    for copy in copies:
        copy.start()
    for copy in copies:
        copy.wait()


def tiles(width, tile=512):
    return [(start, min(start + tile, width)) for start in range(0, width, tile)]


def half_of(which, width):
    return pl.ds(pl.multiple_of(which * (width // 2), LANES), width // 2)


def hidden_kernel(cfg, first_ref, far_ref, *refs):
    parts, local, cap, cap_pad, top = cfg
    blocks, refs = refs[:parts], refs[parts:]
    gate_ref, up_ref, pre_ref, act_ref, info_ref, pick_ref, combine_ref, keep_ref, give_ref = refs[:9]
    held, rows_ref, sems = refs[9:]
    expert = pl.program_id(0)
    tokens = held.shape[0]
    width, hidden = gate_ref.shape[1:]

    @pl.when(expert == 0)
    def _():
        load_blocks(blocks, held, sems)
        meta = held[:, width:].astype(F32).astype(jnp.int32)
        lane = iota(meta.shape, 1)
        hits = jnp.zeros(meta.shape, F32)
        for i in range(local):
            named = (meta == first_ref[0] + i) & (lane < top)
            hit = jnp.sum(jnp.where(named, 1.0, 0.0), axis=1, keepdims=True)
            hits = hits + jnp.where(lane == i, hit, 0.0)
        step = min(tokens, 256)
        below = (iota((step, step), 0) >= iota((step, step), 1)).astype(F32).astype(BF16)
        carry = jnp.zeros((1, LANES), F32)
        slots = []
        for start in range(0, tokens, step):
            part = hits[start:start + step]
            rank = dot(below, part.astype(BF16)) + carry
            carry = rank[step - 1:step]
            slots.append(jnp.where(part > 0.0, rank - 1.0, -1.0))
        slots = jnp.concatenate(slots, axis=0)
        slots_t = jnp.transpose(slots)
        places = iota((tokens, cap_pad), 1).astype(F32)
        places_t = iota((cap, tokens), 0).astype(F32)
        for i in range(local):
            hit = slots[:, i:i + 1] == places
            combine_ref[:, i * cap_pad:(i + 1) * cap_pad] = jnp.where(hit, 1.0, 0.0).astype(BF16)
            hit = slots_t[i:i + 1, :] == places_t
            pick_ref[i * cap:(i + 1) * cap, :] = jnp.where(hit, 1.0, 0.0).astype(BF16)
        for start, stop in tiles(held.shape[1]):
            rows_ref[:, start:stop] = dot(pick_ref[...], held[:, start:stop]).astype(BF16)
        keep_ref[...] = held[:, half_of(far_ref[0], width)]
        give_ref[...] = held[give_ref.shape[0]:, half_of(1 - far_ref[0], width)]

    here = pl.ds(pl.multiple_of(expert * cap, 16), cap)
    pick = pick_ref[here, :].astype(F32)
    token = jnp.sum(pick * iota(pick.shape, 1).astype(F32), axis=1, keepdims=True)
    token = jnp.where(jnp.sum(pick, axis=1, keepdims=True) > 0.0, token, -128.0).astype(jnp.int32)
    meta = rows_ref[here, width:].astype(F32)
    lane = iota(meta.shape, 1)
    named = (meta.astype(jnp.int32) == first_ref[0] + expert) & (lane < top)
    shares = sum(pltpu.roll(meta, LANES - top * (i + 1), 1) for i in range(3))
    share = jnp.sum(jnp.where(named, shares, 0.0), axis=1, keepdims=True)
    info_ref[0] = jnp.where(lane < top, jnp.where(named, 1.0, 0.0), share)

    rows = rows_ref[here, :width]
    gate_pre = dot(rows, gate_ref[0])
    up_pre = dot(rows, up_ref[0])
    pre_ref[0, :, :hidden] = gate_pre
    pre_ref[0, :, hidden:] = up_pre
    active = gate_pre * jax.nn.sigmoid(gate_pre) * up_pre
    act_ref[0, :, :hidden] = (share * active).astype(BF16)
    token_pair = jnp.where(lane == 0, token >> 7, jnp.where(lane == 1, token & 127, 0))
    act_ref[0, :, hidden:] = token_pair.astype(F32).astype(BF16)


def store_parts(plan, value, here, refs):
    refs[0][:, here] = value[:refs[0].shape[0]]
    line, size = refs[0].shape[0], refs[0].shape[0] // sum(len(items) for items in plan)
    for ref, items in zip(refs[1:], plan):
        for i, block in enumerate(items):
            start = line + block * size
            ref[i * size:(i + 1) * size, here] = value[start:start + size]


def mixed_kernel(cfg, far_ref, act_ref, combine_ref, down_ref, *refs):
    plan, levels, local, cap, cap_pad = cfg
    blocks, refs = refs[:levels], refs[levels:]
    outs, give_ref, spread, sems = refs[:-3], refs[-3], refs[-2], refs[-1]
    size = blocks[0].shape[0]
    here = half_of(1 - far_ref[0], blocks[0].shape[1])
    copies = [pltpu.make_async_copy(block.at[:, here], give_ref.at[pl.ds(i * size, size), :], sems.at[i])
              for i, block in enumerate(blocks)]
    hidden = down_ref.shape[2]
    tile = down_ref.shape[1]
    step = pl.program_id(0)

    @pl.when(step == 0)
    def _():
        for copy in copies:
            copy.start()
        for e in range(local):
            here = combine_ref[:, e * cap_pad:e * cap_pad + cap]
            spread[:, e * hidden:(e + 1) * hidden] = dot(here, act_ref[e, :, :hidden]).astype(BF16)

    total = dot_nt(spread[:, :hidden], down_ref[0])
    for e in range(1, local):
        total = total + dot_nt(spread[:, e * hidden:(e + 1) * hidden], down_ref[e])
    store_parts(plan, total.astype(BF16), pl.ds(pl.multiple_of(step * tile, tile), tile), outs)

    @pl.when(step == pl.num_programs(0) - 1)
    def _():
        for copy in copies:
            copy.wait()


def grad_kernel(cfg, far_ref, *refs):
    parts, local, cap, cap_pad, top = cfg
    blocks, refs = refs[:parts], refs[parts:]
    pick_ref, combine_ref, down_ref, pre_ref, info_ref, d_gate_ref, d_up_ref, tail_ref, keep_ref, give_ref = refs[:10]
    held, rows_ref, tails, sems = refs[10:]
    expert = pl.program_id(0)
    hidden = down_ref.shape[2]

    @pl.when(expert == 0)
    def _():
        load_blocks(blocks, held, sems)
        tails[...] = jnp.zeros(tails.shape, BF16)
        for start, stop in tiles(held.shape[1]):
            rows_ref[:, start:stop] = dot(pick_ref[...], held[:, start:stop]).astype(BF16)
        width = held.shape[1]
        keep_ref[...] = held[:, half_of(far_ref[0], width)]
        give_ref[...] = held[give_ref.shape[0]:, half_of(1 - far_ref[0], width)]

    info = info_ref[0]
    lane = iota(info.shape, 1)
    share = info[:, top:top + 1]
    gate_pre, up_pre = pre_ref[0, :, :hidden], pre_ref[0, :, hidden:]
    sig = jax.nn.sigmoid(gate_pre)
    silu = gate_pre * sig
    d_raw = dot(rows_ref[pl.ds(pl.multiple_of(expert * cap, 16), cap), :], down_ref[0])
    share_grad = jnp.sum(silu * up_pre * d_raw, axis=1, keepdims=True)
    d_active = share * d_raw
    d_gate_ref[0] = (d_active * up_pre * sig * (1.0 + gate_pre * (1.0 - sig))).astype(BF16)
    d_up_ref[0] = (d_active * silu).astype(BF16)
    placed = jnp.where((lane < top) & (info > 0.0), share_grad, 0.0)
    high = placed.astype(BF16)
    rest = placed - high.astype(F32)
    middle = rest.astype(BF16)
    low = (rest - middle.astype(F32)).astype(BF16)
    tail = high.astype(F32) + pltpu.roll(middle.astype(F32), top, 1) + pltpu.roll(low.astype(F32), 2 * top, 1)
    tails[pl.ds(pl.multiple_of(expert * cap_pad, cap_pad), cap), :] = tail.astype(BF16)

    @pl.when(expert == local - 1)
    def _():
        tail_ref[...] = dot(combine_ref[...], tails[...]).astype(BF16)


def input_kernel(cfg, d_gate_ref, d_up_ref, combine_ref, tail_ref, gate_ref, up_ref, *refs):
    plan, local, cap, cap_pad = cfg
    outs, rows = refs[:-1], refs[-1]
    tile, hidden = gate_ref.shape[1:]
    step = pl.program_id(0)

    @pl.when(step == 0)
    def _():
        rows[...] = jnp.zeros(rows.shape, BF16)
        width = outs[0].shape[1] - LANES
        store_parts(plan, tail_ref[...], slice(width, width + LANES), outs)

    for e in range(local):
        part = dot_nt(d_gate_ref[e], gate_ref[e]) + dot_nt(d_up_ref[e], up_ref[e])
        rows[e * cap_pad:e * cap_pad + cap, :] = part.astype(BF16)
    total = dot(combine_ref[...], rows[...]).astype(BF16)
    store_parts(plan, total, pl.ds(pl.multiple_of(step * tile, tile), tile), outs)


def store_halves(part, near_ref, both, keep_ref, give_ref):
    both[...] = part.astype(BF16)
    size = keep_ref.shape[1]
    keep_ref[0] = both[pl.ds(pl.multiple_of(near_ref[0] * size, 16), size), :]
    give_ref[0] = both[pl.ds(pl.multiple_of((1 - near_ref[0]) * size, 16), size), :]


def down_kernel(cap, near_ref, pick_ref, *refs):
    x_refs, c_refs, (act_ref, act_far_ref, rows_ref, keep_ref, give_ref, c_rows, acts, both) = refs[:3], refs[3:6], refs[6:]
    hidden = acts.shape[1]
    line = x_refs[1].shape[0]
    acts[:cap, :] = act_ref[0, :, :hidden]
    acts[cap:, :] = act_far_ref[0, :, :hidden]
    pair = act_far_ref[0, :, hidden:].astype(F32)
    token = pair[:, 0:1] * 128.0 + pair[:, 1:2]
    pick = pick_ref[...]
    pick_far = jnp.where(token == iota(pick.shape, 1).astype(F32), 1.0, 0.0).astype(BF16)
    for (own, far, far_pair), rows in ((x_refs, rows_ref.at[0]), (c_refs, c_rows)):
        rows[:cap, :] = dot(pick, own[...]).astype(BF16)
        rows[cap:, :] = (dot(pick_far[:, :line], far[...]) + dot(pick_far[:, line:], far_pair[...])).astype(BF16)
    store_halves(dot_tn(c_rows[...], acts[...]), near_ref, both, keep_ref, give_ref)


def both_kernel(cap, near_ref, rows_ref, d_gate_ref, gate_far_ref, d_up_ref, up_far_ref, keep_ref, give_ref, grads, both):
    hidden = d_gate_ref.shape[2]
    grads[:cap, :hidden] = d_gate_ref[0]
    grads[cap:, :hidden] = gate_far_ref[0]
    grads[:cap, hidden:] = d_up_ref[0]
    grads[cap:, hidden:] = up_far_ref[0]
    store_halves(dot_tn(rows_ref[0], grads[...]), near_ref, both, keep_ref, give_ref)


def cut_kernel(half, plan, word_ref, *refs):
    count = 1 + max(i for i, _, _, _ in plan)
    blocks, outs, sems = refs[:count], refs[count:-1], refs[-1]
    copies = []
    for i, flip, out, row in plan:
        which = 1 - word_ref[0] if flip else word_ref[0]
        here = pl.ds(pl.multiple_of(which * half, LANES), half)
        there = outs[out].at[pl.ds(row, blocks[i].shape[0]), :]
        copies.append(pltpu.make_async_copy(blocks[i].at[:, here], there, sems.at[len(copies)]))
    for copy in copies:
        copy.start()
    for copy in copies:
        copy.wait()


def swap(value, bit, count):
    return lax.ppermute(value, "dp", [(i, i ^ bit) for i in range(count)])


def exchange(value, bit, count):
    return lax.ppermute(value, "expert", [(i, i ^ bit) for i in range(count)])


def fence(*values):
    leaves, tree = jax.tree.flatten(values)
    return jax.tree.unflatten(tree, lax.optimization_barrier(tuple(leaves)))


def split3(value):
    high = lax.reduce_precision(value, 8, 7)
    rest = value - high
    middle = lax.reduce_precision(rest, 8, 7)
    return [high.astype(BF16), middle.astype(BF16), (rest - middle).astype(BF16)]


def shards(tokens, routes, probs, cotangent, w_gate, w_up, w_down):
    tok_rows, top = routes.shape
    local, width, hidden = w_gate.shape
    n_exp = lax.axis_size("expert")
    n_dp = lax.axis_size("dp")
    experts = local * n_exp
    cap = 5 * tok_rows * top // (4 * experts) * n_exp
    cap_pad = round_up(cap, LANES)
    total = n_exp * tok_rows
    levels = n_exp // 2
    line = levels * tok_rows
    wide = width + LANES
    tile = min(width, 512)
    columns = width // n_dp
    half = width // 2
    far_bit = n_dp // 2
    my_dp = lax.axis_index("dp")
    far = jnp.where((my_dp & far_bit) > 0, 1, 0)
    near = jnp.where((my_dp & 1) > 0, 1, 0)
    near_word = near.astype(jnp.int32).reshape(1)
    far_word = far.astype(jnp.int32).reshape(1)
    first = (lax.axis_index("expert") * local).astype(jnp.int32).reshape(1)
    line_blocks = list(range(0, n_exp, 2))
    sides = [k for k in line_blocks if k & 2 and k > 2]
    folds = [k ^ 2 for k in sides]
    groups = [sides, folds, [2, 0]]
    plan = [[k // 2 for k in group] for group in groups]
    upper_bits = [1 << i for i in range(2, n_exp.bit_length() - 1)]

    def send(value, bit):
        return exchange(value, bit, n_exp)

    def gather_upper(value):
        blocks = {0: value}
        for bit in reversed(upper_bits):
            blocks.update({k | bit: send(block, bit) for k, block in list(blocks.items())})
        return blocks

    any_space = pl.BlockSpec(memory_space=pl.ANY)
    smem = pl.BlockSpec(memory_space=pltpu.SMEM)
    params = pltpu.CompilerParams(dimension_semantics=("arbitrary",), vmem_limit_bytes=VMEM_LIMIT)

    def by_expert(*shape):
        return pl.BlockSpec((1,) + shape, lambda e: (e,) + (0,) * len(shape))

    def whole(*shape):
        return pl.BlockSpec(shape, lambda e: (0,) * len(shape))

    def sds(shape, dtype):
        return jax.ShapeDtypeStruct(shape, dtype)

    def cost(gflop, mbyte):
        return pl.CostEstimate(flops=gflop * 10**6, bytes_accessed=mbyte * 10**3, transcendentals=0)

    def cut_blocks(word, blocks, size, wanted, name):
        plan, rows = [], []
        for out, items in enumerate(wanted):
            rows.append(0)
            for i, flip in items:
                plan.append((i, flip, out, rows[out]))
                rows[out] += blocks[i].shape[0]
        return pl.pallas_call(
            functools.partial(cut_kernel, size, plan),
            in_specs=[smem] + [any_space] * len(blocks),
            out_specs=[pl.BlockSpec(memory_space=pltpu.VMEM)] * len(wanted),
            out_shape=[sds((n, size), BF16) for n in rows],
            scratch_shapes=[pltpu.SemaphoreType.DMA((len(plan),))],
            compiler_params=pltpu.CompilerParams(vmem_limit_bytes=VMEM_LIMIT),
            cost_estimate=cost(0, 2),
            name=name,
        )(word, *blocks)

    def cut_far(blocks, name):
        return cut_blocks(far_word, blocks, width // 2, [[(i, 1) for i in range(len(blocks))]], name)[0]

    by_columns = pl.BlockSpec((local, tile, hidden), lambda j: (0, j, 0))
    weight_spec = by_expert(width, hidden)
    parts = n_exp
    cfg = (parts, local, cap, cap_pad, top)

    totals = jnp.sum(probs, axis=1, keepdims=True)
    share = probs / totals
    meta = jnp.concatenate([routes.astype(BF16)] + split3(share), axis=1)
    meta = jnp.pad(meta, ((0, 0), (0, LANES - 4 * top)))

    x_own = jnp.concatenate([tokens, meta], axis=1)
    x_line = gather_upper(x_own)
    x_line[2] = send(x_own, 2)
    x_pair = {k: send(x_line[k], 1) for k in (0, 2)}
    x_line, x_pair[0], cot = fence(x_line, x_pair[0], cotangent)

    x_line.update({k | 2: send(x_line[k], 2) for k in folds})
    c_line = gather_upper(cot)
    x_pair.update({k: send(x_line[k], 1) for k in folds})
    x_line, c_line, x_pair = fence(x_line, c_line, x_pair)
    x_pair.update({k: send(x_line[k], 1) for k in sides})
    x_far = swap(cut_far([x_line[k] for k in line_blocks], "cut_x"), far_bit, n_dp)
    c_line[2] = send(c_line[0], 2)
    c_line.update({k | 2: send(c_line[k], 2) for k in folds})
    c_pair = {k: send(c_line[k], 1) for k in [0] + folds}
    pre, act, info, pick, combine, x_keep, x_give = pl.pallas_call(
        functools.partial(hidden_kernel, cfg),
        grid=(local,),
        in_specs=[smem] * 2 + [any_space] * parts + [weight_spec] * 2,
        out_specs=[by_expert(cap, 2 * hidden), by_expert(cap, hidden + LANES), by_expert(cap, LANES),
                   whole(local * cap, total), whole(total, local * cap_pad), whole(total, half), whole(line, half)],
        out_shape=[sds((local, cap, 2 * hidden), F32), sds((local, cap, hidden + LANES), BF16),
                   sds((local, cap, LANES), F32), sds((local * cap, total), BF16), sds((total, local * cap_pad), BF16),
                   sds((total, half), BF16), sds((line, half), BF16)],
        scratch_shapes=[
            pltpu.VMEM((total, wide), BF16),
            pltpu.VMEM((local * cap, wide), BF16),
            pltpu.SemaphoreType.DMA((parts,)),
        ],
        compiler_params=params,
        cost_estimate=cost(6, 20),
        name="hidden",
    )(first, far_word, *[x_line[k] for k in line_blocks], *[x_pair[k] for k in line_blocks], w_gate, w_up)
    act, c_line, c_pair, x_far = fence(act, c_line, c_pair, x_far)

    c_pair.update({k: send(c_line[k], 1) for k in [2] + sides})
    x_far_pair = swap(x_give, far_bit, n_dp)
    act_far = swap(act, far_bit, n_dp)
    level_rows = [line] + [len(group) * tok_rows for group in groups]
    level_specs = [whole(rows, width) for rows in level_rows]
    mixed_keep, *mixed_out, c_give = pl.pallas_call(
        functools.partial(mixed_kernel, (plan, levels, local, cap, cap_pad)),
        grid=(width // tile,),
        in_specs=[smem, whole(local, cap, hidden + LANES), whole(total, local * cap_pad), by_columns] + [any_space] * levels,
        out_specs=level_specs + [whole(line, half)],
        out_shape=[sds((rows, width), BF16) for rows in level_rows] + [sds((line, half), BF16)],
        scratch_shapes=[pltpu.VMEM((total, local * hidden), BF16), pltpu.SemaphoreType.DMA((levels,))],
        compiler_params=params,
        cost_estimate=cost(6, 10),
        name="mixed",
    )(far_word, act, combine, w_down, *[c_line[k] for k in line_blocks])
    c_pair, mixed_keep, mixed_out, c_give, x_far_pair = fence(c_pair, mixed_keep, mixed_out, c_give, x_far_pair)

    def back_rows(keep, got):
        return keep.astype(F32) + got.astype(F32)

    def pair_sums(keep, got, group):
        mine = jnp.concatenate([keep[k // 2 * tok_rows:(k // 2 + 1) * tok_rows] for k in group], axis=0)
        return back_rows(mine, got)

    def fold_upper(sums):
        blocks = {k: sums[i * tok_rows:(i + 1) * tok_rows] for i, k in enumerate(folds)}
        landed = []
        for bit in upper_bits:
            for k in [k for k in blocks if k & bit]:
                got = send(blocks.pop(k).astype(BF16), bit)
                if k == bit:
                    landed.append(got)
                else:
                    blocks[k ^ bit] = back_rows(blocks[k ^ bit], got)
        return landed

    def finish(sums, landed):
        return sum([part.astype(F32) for part in landed], sums[tok_rows:].astype(F32))

    mixed_got = [send(part, 1) for part in mixed_out[:2]]
    c_far = swap(c_give, far_bit, n_dp)
    d_gate, d_up, tail, c_keep, c_give = pl.pallas_call(
        functools.partial(grad_kernel, cfg),
        grid=(local,),
        in_specs=[smem] + [any_space] * parts + [whole(local * cap, total), whole(total, local * cap_pad), weight_spec,
                                                 by_expert(cap, 2 * hidden), by_expert(cap, LANES)],
        out_specs=[by_expert(cap, hidden)] * 2 + [whole(total, LANES), whole(total, half), whole(line, half)],
        out_shape=[sds((local, cap, hidden), BF16)] * 2 + [sds((total, LANES), BF16),
                   sds((total, half), BF16), sds((line, half), BF16)],
        scratch_shapes=[
            pltpu.VMEM((total, width), BF16),
            pltpu.VMEM((local * cap, width), BF16),
            pltpu.VMEM((local * cap_pad, LANES), BF16),
            pltpu.SemaphoreType.DMA((parts,)),
        ],
        compiler_params=params,
        cost_estimate=cost(6, 12),
        name="hidden_grads",
    )(far_word, *[c_line[k] for k in line_blocks], *[c_pair[k] for k in line_blocks], pick, combine, w_down, pre, info)
    mixed_sides, mixed_got, mixed_out, d_gate, d_up, tail, c_give, act_far = fence(
        pair_sums(mixed_keep, mixed_got[0], sides).astype(BF16), mixed_got, mixed_out, d_gate, d_up, tail, c_give, act_far)

    mixed_sides = send(mixed_sides, 2)
    mixed_got.append(send(mixed_out[2], 1))
    c_far_pair = swap(c_give, far_bit, n_dp)
    wide_specs = [whole(rows, wide) for rows in level_rows]
    input_keep, *input_out = pl.pallas_call(
        functools.partial(input_kernel, (plan, local, cap, cap_pad)),
        grid=(width // tile,),
        in_specs=[whole(local, cap, hidden)] * 2 + [whole(total, local * cap_pad), whole(total, LANES),
                                                    by_columns, by_columns],
        out_specs=wide_specs,
        out_shape=[sds((rows, wide), BF16) for rows in level_rows],
        scratch_shapes=[pltpu.VMEM((local * cap_pad, tile), BF16)],
        compiler_params=params,
        cost_estimate=cost(6, 16),
        name="input_grads",
    )(d_gate, d_up, combine, tail, w_gate, w_up)
    input_keep, input_out, mixed_sides, mixed_got, c_far, d_gate = fence(
        input_keep, input_out, mixed_sides, mixed_got, c_far, d_gate)

    input_got = [send(part, 1) for part in input_out[:2]]
    mixed_landed = fold_upper(back_rows(pair_sums(mixed_keep, mixed_got[1], folds), mixed_sides))
    gate_far = swap(d_gate, far_bit, n_dp)
    input_sides, input_out, c_far_pair, x_keep, d_up, mixed_got[2] = fence(
        pair_sums(input_keep, input_got[0], sides).astype(BF16), input_out, c_far_pair, x_keep, d_up, mixed_got[2])
    input_sides = send(input_sides, 2)
    input_got.append(send(input_out[2], 1))
    up_far = swap(d_up, far_bit, n_dp)
    mixed_ends = pair_sums(mixed_keep, mixed_got[2], [2, 0])
    partial_specs = [by_expert(columns, hidden)] * 2
    partial_shapes = [sds((local, columns, hidden), BF16)] * 2
    x_rows, down_keep, down_give = pl.pallas_call(
        functools.partial(down_kernel, cap),
        grid=(local,),
        in_specs=[smem, pl.BlockSpec((cap, total), lambda e: (e, 0))] + [whole(total, half), whole(line, half), whole(line, half)] * 2
        + [by_expert(cap, hidden + LANES)] * 2,
        out_specs=[by_expert(2 * cap, half)] + partial_specs,
        out_shape=[sds((local, 2 * cap, half), BF16)] + partial_shapes,
        scratch_shapes=[pltpu.VMEM((2 * cap, half), BF16), pltpu.VMEM((2 * cap, hidden), BF16), pltpu.VMEM((half, hidden), BF16)],
        compiler_params=params,
        cost_estimate=cost(6, 12),
        name="down_grads",
    )(near_word, pick, x_keep, x_far, x_far_pair, c_keep, c_far, c_far_pair, act, act_far)
    input_folds, mixed_landed, x_rows, down_keep, down_give = fence(
        back_rows(pair_sums(input_keep, input_got[1], folds), input_sides).astype(BF16),
        mixed_landed, x_rows, down_keep, down_give)

    input_landed = fold_upper(input_folds)
    mixed_landed.append(send(mixed_ends[:tok_rows].astype(BF16), 2))
    input_ends = pair_sums(input_keep, input_got[2], [2, 0])
    input_landed.append(send(input_ends[:tok_rows].astype(BF16), 2))
    down_got = swap(down_give, 1, n_dp)
    mixed = finish(mixed_ends, mixed_landed).astype(BF16)
    mixed, input_ends, input_landed, gate_far, up_far = fence(mixed, input_ends, input_landed, gate_far, up_far)
    both_specs = [by_expert(columns, 2 * hidden)] * 2
    both_keep, both_give = pl.pallas_call(
        functools.partial(both_kernel, cap),
        grid=(local,),
        in_specs=[smem, by_expert(2 * cap, half)] + [by_expert(cap, hidden)] * 4,
        out_specs=both_specs,
        out_shape=[sds((local, columns, 2 * hidden), BF16)] * 2,
        scratch_shapes=[pltpu.VMEM((2 * cap, 2 * hidden), BF16), pltpu.VMEM((half, 2 * hidden), BF16)],
        compiler_params=params,
        cost_estimate=cost(3, 10),
        name="gate_up_grads",
    )(near_word, x_rows, d_gate, gate_far, d_up, up_far)
    both_got = swap(both_give, 1, n_dp)
    down_grad = back_rows(down_keep, down_got).astype(BF16)
    gate_grad = back_rows(both_keep[:, :, :hidden], both_got[:, :, :hidden]).astype(BF16)
    up_grad = back_rows(both_keep[:, :, hidden:], both_got[:, :, hidden:]).astype(BF16)

    back = finish(input_ends, input_landed)
    token_grad = back[:, :width].astype(BF16)
    tail = back[:, width:]
    slot_sg = tail[:, :top] + tail[:, top:2 * top] + tail[:, 2 * top:3 * top]
    prob_grad = (slot_sg - jnp.sum(share * slot_sg, axis=1, keepdims=True)) / totals
    return mixed, token_grad, prob_grad, gate_grad, up_grad, down_grad


def solution(mesh):
    rows = P(("expert", "dp"), None)
    weight = P("expert", None, None)
    grad = P("expert", "dp", None)
    return jax.shard_map(
        shards,
        mesh=mesh,
        in_specs=(rows, rows, rows, rows, weight, weight, weight),
        out_specs=(rows, rows, rows, grad, grad, grad),
        check_vma=False,
    )
```

```python
import functools

import jax
import jax.numpy as jnp
from jax import lax
from jax.experimental import pallas as pl
from jax.experimental.pallas import tpu as pltpu
from jax.sharding import PartitionSpec as P


F32 = jnp.float32
BF16 = jnp.bfloat16
LANES = 128
VMEM_LIMIT = 60 * 1024 * 1024


def round_up(value, unit):
    return -(-value // unit) * unit


def dot(a, b):
    return jnp.dot(a, b, preferred_element_type=F32)


def dot_nt(a, b):
    return lax.dot_general(a, b, (((1,), (1,)), ((), ())), preferred_element_type=F32)


def dot_tn(a, b):
    return lax.dot_general(a, b, (((0,), (0,)), ((), ())), preferred_element_type=F32)


def iota(shape, dim):
    return lax.broadcasted_iota(jnp.int32, shape, dim)


def load_blocks(blocks, held, sems):
    copies, start = [], 0
    for i, block in enumerate(blocks):
        size = block.shape[0]
        copies.append(pltpu.make_async_copy(block, held.at[pl.ds(start, size), :], sems.at[i]))
        start += size
    for copy in copies:
        copy.start()
    for copy in copies:
        copy.wait()


def tiles(width, tile=512):
    return [(start, min(start + tile, width)) for start in range(0, width, tile)]


def half_of(which, width):
    return pl.ds(pl.multiple_of(which * (width // 2), LANES), width // 2)


def hidden_kernel(cfg, first_ref, far_ref, *refs):
    parts, local, cap, cap_pad, top = cfg
    blocks, refs = refs[:parts], refs[parts:]
    gate_ref, up_ref, pre_ref, act_ref, info_ref, pick_ref, combine_ref, keep_ref, give_ref = refs[:9]
    held, rows_ref, sems = refs[9:]
    expert = pl.program_id(0)
    tokens = held.shape[0]
    width, hidden = gate_ref.shape[1:]

    @pl.when(expert == 0)
    def _():
        load_blocks(blocks, held, sems)
        meta = held[:, width:].astype(F32).astype(jnp.int32)
        lane = iota(meta.shape, 1)
        hits = jnp.zeros(meta.shape, F32)
        for i in range(local):
            named = (meta == first_ref[0] + i) & (lane < top)
            hit = jnp.sum(jnp.where(named, 1.0, 0.0), axis=1, keepdims=True)
            hits = hits + jnp.where(lane == i, hit, 0.0)
        step = min(tokens, 256)
        below = (iota((step, step), 0) >= iota((step, step), 1)).astype(F32).astype(BF16)
        carry = jnp.zeros((1, LANES), F32)
        slots = []
        for start in range(0, tokens, step):
            part = hits[start:start + step]
            rank = dot(below, part.astype(BF16)) + carry
            carry = rank[step - 1:step]
            slots.append(jnp.where(part > 0.0, rank - 1.0, -1.0))
        slots = jnp.concatenate(slots, axis=0)
        slots_t = jnp.transpose(slots)
        places = iota((tokens, cap_pad), 1).astype(F32)
        places_t = iota((cap, tokens), 0).astype(F32)
        for i in range(local):
            hit = slots[:, i:i + 1] == places
            combine_ref[:, i * cap_pad:(i + 1) * cap_pad] = jnp.where(hit, 1.0, 0.0).astype(BF16)
            hit = slots_t[i:i + 1, :] == places_t
            pick_ref[i * cap:(i + 1) * cap, :] = jnp.where(hit, 1.0, 0.0).astype(BF16)
        for start, stop in tiles(held.shape[1]):
            rows_ref[:, start:stop] = dot(pick_ref[...], held[:, start:stop]).astype(BF16)
        keep_ref[...] = held[:, half_of(far_ref[0], width)]
        give_ref[...] = held[give_ref.shape[0]:, half_of(1 - far_ref[0], width)]

    here = pl.ds(pl.multiple_of(expert * cap, 16), cap)
    pick = pick_ref[here, :].astype(F32)
    token = jnp.sum(pick * iota(pick.shape, 1).astype(F32), axis=1, keepdims=True)
    token = jnp.where(jnp.sum(pick, axis=1, keepdims=True) > 0.0, token, -128.0).astype(jnp.int32)
    meta = rows_ref[here, width:].astype(F32)
    lane = iota(meta.shape, 1)
    named = (meta.astype(jnp.int32) == first_ref[0] + expert) & (lane < top)
    shares = sum(pltpu.roll(meta, LANES - top * (i + 1), 1) for i in range(3))
    share = jnp.sum(jnp.where(named, shares, 0.0), axis=1, keepdims=True)
    info_ref[0] = jnp.where(lane < top, jnp.where(named, 1.0, 0.0), share)

    rows = rows_ref[here, :width]
    gate_pre = dot(rows, gate_ref[0])
    up_pre = dot(rows, up_ref[0])
    pre_ref[0, :, :hidden] = gate_pre
    pre_ref[0, :, hidden:] = up_pre
    active = gate_pre * jax.nn.sigmoid(gate_pre) * up_pre
    act_ref[0, :, :hidden] = (share * active).astype(BF16)
    token_pair = jnp.where(lane == 0, token >> 7, jnp.where(lane == 1, token & 127, 0))
    act_ref[0, :, hidden:] = token_pair.astype(F32).astype(BF16)


def store_parts(plan, value, here, refs):
    refs[0][:, here] = value[:refs[0].shape[0]]
    line, size = refs[0].shape[0], refs[0].shape[0] // sum(len(items) for items in plan)
    for ref, items in zip(refs[1:], plan):
        for i, block in enumerate(items):
            start = line + block * size
            ref[i * size:(i + 1) * size, here] = value[start:start + size]


def mixed_kernel(cfg, far_ref, act_ref, combine_ref, down_ref, *refs):
    plan, levels, local, cap, cap_pad = cfg
    blocks, refs = refs[:levels], refs[levels:]
    outs, give_ref, spread, sems = refs[:-3], refs[-3], refs[-2], refs[-1]
    size = blocks[0].shape[0]
    here = half_of(1 - far_ref[0], blocks[0].shape[1])
    copies = [pltpu.make_async_copy(block.at[:, here], give_ref.at[pl.ds(i * size, size), :], sems.at[i])
              for i, block in enumerate(blocks)]
    hidden = down_ref.shape[2]
    tile = down_ref.shape[1]
    step = pl.program_id(0)

    @pl.when(step == 0)
    def _():
        for copy in copies:
            copy.start()
        for e in range(local):
            here = combine_ref[:, e * cap_pad:e * cap_pad + cap]
            spread[:, e * hidden:(e + 1) * hidden] = dot(here, act_ref[e, :, :hidden]).astype(BF16)

    total = dot_nt(spread[:, :hidden], down_ref[0])
    for e in range(1, local):
        total = total + dot_nt(spread[:, e * hidden:(e + 1) * hidden], down_ref[e])
    store_parts(plan, total.astype(BF16), pl.ds(pl.multiple_of(step * tile, tile), tile), outs)

    @pl.when(step == pl.num_programs(0) - 1)
    def _():
        for copy in copies:
            copy.wait()


def grad_kernel(cfg, far_ref, *refs):
    parts, local, cap, cap_pad, top = cfg
    blocks, refs = refs[:parts], refs[parts:]
    pick_ref, combine_ref, down_ref, pre_ref, info_ref, d_gate_ref, d_up_ref, tail_ref, keep_ref, give_ref = refs[:10]
    held, rows_ref, tails, sems = refs[10:]
    expert = pl.program_id(0)
    hidden = down_ref.shape[2]

    @pl.when(expert == 0)
    def _():
        load_blocks(blocks, held, sems)
        tails[...] = jnp.zeros(tails.shape, BF16)
        for start, stop in tiles(held.shape[1]):
            rows_ref[:, start:stop] = dot(pick_ref[...], held[:, start:stop]).astype(BF16)
        width = held.shape[1]
        keep_ref[...] = held[:, half_of(far_ref[0], width)]
        give_ref[...] = held[give_ref.shape[0]:, half_of(1 - far_ref[0], width)]

    info = info_ref[0]
    lane = iota(info.shape, 1)
    share = info[:, top:top + 1]
    gate_pre, up_pre = pre_ref[0, :, :hidden], pre_ref[0, :, hidden:]
    sig = jax.nn.sigmoid(gate_pre)
    silu = gate_pre * sig
    d_raw = dot(rows_ref[pl.ds(pl.multiple_of(expert * cap, 16), cap), :], down_ref[0])
    share_grad = jnp.sum(silu * up_pre * d_raw, axis=1, keepdims=True)
    d_active = share * d_raw
    d_gate_ref[0] = (d_active * up_pre * sig * (1.0 + gate_pre * (1.0 - sig))).astype(BF16)
    d_up_ref[0] = (d_active * silu).astype(BF16)
    placed = jnp.where((lane < top) & (info > 0.0), share_grad, 0.0)
    high = placed.astype(BF16)
    rest = placed - high.astype(F32)
    middle = rest.astype(BF16)
    low = (rest - middle.astype(F32)).astype(BF16)
    tail = high.astype(F32) + pltpu.roll(middle.astype(F32), top, 1) + pltpu.roll(low.astype(F32), 2 * top, 1)
    tails[pl.ds(pl.multiple_of(expert * cap_pad, cap_pad), cap), :] = tail.astype(BF16)

    @pl.when(expert == local - 1)
    def _():
        tail_ref[...] = dot(combine_ref[...], tails[...]).astype(BF16)


def input_kernel(cfg, d_gate_ref, d_up_ref, combine_ref, tail_ref, gate_ref, up_ref, *refs):
    plan, local, cap, cap_pad = cfg
    outs, rows = refs[:-1], refs[-1]
    tile, hidden = gate_ref.shape[1:]
    step = pl.program_id(0)

    @pl.when(step == 0)
    def _():
        rows[...] = jnp.zeros(rows.shape, BF16)
        width = outs[0].shape[1] - LANES
        store_parts(plan, tail_ref[...], slice(width, width + LANES), outs)

    for e in range(local):
        part = dot_nt(d_gate_ref[e], gate_ref[e]) + dot_nt(d_up_ref[e], up_ref[e])
        rows[e * cap_pad:e * cap_pad + cap, :] = part.astype(BF16)
    total = dot(combine_ref[...], rows[...]).astype(BF16)
    store_parts(plan, total, pl.ds(pl.multiple_of(step * tile, tile), tile), outs)


def store_halves(part, near_ref, both, keep_ref, give_ref):
    both[...] = part.astype(BF16)
    size = keep_ref.shape[1]
    keep_ref[0] = both[pl.ds(pl.multiple_of(near_ref[0] * size, 16), size), :]
    give_ref[0] = both[pl.ds(pl.multiple_of((1 - near_ref[0]) * size, 16), size), :]


def down_kernel(cap, near_ref, pick_ref, *refs):
    x_refs, c_refs, (act_ref, act_far_ref, rows_ref, keep_ref, give_ref, c_rows, acts, both) = refs[:3], refs[3:6], refs[6:]
    hidden = acts.shape[1]
    line = x_refs[1].shape[0]
    acts[:cap, :] = act_ref[0, :, :hidden]
    acts[cap:, :] = act_far_ref[0, :, :hidden]
    pair = act_far_ref[0, :, hidden:].astype(F32)
    token = pair[:, 0:1] * 128.0 + pair[:, 1:2]
    pick = pick_ref[...]
    pick_far = jnp.where(token == iota(pick.shape, 1).astype(F32), 1.0, 0.0).astype(BF16)
    for (own, far, far_pair), rows in ((x_refs, rows_ref.at[0]), (c_refs, c_rows)):
        rows[:cap, :] = dot(pick, own[...]).astype(BF16)
        rows[cap:, :] = (dot(pick_far[:, :line], far[...]) + dot(pick_far[:, line:], far_pair[...])).astype(BF16)
    store_halves(dot_tn(c_rows[...], acts[...]), near_ref, both, keep_ref, give_ref)


def both_kernel(cap, near_ref, rows_ref, d_gate_ref, gate_far_ref, d_up_ref, up_far_ref, keep_ref, give_ref, grads, both):
    hidden = d_gate_ref.shape[2]
    grads[:cap, :hidden] = d_gate_ref[0]
    grads[cap:, :hidden] = gate_far_ref[0]
    grads[:cap, hidden:] = d_up_ref[0]
    grads[cap:, hidden:] = up_far_ref[0]
    store_halves(dot_tn(rows_ref[0], grads[...]), near_ref, both, keep_ref, give_ref)


def cut_kernel(half, plan, word_ref, *refs):
    count = 1 + max(i for i, _, _, _ in plan)
    blocks, outs, sems = refs[:count], refs[count:-1], refs[-1]
    copies = []
    for i, flip, out, row in plan:
        which = 1 - word_ref[0] if flip else word_ref[0]
        here = pl.ds(pl.multiple_of(which * half, LANES), half)
        there = outs[out].at[pl.ds(row, blocks[i].shape[0]), :]
        copies.append(pltpu.make_async_copy(blocks[i].at[:, here], there, sems.at[len(copies)]))
    for copy in copies:
        copy.start()
    for copy in copies:
        copy.wait()


def swap(value, bit, count):
    return lax.ppermute(value, "dp", [(i, i ^ bit) for i in range(count)])


def exchange(value, bit, count):
    return lax.ppermute(value, "expert", [(i, i ^ bit) for i in range(count)])


def fence(*values):
    leaves, tree = jax.tree.flatten(values)
    return jax.tree.unflatten(tree, lax.optimization_barrier(tuple(leaves)))


def split3(value):
    high = lax.reduce_precision(value, 8, 7)
    rest = value - high
    middle = lax.reduce_precision(rest, 8, 7)
    return [high.astype(BF16), middle.astype(BF16), (rest - middle).astype(BF16)]


def shards(tokens, routes, probs, cotangent, w_gate, w_up, w_down):
    tok_rows, top = routes.shape
    local, width, hidden = w_gate.shape
    n_exp = lax.axis_size("expert")
    n_dp = lax.axis_size("dp")
    experts = local * n_exp
    cap = 5 * tok_rows * top // (4 * experts) * n_exp
    cap_pad = round_up(cap, LANES)
    total = n_exp * tok_rows
    levels = n_exp // 2
    line = levels * tok_rows
    wide = width + LANES
    tile = min(width, 512)
    columns = width // n_dp
    half = width // 2
    far_bit = n_dp // 2
    my_dp = lax.axis_index("dp")
    far = jnp.where((my_dp & far_bit) > 0, 1, 0)
    near = jnp.where((my_dp & 1) > 0, 1, 0)
    near_word = near.astype(jnp.int32).reshape(1)
    far_word = far.astype(jnp.int32).reshape(1)
    first = (lax.axis_index("expert") * local).astype(jnp.int32).reshape(1)
    line_blocks = list(range(0, n_exp, 2))
    sides = [k for k in line_blocks if k & 2 and k > 2]
    folds = [k ^ 2 for k in sides]
    groups = [sides, folds, [2, 0]]
    plan = [[k // 2 for k in group] for group in groups]
    upper_bits = [1 << i for i in range(2, n_exp.bit_length() - 1)]

    def send(value, bit):
        return exchange(value, bit, n_exp)

    def gather_upper(value):
        blocks = {0: value}
        for bit in reversed(upper_bits):
            blocks.update({k | bit: send(block, bit) for k, block in list(blocks.items())})
        return blocks

    any_space = pl.BlockSpec(memory_space=pl.ANY)
    smem = pl.BlockSpec(memory_space=pltpu.SMEM)
    params = pltpu.CompilerParams(dimension_semantics=("arbitrary",), vmem_limit_bytes=VMEM_LIMIT)

    def by_expert(*shape):
        return pl.BlockSpec((1,) + shape, lambda e: (e,) + (0,) * len(shape))

    def whole(*shape):
        return pl.BlockSpec(shape, lambda e: (0,) * len(shape))

    def sds(shape, dtype):
        return jax.ShapeDtypeStruct(shape, dtype)

    def cost(gflop, mbyte):
        return pl.CostEstimate(flops=gflop * 10**6, bytes_accessed=mbyte * 10**3, transcendentals=0)

    def cut_blocks(word, blocks, size, wanted, name):
        plan, rows = [], []
        for out, items in enumerate(wanted):
            rows.append(0)
            for i, flip in items:
                plan.append((i, flip, out, rows[out]))
                rows[out] += blocks[i].shape[0]
        return pl.pallas_call(
            functools.partial(cut_kernel, size, plan),
            in_specs=[smem] + [any_space] * len(blocks),
            out_specs=[pl.BlockSpec(memory_space=pltpu.VMEM)] * len(wanted),
            out_shape=[sds((n, size), BF16) for n in rows],
            scratch_shapes=[pltpu.SemaphoreType.DMA((len(plan),))],
            compiler_params=pltpu.CompilerParams(vmem_limit_bytes=VMEM_LIMIT),
            cost_estimate=cost(0, 2),
            name=name,
        )(word, *blocks)

    def cut_far(blocks, name):
        return cut_blocks(far_word, blocks, width // 2, [[(i, 1) for i in range(len(blocks))]], name)[0]

    by_columns = pl.BlockSpec((local, tile, hidden), lambda j: (0, j, 0))
    weight_spec = by_expert(width, hidden)
    parts = n_exp
    cfg = (parts, local, cap, cap_pad, top)

    totals = jnp.sum(probs, axis=1, keepdims=True)
    share = probs / totals
    meta = jnp.concatenate([routes.astype(BF16)] + split3(share), axis=1)
    meta = jnp.pad(meta, ((0, 0), (0, LANES - 4 * top)))

    x_own = jnp.concatenate([tokens, meta], axis=1)
    x_line = gather_upper(x_own)
    x_line[2] = send(x_own, 2)
    x_pair = {k: send(x_line[k], 1) for k in (0, 2)}
    x_line, x_pair[0], cot = fence(x_line, x_pair[0], cotangent)

    x_line.update({k | 2: send(x_line[k], 2) for k in folds})
    c_line = gather_upper(cot)
    x_pair.update({k: send(x_line[k], 1) for k in folds})
    x_line, c_line, x_pair = fence(x_line, c_line, x_pair)
    x_pair.update({k: send(x_line[k], 1) for k in sides})
    x_far = swap(cut_far([x_line[k] for k in line_blocks], "cut_x"), far_bit, n_dp)
    c_line[2] = send(c_line[0], 2)
    c_line.update({k | 2: send(c_line[k], 2) for k in folds})
    c_pair = {k: send(c_line[k], 1) for k in [0] + folds}
    pre, act, info, pick, combine, x_keep, x_give = pl.pallas_call(
        functools.partial(hidden_kernel, cfg),
        grid=(local,),
        in_specs=[smem] * 2 + [any_space] * parts + [weight_spec] * 2,
        out_specs=[by_expert(cap, 2 * hidden), by_expert(cap, hidden + LANES), by_expert(cap, LANES),
                   whole(local * cap, total), whole(total, local * cap_pad), whole(total, half), whole(line, half)],
        out_shape=[sds((local, cap, 2 * hidden), F32), sds((local, cap, hidden + LANES), BF16),
                   sds((local, cap, LANES), F32), sds((local * cap, total), BF16), sds((total, local * cap_pad), BF16),
                   sds((total, half), BF16), sds((line, half), BF16)],
        scratch_shapes=[
            pltpu.VMEM((total, wide), BF16),
            pltpu.VMEM((local * cap, wide), BF16),
            pltpu.SemaphoreType.DMA((parts,)),
        ],
        compiler_params=params,
        cost_estimate=cost(6, 20),
        name="hidden",
    )(first, far_word, *[x_line[k] for k in line_blocks], *[x_pair[k] for k in line_blocks], w_gate, w_up)
    act, c_line, c_pair, x_far = fence(act, c_line, c_pair, x_far)

    c_pair.update({k: send(c_line[k], 1) for k in [2] + sides})
    act_far = swap(act, far_bit, n_dp)
    level_rows = [line] + [len(group) * tok_rows for group in groups]
    level_specs = [whole(rows, width) for rows in level_rows]
    mixed_keep, *mixed_out, c_give = pl.pallas_call(
        functools.partial(mixed_kernel, (plan, levels, local, cap, cap_pad)),
        grid=(width // tile,),
        in_specs=[smem, whole(local, cap, hidden + LANES), whole(total, local * cap_pad), by_columns] + [any_space] * levels,
        out_specs=level_specs + [whole(line, half)],
        out_shape=[sds((rows, width), BF16) for rows in level_rows] + [sds((line, half), BF16)],
        scratch_shapes=[pltpu.VMEM((total, local * hidden), BF16), pltpu.SemaphoreType.DMA((levels,))],
        compiler_params=params,
        cost_estimate=cost(6, 10),
        name="mixed",
    )(far_word, act, combine, w_down, *[c_line[k] for k in line_blocks])
    c_pair, mixed_keep, mixed_out, c_give, act_far = fence(c_pair, mixed_keep, mixed_out, c_give, act_far)

    def back_rows(keep, got):
        return keep.astype(F32) + got.astype(F32)

    def pair_sums(keep, got, group):
        mine = jnp.concatenate([keep[k // 2 * tok_rows:(k // 2 + 1) * tok_rows] for k in group], axis=0)
        return back_rows(mine, got)

    def fold_upper(sums):
        blocks = {k: sums[i * tok_rows:(i + 1) * tok_rows] for i, k in enumerate(folds)}
        landed = []
        for bit in upper_bits:
            for k in [k for k in blocks if k & bit]:
                got = send(blocks.pop(k).astype(BF16), bit)
                if k == bit:
                    landed.append(got)
                else:
                    blocks[k ^ bit] = back_rows(blocks[k ^ bit], got)
        return landed

    def finish(sums, landed):
        return sum([part.astype(F32) for part in landed], sums[tok_rows:].astype(F32))

    mixed_got = [send(part, 1) for part in mixed_out[:2]]
    c_far = swap(c_give, far_bit, n_dp)
    d_gate, d_up, tail, c_keep, c_give = pl.pallas_call(
        functools.partial(grad_kernel, cfg),
        grid=(local,),
        in_specs=[smem] + [any_space] * parts + [whole(local * cap, total), whole(total, local * cap_pad), weight_spec,
                                                 by_expert(cap, 2 * hidden), by_expert(cap, LANES)],
        out_specs=[by_expert(cap, hidden)] * 2 + [whole(total, LANES), whole(total, half), whole(line, half)],
        out_shape=[sds((local, cap, hidden), BF16)] * 2 + [sds((total, LANES), BF16),
                   sds((total, half), BF16), sds((line, half), BF16)],
        scratch_shapes=[
            pltpu.VMEM((total, width), BF16),
            pltpu.VMEM((local * cap, width), BF16),
            pltpu.VMEM((local * cap_pad, LANES), BF16),
            pltpu.SemaphoreType.DMA((parts,)),
        ],
        compiler_params=params,
        cost_estimate=cost(6, 12),
        name="hidden_grads",
    )(far_word, *[c_line[k] for k in line_blocks], *[c_pair[k] for k in line_blocks], pick, combine, w_down, pre, info)
    mixed_sides, mixed_got, mixed_out, d_gate, d_up, tail, c_give, c_far = fence(
        pair_sums(mixed_keep, mixed_got[0], sides).astype(BF16), mixed_got, mixed_out, d_gate, d_up, tail, c_give, c_far)

    mixed_sides = send(mixed_sides, 2)
    mixed_got.append(send(mixed_out[2], 1))
    c_far_pair = swap(c_give, far_bit, n_dp)
    wide_specs = [whole(rows, wide) for rows in level_rows]
    input_keep, *input_out = pl.pallas_call(
        functools.partial(input_kernel, (plan, local, cap, cap_pad)),
        grid=(width // tile,),
        in_specs=[whole(local, cap, hidden)] * 2 + [whole(total, local * cap_pad), whole(total, LANES),
                                                    by_columns, by_columns],
        out_specs=wide_specs,
        out_shape=[sds((rows, wide), BF16) for rows in level_rows],
        scratch_shapes=[pltpu.VMEM((local * cap_pad, tile), BF16)],
        compiler_params=params,
        cost_estimate=cost(6, 16),
        name="input_grads",
    )(d_gate, d_up, combine, tail, w_gate, w_up)
    input_keep, input_out, mixed_sides, mixed_got, c_far_pair, d_gate, x_give = fence(
        input_keep, input_out, mixed_sides, mixed_got, c_far_pair, d_gate, x_give)
    x_far_pair = swap(x_give, far_bit, n_dp)

    input_got = [send(part, 1) for part in input_out[:2]]
    mixed_landed = fold_upper(back_rows(pair_sums(mixed_keep, mixed_got[1], folds), mixed_sides))
    gate_far = swap(d_gate, far_bit, n_dp)
    input_sides, input_out, x_far_pair, x_keep, d_up = fence(
        pair_sums(input_keep, input_got[0], sides).astype(BF16), input_out, x_far_pair, x_keep, d_up)
    input_sides = send(input_sides, 2)
    input_got.append(send(input_out[2], 1))
    up_far = swap(d_up, far_bit, n_dp)
    partial_specs = [by_expert(columns, hidden)] * 2
    partial_shapes = [sds((local, columns, hidden), BF16)] * 2
    x_rows, down_keep, down_give = pl.pallas_call(
        functools.partial(down_kernel, cap),
        grid=(local,),
        in_specs=[smem, pl.BlockSpec((cap, total), lambda e: (e, 0))] + [whole(total, half), whole(line, half), whole(line, half)] * 2
        + [by_expert(cap, hidden + LANES)] * 2,
        out_specs=[by_expert(2 * cap, half)] + partial_specs,
        out_shape=[sds((local, 2 * cap, half), BF16)] + partial_shapes,
        scratch_shapes=[pltpu.VMEM((2 * cap, half), BF16), pltpu.VMEM((2 * cap, hidden), BF16), pltpu.VMEM((half, hidden), BF16)],
        compiler_params=params,
        cost_estimate=cost(6, 12),
        name="down_grads",
    )(near_word, pick, x_keep, x_far, x_far_pair, c_keep, c_far, c_far_pair, act, act_far)
    input_folds, mixed_landed, x_rows, down_keep, down_give = fence(
        back_rows(pair_sums(input_keep, input_got[1], folds), input_sides).astype(BF16),
        mixed_landed, x_rows, down_keep, down_give)

    input_landed = fold_upper(input_folds)
    input_ends = pair_sums(input_keep, input_got[2], [2, 0])
    input_landed.append(send(input_ends[:tok_rows].astype(BF16), 2))
    down_got = swap(down_give, 1, n_dp)
    input_ends, mixed_got[2], gate_far, up_far, down_got = fence(input_ends, mixed_got[2], gate_far, up_far, down_got)
    mixed_ends = pair_sums(mixed_keep, mixed_got[2], [2, 0])
    mixed_landed.append(send(mixed_ends[:tok_rows].astype(BF16), 2))
    mixed = finish(mixed_ends, mixed_landed).astype(BF16)
    both_specs = [by_expert(columns, 2 * hidden)] * 2
    both_keep, both_give = pl.pallas_call(
        functools.partial(both_kernel, cap),
        grid=(local,),
        in_specs=[smem, by_expert(2 * cap, half)] + [by_expert(cap, hidden)] * 4,
        out_specs=both_specs,
        out_shape=[sds((local, columns, 2 * hidden), BF16)] * 2,
        scratch_shapes=[pltpu.VMEM((2 * cap, 2 * hidden), BF16), pltpu.VMEM((half, 2 * hidden), BF16)],
        compiler_params=params,
        cost_estimate=cost(3, 10),
        name="gate_up_grads",
    )(near_word, x_rows, d_gate, gate_far, d_up, up_far)
    both_give, input_landed = fence(both_give, input_landed)
    both_got = swap(both_give, 1, n_dp)
    down_grad = back_rows(down_keep, down_got).astype(BF16)
    gate_grad = back_rows(both_keep[:, :, :hidden], both_got[:, :, :hidden]).astype(BF16)
    up_grad = back_rows(both_keep[:, :, hidden:], both_got[:, :, hidden:]).astype(BF16)

    back = finish(input_ends, input_landed)
    token_grad = back[:, :width].astype(BF16)
    tail = back[:, width:]
    slot_sg = tail[:, :top] + tail[:, top:2 * top] + tail[:, 2 * top:3 * top]
    prob_grad = (slot_sg - jnp.sum(share * slot_sg, axis=1, keepdims=True)) / totals
    return mixed, token_grad, prob_grad, gate_grad, up_grad, down_grad


def solution(mesh):
    rows = P(("expert", "dp"), None)
    weight = P("expert", None, None)
    grad = P("expert", "dp", None)
    return jax.shard_map(
        shards,
        mesh=mesh,
        in_specs=(rows, rows, rows, rows, weight, weight, weight),
        out_specs=(rows, rows, rows, grad, grad, grad),
        check_vma=False,
    )
```

```python
import functools

import jax
import jax.numpy as jnp
from jax import lax
from jax.experimental import pallas as pl
from jax.experimental.pallas import tpu as pltpu
from jax.sharding import PartitionSpec as P


F32 = jnp.float32
BF16 = jnp.bfloat16
LANES = 128
VMEM_LIMIT = 60 * 1024 * 1024


def round_up(value, unit):
    return -(-value // unit) * unit


def dot(a, b):
    return jnp.dot(a, b, preferred_element_type=F32)


def dot_nt(a, b):
    return lax.dot_general(a, b, (((1,), (1,)), ((), ())), preferred_element_type=F32)


def dot_tn(a, b):
    return lax.dot_general(a, b, (((0,), (0,)), ((), ())), preferred_element_type=F32)


def iota(shape, dim):
    return lax.broadcasted_iota(jnp.int32, shape, dim)


def load_blocks(blocks, held, sems):
    copies, start = [], 0
    for i, block in enumerate(blocks):
        size = block.shape[0]
        copies.append(pltpu.make_async_copy(block, held.at[pl.ds(start, size), :], sems.at[i]))
        start += size
    for copy in copies:
        copy.start()
    for copy in copies:
        copy.wait()


def tiles(width, tile=512):
    return [(start, min(start + tile, width)) for start in range(0, width, tile)]


def half_of(which, width):
    return pl.ds(pl.multiple_of(which * (width // 2), LANES), width // 2)


def hidden_kernel(cfg, first_ref, far_ref, *refs):
    parts, local, cap, cap_pad, top = cfg
    blocks, refs = refs[:parts], refs[parts:]
    gate_ref, up_ref, pre_ref, act_ref, info_ref, pick_ref, combine_ref, keep_ref, give_ref = refs[:9]
    held, rows_ref, sems = refs[9:]
    expert = pl.program_id(0)
    tokens = held.shape[0]
    width, hidden = gate_ref.shape[1:]

    @pl.when(expert == 0)
    def _():
        load_blocks(blocks, held, sems)
        meta = held[:, width:].astype(F32).astype(jnp.int32)
        lane = iota(meta.shape, 1)
        hits = jnp.zeros(meta.shape, F32)
        for i in range(local):
            named = (meta == first_ref[0] + i) & (lane < top)
            hit = jnp.sum(jnp.where(named, 1.0, 0.0), axis=1, keepdims=True)
            hits = hits + jnp.where(lane == i, hit, 0.0)
        step = min(tokens, 256)
        below = (iota((step, step), 0) >= iota((step, step), 1)).astype(F32).astype(BF16)
        carry = jnp.zeros((1, LANES), F32)
        slots = []
        for start in range(0, tokens, step):
            part = hits[start:start + step]
            rank = dot(below, part.astype(BF16)) + carry
            carry = rank[step - 1:step]
            slots.append(jnp.where(part > 0.0, rank - 1.0, -1.0))
        slots = jnp.concatenate(slots, axis=0)
        slots_t = jnp.transpose(slots)
        places = iota((tokens, cap_pad), 1).astype(F32)
        places_t = iota((cap, tokens), 0).astype(F32)
        for i in range(local):
            hit = slots[:, i:i + 1] == places
            combine_ref[:, i * cap_pad:(i + 1) * cap_pad] = jnp.where(hit, 1.0, 0.0).astype(BF16)
            hit = slots_t[i:i + 1, :] == places_t
            pick_ref[i * cap:(i + 1) * cap, :] = jnp.where(hit, 1.0, 0.0).astype(BF16)
        for start, stop in tiles(held.shape[1]):
            rows_ref[:, start:stop] = dot(pick_ref[...], held[:, start:stop]).astype(BF16)
        keep_ref[...] = held[:, half_of(far_ref[0], width)]
        give_ref[...] = held[give_ref.shape[0]:, half_of(1 - far_ref[0], width)]

    here = pl.ds(pl.multiple_of(expert * cap, 16), cap)
    pick = pick_ref[here, :].astype(F32)
    token = jnp.sum(pick * iota(pick.shape, 1).astype(F32), axis=1, keepdims=True)
    token = jnp.where(jnp.sum(pick, axis=1, keepdims=True) > 0.0, token, -128.0).astype(jnp.int32)
    meta = rows_ref[here, width:].astype(F32)
    lane = iota(meta.shape, 1)
    named = (meta.astype(jnp.int32) == first_ref[0] + expert) & (lane < top)
    shares = sum(pltpu.roll(meta, LANES - top * (i + 1), 1) for i in range(3))
    share = jnp.sum(jnp.where(named, shares, 0.0), axis=1, keepdims=True)
    info_ref[0] = jnp.where(lane < top, jnp.where(named, 1.0, 0.0), share)

    rows = rows_ref[here, :width]
    gate_pre = dot(rows, gate_ref[0])
    up_pre = dot(rows, up_ref[0])
    pre_ref[0, :, :hidden] = gate_pre
    pre_ref[0, :, hidden:] = up_pre
    active = gate_pre * jax.nn.sigmoid(gate_pre) * up_pre
    act_ref[0, :, :hidden] = (share * active).astype(BF16)
    token_pair = jnp.where(lane == 0, token >> 7, jnp.where(lane == 1, token & 127, 0))
    act_ref[0, :, hidden:] = token_pair.astype(F32).astype(BF16)


def store_parts(plan, value, here, refs):
    refs[0][:, here] = value[:refs[0].shape[0]]
    line, size = refs[0].shape[0], refs[0].shape[0] // sum(len(items) for items in plan)
    for ref, items in zip(refs[1:], plan):
        for i, block in enumerate(items):
            start = line + block * size
            ref[i * size:(i + 1) * size, here] = value[start:start + size]


def mixed_kernel(cfg, far_ref, act_ref, combine_ref, down_ref, *refs):
    plan, levels, local, cap, cap_pad = cfg
    blocks, refs = refs[:levels], refs[levels:]
    outs, give_ref, spread, sems = refs[:-3], refs[-3], refs[-2], refs[-1]
    size = blocks[0].shape[0]
    here = half_of(1 - far_ref[0], blocks[0].shape[1])
    copies = [pltpu.make_async_copy(block.at[:, here], give_ref.at[pl.ds(i * size, size), :], sems.at[i])
              for i, block in enumerate(blocks)]
    hidden = down_ref.shape[2]
    tile = down_ref.shape[1]
    step = pl.program_id(0)

    @pl.when(step == 0)
    def _():
        for copy in copies:
            copy.start()
        for e in range(local):
            here = combine_ref[:, e * cap_pad:e * cap_pad + cap]
            spread[:, e * hidden:(e + 1) * hidden] = dot(here, act_ref[e, :, :hidden]).astype(BF16)

    total = dot_nt(spread[:, :hidden], down_ref[0])
    for e in range(1, local):
        total = total + dot_nt(spread[:, e * hidden:(e + 1) * hidden], down_ref[e])
    store_parts(plan, total.astype(BF16), pl.ds(pl.multiple_of(step * tile, tile), tile), outs)

    @pl.when(step == pl.num_programs(0) - 1)
    def _():
        for copy in copies:
            copy.wait()


def grad_kernel(cfg, far_ref, *refs):
    parts, local, cap, cap_pad, top = cfg
    blocks, refs = refs[:parts], refs[parts:]
    pick_ref, combine_ref, down_ref, pre_ref, info_ref, d_gate_ref, d_up_ref, tail_ref, keep_ref, give_ref = refs[:10]
    held, rows_ref, tails, sems = refs[10:]
    expert = pl.program_id(0)
    hidden = down_ref.shape[2]

    @pl.when(expert == 0)
    def _():
        load_blocks(blocks, held, sems)
        tails[...] = jnp.zeros(tails.shape, BF16)
        for start, stop in tiles(held.shape[1]):
            rows_ref[:, start:stop] = dot(pick_ref[...], held[:, start:stop]).astype(BF16)
        width = held.shape[1]
        keep_ref[...] = held[:, half_of(far_ref[0], width)]
        give_ref[...] = held[give_ref.shape[0]:, half_of(1 - far_ref[0], width)]

    info = info_ref[0]
    lane = iota(info.shape, 1)
    share = info[:, top:top + 1]
    gate_pre, up_pre = pre_ref[0, :, :hidden], pre_ref[0, :, hidden:]
    sig = jax.nn.sigmoid(gate_pre)
    silu = gate_pre * sig
    d_raw = dot(rows_ref[pl.ds(pl.multiple_of(expert * cap, 16), cap), :], down_ref[0])
    share_grad = jnp.sum(silu * up_pre * d_raw, axis=1, keepdims=True)
    d_active = share * d_raw
    d_gate_ref[0] = (d_active * up_pre * sig * (1.0 + gate_pre * (1.0 - sig))).astype(BF16)
    d_up_ref[0] = (d_active * silu).astype(BF16)
    placed = jnp.where((lane < top) & (info > 0.0), share_grad, 0.0)
    high = placed.astype(BF16)
    rest = placed - high.astype(F32)
    middle = rest.astype(BF16)
    low = (rest - middle.astype(F32)).astype(BF16)
    tail = high.astype(F32) + pltpu.roll(middle.astype(F32), top, 1) + pltpu.roll(low.astype(F32), 2 * top, 1)
    tails[pl.ds(pl.multiple_of(expert * cap_pad, cap_pad), cap), :] = tail.astype(BF16)

    @pl.when(expert == local - 1)
    def _():
        tail_ref[...] = dot(combine_ref[...], tails[...]).astype(BF16)


def input_kernel(cfg, d_gate_ref, d_up_ref, combine_ref, tail_ref, gate_ref, up_ref, *refs):
    plan, local, cap, cap_pad = cfg
    outs, rows = refs[:-1], refs[-1]
    tile, hidden = gate_ref.shape[1:]
    step = pl.program_id(0)

    @pl.when(step == 0)
    def _():
        rows[...] = jnp.zeros(rows.shape, BF16)
        width = outs[0].shape[1] - LANES
        store_parts(plan, tail_ref[...], slice(width, width + LANES), outs)

    for e in range(local):
        part = dot_nt(d_gate_ref[e], gate_ref[e]) + dot_nt(d_up_ref[e], up_ref[e])
        rows[e * cap_pad:e * cap_pad + cap, :] = part.astype(BF16)
    total = dot(combine_ref[...], rows[...]).astype(BF16)
    store_parts(plan, total, pl.ds(pl.multiple_of(step * tile, tile), tile), outs)


def store_halves(part, near_ref, both, keep_ref, give_ref):
    both[...] = part.astype(BF16)
    size = keep_ref.shape[1]
    keep_ref[0] = both[pl.ds(pl.multiple_of(near_ref[0] * size, 16), size), :]
    give_ref[0] = both[pl.ds(pl.multiple_of((1 - near_ref[0]) * size, 16), size), :]


def down_kernel(cap, near_ref, pick_ref, *refs):
    x_refs, c_refs, (act_ref, act_far_ref, rows_ref, keep_ref, give_ref, c_rows, acts, both) = refs[:3], refs[3:6], refs[6:]
    hidden = acts.shape[1]
    line = x_refs[1].shape[0]
    acts[:cap, :] = act_ref[0, :, :hidden]
    acts[cap:, :] = act_far_ref[0, :, :hidden]
    pair = act_far_ref[0, :, hidden:].astype(F32)
    token = pair[:, 0:1] * 128.0 + pair[:, 1:2]
    pick = pick_ref[...]
    pick_far = jnp.where(token == iota(pick.shape, 1).astype(F32), 1.0, 0.0).astype(BF16)
    for (own, far, far_pair), rows in ((x_refs, rows_ref.at[0]), (c_refs, c_rows)):
        rows[:cap, :] = dot(pick, own[...]).astype(BF16)
        rows[cap:, :] = (dot(pick_far[:, :line], far[...]) + dot(pick_far[:, line:], far_pair[...])).astype(BF16)
    store_halves(dot_tn(c_rows[...], acts[...]), near_ref, both, keep_ref, give_ref)


def both_kernel(cap, near_ref, rows_ref, d_gate_ref, gate_far_ref, d_up_ref, up_far_ref, keep_ref, give_ref, grads, both):
    hidden = d_gate_ref.shape[2]
    grads[:cap, :hidden] = d_gate_ref[0]
    grads[cap:, :hidden] = gate_far_ref[0]
    grads[:cap, hidden:] = d_up_ref[0]
    grads[cap:, hidden:] = up_far_ref[0]
    store_halves(dot_tn(rows_ref[0], grads[...]), near_ref, both, keep_ref, give_ref)


def cut_kernel(half, plan, word_ref, *refs):
    count = 1 + max(i for i, _, _, _ in plan)
    blocks, outs, sems = refs[:count], refs[count:-1], refs[-1]
    copies = []
    for i, flip, out, row in plan:
        which = 1 - word_ref[0] if flip else word_ref[0]
        here = pl.ds(pl.multiple_of(which * half, LANES), half)
        there = outs[out].at[pl.ds(row, blocks[i].shape[0]), :]
        copies.append(pltpu.make_async_copy(blocks[i].at[:, here], there, sems.at[len(copies)]))
    for copy in copies:
        copy.start()
    for copy in copies:
        copy.wait()


def swap(value, bit, count):
    return lax.ppermute(value, "dp", [(i, i ^ bit) for i in range(count)])


def exchange(value, bit, count):
    return lax.ppermute(value, "expert", [(i, i ^ bit) for i in range(count)])


def fence(*values):
    leaves, tree = jax.tree.flatten(values)
    return jax.tree.unflatten(tree, lax.optimization_barrier(tuple(leaves)))


def split3(value):
    high = lax.reduce_precision(value, 8, 7)
    rest = value - high
    middle = lax.reduce_precision(rest, 8, 7)
    return [high.astype(BF16), middle.astype(BF16), (rest - middle).astype(BF16)]


def shards(tokens, routes, probs, cotangent, w_gate, w_up, w_down):
    tok_rows, top = routes.shape
    local, width, hidden = w_gate.shape
    n_exp = lax.axis_size("expert")
    n_dp = lax.axis_size("dp")
    experts = local * n_exp
    cap = 5 * tok_rows * top // (4 * experts) * n_exp
    cap_pad = round_up(cap, LANES)
    total = n_exp * tok_rows
    levels = n_exp // 2
    line = levels * tok_rows
    wide = width + LANES
    tile = min(width, 512)
    columns = width // n_dp
    half = width // 2
    far_bit = n_dp // 2
    my_dp = lax.axis_index("dp")
    far = jnp.where((my_dp & far_bit) > 0, 1, 0)
    near = jnp.where((my_dp & 1) > 0, 1, 0)
    near_word = near.astype(jnp.int32).reshape(1)
    far_word = far.astype(jnp.int32).reshape(1)
    first = (lax.axis_index("expert") * local).astype(jnp.int32).reshape(1)
    line_blocks = list(range(0, n_exp, 2))
    sides = [k for k in line_blocks if k & 2 and k > 2]
    folds = [k ^ 2 for k in sides]
    groups = [sides, folds, [2, 0]]
    plan = [[k // 2 for k in group] for group in groups]
    upper_bits = [1 << i for i in range(2, n_exp.bit_length() - 1)]

    def send(value, bit):
        return exchange(value, bit, n_exp)

    def gather_upper(value):
        blocks = {0: value}
        for bit in reversed(upper_bits):
            blocks.update({k | bit: send(block, bit) for k, block in list(blocks.items())})
        return blocks

    any_space = pl.BlockSpec(memory_space=pl.ANY)
    smem = pl.BlockSpec(memory_space=pltpu.SMEM)
    params = pltpu.CompilerParams(dimension_semantics=("arbitrary",), vmem_limit_bytes=VMEM_LIMIT)

    def by_expert(*shape):
        return pl.BlockSpec((1,) + shape, lambda e: (e,) + (0,) * len(shape))

    def whole(*shape):
        return pl.BlockSpec(shape, lambda e: (0,) * len(shape))

    def sds(shape, dtype):
        return jax.ShapeDtypeStruct(shape, dtype)

    def cost(gflop, mbyte):
        return pl.CostEstimate(flops=gflop * 10**6, bytes_accessed=mbyte * 10**3, transcendentals=0)

    def cut_blocks(word, blocks, size, wanted, name):
        plan, rows = [], []
        for out, items in enumerate(wanted):
            rows.append(0)
            for i, flip in items:
                plan.append((i, flip, out, rows[out]))
                rows[out] += blocks[i].shape[0]
        return pl.pallas_call(
            functools.partial(cut_kernel, size, plan),
            in_specs=[smem] + [any_space] * len(blocks),
            out_specs=[pl.BlockSpec(memory_space=pltpu.VMEM)] * len(wanted),
            out_shape=[sds((n, size), BF16) for n in rows],
            scratch_shapes=[pltpu.SemaphoreType.DMA((len(plan),))],
            compiler_params=pltpu.CompilerParams(vmem_limit_bytes=VMEM_LIMIT),
            cost_estimate=cost(0, 2),
            name=name,
        )(word, *blocks)

    def cut_far(blocks, name):
        return cut_blocks(far_word, blocks, width // 2, [[(i, 1) for i in range(len(blocks))]], name)[0]

    by_columns = pl.BlockSpec((local, tile, hidden), lambda j: (0, j, 0))
    weight_spec = by_expert(width, hidden)
    parts = n_exp
    cfg = (parts, local, cap, cap_pad, top)

    totals = jnp.sum(probs, axis=1, keepdims=True)
    share = probs / totals
    meta = jnp.concatenate([routes.astype(BF16)] + split3(share), axis=1)
    meta = jnp.pad(meta, ((0, 0), (0, LANES - 4 * top)))

    x_own = jnp.concatenate([tokens, meta], axis=1)
    x_line = gather_upper(x_own)
    x_line[2] = send(x_own, 2)
    x_pair = {k: send(x_line[k], 1) for k in (0, 2)}
    x_line, x_pair[0], cot = fence(x_line, x_pair[0], cotangent)

    x_line.update({k | 2: send(x_line[k], 2) for k in folds})
    c_line = gather_upper(cot)
    x_pair.update({k: send(x_line[k], 1) for k in folds})
    x_line, c_line, x_pair = fence(x_line, c_line, x_pair)
    x_pair.update({k: send(x_line[k], 1) for k in sides})
    x_far = swap(cut_far([x_line[k] for k in line_blocks], "cut_x"), far_bit, n_dp)
    c_line[2] = send(c_line[0], 2)
    c_line.update({k | 2: send(c_line[k], 2) for k in folds})
    c_pair = {k: send(c_line[k], 1) for k in [0] + folds}
    pre, act, info, pick, combine, x_keep, x_give = pl.pallas_call(
        functools.partial(hidden_kernel, cfg),
        grid=(local,),
        in_specs=[smem] * 2 + [any_space] * parts + [weight_spec] * 2,
        out_specs=[by_expert(cap, 2 * hidden), by_expert(cap, hidden + LANES), by_expert(cap, LANES),
                   whole(local * cap, total), whole(total, local * cap_pad), whole(total, half), whole(line, half)],
        out_shape=[sds((local, cap, 2 * hidden), F32), sds((local, cap, hidden + LANES), BF16),
                   sds((local, cap, LANES), F32), sds((local * cap, total), BF16), sds((total, local * cap_pad), BF16),
                   sds((total, half), BF16), sds((line, half), BF16)],
        scratch_shapes=[
            pltpu.VMEM((total, wide), BF16),
            pltpu.VMEM((local * cap, wide), BF16),
            pltpu.SemaphoreType.DMA((parts,)),
        ],
        compiler_params=params,
        cost_estimate=cost(6, 20),
        name="hidden",
    )(first, far_word, *[x_line[k] for k in line_blocks], *[x_pair[k] for k in line_blocks], w_gate, w_up)
    act, c_line, c_pair, x_far = fence(act, c_line, c_pair, x_far)

    c_pair.update({k: send(c_line[k], 1) for k in [2] + sides})
    x_far_pair = swap(x_give, far_bit, n_dp)
    act_far = swap(act, far_bit, n_dp)
    level_rows = [line] + [len(group) * tok_rows for group in groups]
    level_specs = [whole(rows, width) for rows in level_rows]
    mixed_keep, *mixed_out, c_give = pl.pallas_call(
        functools.partial(mixed_kernel, (plan, levels, local, cap, cap_pad)),
        grid=(width // tile,),
        in_specs=[smem, whole(local, cap, hidden + LANES), whole(total, local * cap_pad), by_columns] + [any_space] * levels,
        out_specs=level_specs + [whole(line, half)],
        out_shape=[sds((rows, width), BF16) for rows in level_rows] + [sds((line, half), BF16)],
        scratch_shapes=[pltpu.VMEM((total, local * hidden), BF16), pltpu.SemaphoreType.DMA((levels,))],
        compiler_params=params,
        cost_estimate=cost(6, 10),
        name="mixed",
    )(far_word, act, combine, w_down, *[c_line[k] for k in line_blocks])
    c_pair, mixed_keep, mixed_out, c_give, x_far_pair = fence(c_pair, mixed_keep, mixed_out, c_give, x_far_pair)

    def back_rows(keep, got):
        return keep.astype(F32) + got.astype(F32)

    def pair_sums(keep, got, group):
        mine = jnp.concatenate([keep[k // 2 * tok_rows:(k // 2 + 1) * tok_rows] for k in group], axis=0)
        return back_rows(mine, got)

    def fold_upper(sums):
        blocks = {k: sums[i * tok_rows:(i + 1) * tok_rows] for i, k in enumerate(folds)}
        landed = []
        for bit in upper_bits:
            for k in [k for k in blocks if k & bit]:
                got = send(blocks.pop(k).astype(BF16), bit)
                if k == bit:
                    landed.append(got)
                else:
                    blocks[k ^ bit] = back_rows(blocks[k ^ bit], got)
        return landed

    def finish(sums, landed):
        return sum([part.astype(F32) for part in landed], sums[tok_rows:].astype(F32))

    mixed_got = [send(part, 1) for part in mixed_out[:2]]
    c_far = swap(c_give, far_bit, n_dp)
    d_gate, d_up, tail, c_keep, c_give = pl.pallas_call(
        functools.partial(grad_kernel, cfg),
        grid=(local,),
        in_specs=[smem] + [any_space] * parts + [whole(local * cap, total), whole(total, local * cap_pad), weight_spec,
                                                 by_expert(cap, 2 * hidden), by_expert(cap, LANES)],
        out_specs=[by_expert(cap, hidden)] * 2 + [whole(total, LANES), whole(total, half), whole(line, half)],
        out_shape=[sds((local, cap, hidden), BF16)] * 2 + [sds((total, LANES), BF16),
                   sds((total, half), BF16), sds((line, half), BF16)],
        scratch_shapes=[
            pltpu.VMEM((total, width), BF16),
            pltpu.VMEM((local * cap, width), BF16),
            pltpu.VMEM((local * cap_pad, LANES), BF16),
            pltpu.SemaphoreType.DMA((parts,)),
        ],
        compiler_params=params,
        cost_estimate=cost(6, 12),
        name="hidden_grads",
    )(far_word, *[c_line[k] for k in line_blocks], *[c_pair[k] for k in line_blocks], pick, combine, w_down, pre, info)
    mixed_sides, mixed_got, mixed_out, d_gate, d_up, tail, c_give, act_far = fence(
        pair_sums(mixed_keep, mixed_got[0], sides).astype(BF16), mixed_got, mixed_out, d_gate, d_up, tail, c_give, act_far)

    mixed_sides = send(mixed_sides, 2)
    mixed_got.append(send(mixed_out[2], 1))
    c_far_pair = swap(c_give, far_bit, n_dp)
    wide_specs = [whole(rows, wide) for rows in level_rows]
    input_keep, *input_out = pl.pallas_call(
        functools.partial(input_kernel, (plan, local, cap, cap_pad)),
        grid=(width // tile,),
        in_specs=[whole(local, cap, hidden)] * 2 + [whole(total, local * cap_pad), whole(total, LANES),
                                                    by_columns, by_columns],
        out_specs=wide_specs,
        out_shape=[sds((rows, wide), BF16) for rows in level_rows],
        scratch_shapes=[pltpu.VMEM((local * cap_pad, tile), BF16)],
        compiler_params=params,
        cost_estimate=cost(6, 16),
        name="input_grads",
    )(d_gate, d_up, combine, tail, w_gate, w_up)
    input_keep, input_out, mixed_sides, mixed_got, c_far, d_gate = fence(
        input_keep, input_out, mixed_sides, mixed_got, c_far, d_gate)

    input_got = [send(part, 1) for part in input_out[:2]]
    mixed_landed = fold_upper(back_rows(pair_sums(mixed_keep, mixed_got[1], folds), mixed_sides))
    gate_far = swap(d_gate, far_bit, n_dp)
    input_sides, input_out, c_far_pair, x_keep, d_up = fence(
        pair_sums(input_keep, input_got[0], sides).astype(BF16), input_out, c_far_pair, x_keep, d_up)
    input_sides = send(input_sides, 2)
    input_got.append(send(input_out[2], 1))
    up_far = swap(d_up, far_bit, n_dp)
    partial_specs = [by_expert(columns, hidden)] * 2
    partial_shapes = [sds((local, columns, hidden), BF16)] * 2
    x_rows, down_keep, down_give = pl.pallas_call(
        functools.partial(down_kernel, cap),
        grid=(local,),
        in_specs=[smem, pl.BlockSpec((cap, total), lambda e: (e, 0))] + [whole(total, half), whole(line, half), whole(line, half)] * 2
        + [by_expert(cap, hidden + LANES)] * 2,
        out_specs=[by_expert(2 * cap, half)] + partial_specs,
        out_shape=[sds((local, 2 * cap, half), BF16)] + partial_shapes,
        scratch_shapes=[pltpu.VMEM((2 * cap, half), BF16), pltpu.VMEM((2 * cap, hidden), BF16), pltpu.VMEM((half, hidden), BF16)],
        compiler_params=params,
        cost_estimate=cost(6, 12),
        name="down_grads",
    )(near_word, pick, x_keep, x_far, x_far_pair, c_keep, c_far, c_far_pair, act, act_far)
    input_folds, mixed_landed, mixed_got[2], x_rows, down_keep, down_give = fence(
        back_rows(pair_sums(input_keep, input_got[1], folds), input_sides).astype(BF16),
        mixed_landed, mixed_got[2], x_rows, down_keep, down_give)

    input_landed = fold_upper(input_folds)
    mixed_ends = pair_sums(mixed_keep, mixed_got[2], [2, 0])
    mixed_landed.append(send(mixed_ends[:tok_rows].astype(BF16), 2))
    input_ends = pair_sums(input_keep, input_got[2], [2, 0])
    input_landed.append(send(input_ends[:tok_rows].astype(BF16), 2))
    down_got = swap(down_give, 1, n_dp)
    mixed = finish(mixed_ends, mixed_landed).astype(BF16)
    mixed, input_ends, gate_far, up_far, down_got = fence(mixed, input_ends, gate_far, up_far, down_got)
    both_specs = [by_expert(columns, 2 * hidden)] * 2
    both_keep, both_give = pl.pallas_call(
        functools.partial(both_kernel, cap),
        grid=(local,),
        in_specs=[smem, by_expert(2 * cap, half)] + [by_expert(cap, hidden)] * 4,
        out_specs=both_specs,
        out_shape=[sds((local, columns, 2 * hidden), BF16)] * 2,
        scratch_shapes=[pltpu.VMEM((2 * cap, 2 * hidden), BF16), pltpu.VMEM((half, 2 * hidden), BF16)],
        compiler_params=params,
        cost_estimate=cost(3, 10),
        name="gate_up_grads",
    )(near_word, x_rows, d_gate, gate_far, d_up, up_far)
    both_give, input_landed = fence(both_give, input_landed)
    both_got = swap(both_give, 1, n_dp)
    down_grad = back_rows(down_keep, down_got).astype(BF16)
    gate_grad = back_rows(both_keep[:, :, :hidden], both_got[:, :, :hidden]).astype(BF16)
    up_grad = back_rows(both_keep[:, :, hidden:], both_got[:, :, hidden:]).astype(BF16)

    back = finish(input_ends, input_landed)
    token_grad = back[:, :width].astype(BF16)
    tail = back[:, width:]
    slot_sg = tail[:, :top] + tail[:, top:2 * top] + tail[:, 2 * top:3 * top]
    prob_grad = (slot_sg - jnp.sum(share * slot_sg, axis=1, keepdims=True)) / totals
    return mixed, token_grad, prob_grad, gate_grad, up_grad, down_grad


def solution(mesh):
    rows = P(("expert", "dp"), None)
    weight = P("expert", None, None)
    grad = P("expert", "dp", None)
    return jax.shard_map(
        shards,
        mesh=mesh,
        in_specs=(rows, rows, rows, rows, weight, weight, weight),
        out_specs=(rows, rows, rows, grad, grad, grad),
        check_vma=False,
    )
```

```python
import functools

import jax
import jax.numpy as jnp
from jax import lax
from jax.experimental import pallas as pl
from jax.experimental.pallas import tpu as pltpu
from jax.sharding import PartitionSpec as P


F32 = jnp.float32
BF16 = jnp.bfloat16
LANES = 128
VMEM_LIMIT = 60 * 1024 * 1024


def round_up(value, unit):
    return -(-value // unit) * unit


def dot(a, b):
    return jnp.dot(a, b, preferred_element_type=F32)


def dot_nt(a, b):
    return lax.dot_general(a, b, (((1,), (1,)), ((), ())), preferred_element_type=F32)


def dot_tn(a, b):
    return lax.dot_general(a, b, (((0,), (0,)), ((), ())), preferred_element_type=F32)


def iota(shape, dim):
    return lax.broadcasted_iota(jnp.int32, shape, dim)


def load_blocks(blocks, held, sems):
    copies, start = [], 0
    for i, block in enumerate(blocks):
        size = block.shape[0]
        copies.append(pltpu.make_async_copy(block, held.at[pl.ds(start, size), :], sems.at[i]))
        start += size
    for copy in copies:
        copy.start()
    for copy in copies:
        copy.wait()


def tiles(width, tile=512):
    return [(start, min(start + tile, width)) for start in range(0, width, tile)]


def half_of(which, width):
    return pl.ds(pl.multiple_of(which * (width // 2), LANES), width // 2)


def hidden_kernel(cfg, first_ref, far_ref, *refs):
    parts, local, cap, cap_pad, top = cfg
    blocks, refs = refs[:parts], refs[parts:]
    gate_ref, up_ref, pre_ref, act_ref, info_ref, pick_ref, combine_ref, keep_ref, give_ref = refs[:9]
    held, rows_ref, sems = refs[9:]
    expert = pl.program_id(0)
    tokens = held.shape[0]
    width, hidden = gate_ref.shape[1:]

    @pl.when(expert == 0)
    def _():
        load_blocks(blocks, held, sems)
        meta = held[:, width:].astype(F32).astype(jnp.int32)
        lane = iota(meta.shape, 1)
        hits = jnp.zeros(meta.shape, F32)
        for i in range(local):
            named = (meta == first_ref[0] + i) & (lane < top)
            hit = jnp.sum(jnp.where(named, 1.0, 0.0), axis=1, keepdims=True)
            hits = hits + jnp.where(lane == i, hit, 0.0)
        step = min(tokens, 256)
        below = (iota((step, step), 0) >= iota((step, step), 1)).astype(F32).astype(BF16)
        carry = jnp.zeros((1, LANES), F32)
        slots = []
        for start in range(0, tokens, step):
            part = hits[start:start + step]
            rank = dot(below, part.astype(BF16)) + carry
            carry = rank[step - 1:step]
            slots.append(jnp.where(part > 0.0, rank - 1.0, -1.0))
        slots = jnp.concatenate(slots, axis=0)
        slots_t = jnp.transpose(slots)
        places = iota((tokens, cap_pad), 1).astype(F32)
        places_t = iota((cap, tokens), 0).astype(F32)
        for i in range(local):
            hit = slots[:, i:i + 1] == places
            combine_ref[:, i * cap_pad:(i + 1) * cap_pad] = jnp.where(hit, 1.0, 0.0).astype(BF16)
            hit = slots_t[i:i + 1, :] == places_t
            pick_ref[i * cap:(i + 1) * cap, :] = jnp.where(hit, 1.0, 0.0).astype(BF16)
        for start, stop in tiles(held.shape[1]):
            rows_ref[:, start:stop] = dot(pick_ref[...], held[:, start:stop]).astype(BF16)
        keep_ref[...] = held[:, half_of(far_ref[0], width)]
        give_ref[...] = held[give_ref.shape[0]:, half_of(1 - far_ref[0], width)]

    here = pl.ds(pl.multiple_of(expert * cap, 16), cap)
    pick = pick_ref[here, :].astype(F32)
    token = jnp.sum(pick * iota(pick.shape, 1).astype(F32), axis=1, keepdims=True)
    token = jnp.where(jnp.sum(pick, axis=1, keepdims=True) > 0.0, token, -128.0).astype(jnp.int32)
    meta = rows_ref[here, width:].astype(F32)
    lane = iota(meta.shape, 1)
    named = (meta.astype(jnp.int32) == first_ref[0] + expert) & (lane < top)
    shares = sum(pltpu.roll(meta, LANES - top * (i + 1), 1) for i in range(3))
    share = jnp.sum(jnp.where(named, shares, 0.0), axis=1, keepdims=True)
    info_ref[0] = jnp.where(lane < top, jnp.where(named, 1.0, 0.0), share)

    rows = rows_ref[here, :width]
    gate_pre = dot(rows, gate_ref[0])
    up_pre = dot(rows, up_ref[0])
    pre_ref[0, :, :hidden] = gate_pre
    pre_ref[0, :, hidden:] = up_pre
    active = gate_pre * jax.nn.sigmoid(gate_pre) * up_pre
    act_ref[0, :, :hidden] = (share * active).astype(BF16)
    token_pair = jnp.where(lane == 0, token >> 7, jnp.where(lane == 1, token & 127, 0))
    act_ref[0, :, hidden:] = token_pair.astype(F32).astype(BF16)


def store_parts(plan, value, here, refs):
    refs[0][:, here] = value[:refs[0].shape[0]]
    line, size = refs[0].shape[0], refs[0].shape[0] // sum(len(items) for items in plan)
    for ref, items in zip(refs[1:], plan):
        for i, block in enumerate(items):
            start = line + block * size
            ref[i * size:(i + 1) * size, here] = value[start:start + size]


def mixed_kernel(cfg, far_ref, act_ref, combine_ref, down_ref, *refs):
    plan, levels, local, cap, cap_pad = cfg
    blocks, refs = refs[:levels], refs[levels:]
    outs, give_ref, spread, sems = refs[:-3], refs[-3], refs[-2], refs[-1]
    size = blocks[0].shape[0]
    here = half_of(1 - far_ref[0], blocks[0].shape[1])
    copies = [pltpu.make_async_copy(block.at[:, here], give_ref.at[pl.ds(i * size, size), :], sems.at[i])
              for i, block in enumerate(blocks)]
    hidden = down_ref.shape[2]
    tile = down_ref.shape[1]
    step = pl.program_id(0)

    @pl.when(step == 0)
    def _():
        for copy in copies:
            copy.start()
        for e in range(local):
            here = combine_ref[:, e * cap_pad:e * cap_pad + cap]
            spread[:, e * hidden:(e + 1) * hidden] = dot(here, act_ref[e, :, :hidden]).astype(BF16)

    total = dot_nt(spread[:, :hidden], down_ref[0])
    for e in range(1, local):
        total = total + dot_nt(spread[:, e * hidden:(e + 1) * hidden], down_ref[e])
    store_parts(plan, total.astype(BF16), pl.ds(pl.multiple_of(step * tile, tile), tile), outs)

    @pl.when(step == pl.num_programs(0) - 1)
    def _():
        for copy in copies:
            copy.wait()


def grad_kernel(cfg, far_ref, *refs):
    parts, local, cap, cap_pad, top = cfg
    blocks, refs = refs[:parts], refs[parts:]
    pick_ref, combine_ref, down_ref, pre_ref, info_ref, d_gate_ref, d_up_ref, tail_ref, keep_ref, give_ref = refs[:10]
    held, rows_ref, tails, sems = refs[10:]
    expert = pl.program_id(0)
    hidden = down_ref.shape[2]

    @pl.when(expert == 0)
    def _():
        load_blocks(blocks, held, sems)
        tails[...] = jnp.zeros(tails.shape, BF16)
        for start, stop in tiles(held.shape[1]):
            rows_ref[:, start:stop] = dot(pick_ref[...], held[:, start:stop]).astype(BF16)
        width = held.shape[1]
        keep_ref[...] = held[:, half_of(far_ref[0], width)]
        give_ref[...] = held[give_ref.shape[0]:, half_of(1 - far_ref[0], width)]

    info = info_ref[0]
    lane = iota(info.shape, 1)
    share = info[:, top:top + 1]
    gate_pre, up_pre = pre_ref[0, :, :hidden], pre_ref[0, :, hidden:]
    sig = jax.nn.sigmoid(gate_pre)
    silu = gate_pre * sig
    d_raw = dot(rows_ref[pl.ds(pl.multiple_of(expert * cap, 16), cap), :], down_ref[0])
    share_grad = jnp.sum(silu * up_pre * d_raw, axis=1, keepdims=True)
    d_active = share * d_raw
    d_gate_ref[0] = (d_active * up_pre * sig * (1.0 + gate_pre * (1.0 - sig))).astype(BF16)
    d_up_ref[0] = (d_active * silu).astype(BF16)
    placed = jnp.where((lane < top) & (info > 0.0), share_grad, 0.0)
    high = placed.astype(BF16)
    rest = placed - high.astype(F32)
    middle = rest.astype(BF16)
    low = (rest - middle.astype(F32)).astype(BF16)
    tail = high.astype(F32) + pltpu.roll(middle.astype(F32), top, 1) + pltpu.roll(low.astype(F32), 2 * top, 1)
    tails[pl.ds(pl.multiple_of(expert * cap_pad, cap_pad), cap), :] = tail.astype(BF16)

    @pl.when(expert == local - 1)
    def _():
        tail_ref[...] = dot(combine_ref[...], tails[...]).astype(BF16)


def input_kernel(cfg, d_gate_ref, d_up_ref, combine_ref, tail_ref, gate_ref, up_ref, *refs):
    plan, local, cap, cap_pad = cfg
    outs, rows = refs[:-1], refs[-1]
    tile, hidden = gate_ref.shape[1:]
    step = pl.program_id(0)

    @pl.when(step == 0)
    def _():
        rows[...] = jnp.zeros(rows.shape, BF16)
        width = outs[0].shape[1] - LANES
        store_parts(plan, tail_ref[...], slice(width, width + LANES), outs)

    for e in range(local):
        part = dot_nt(d_gate_ref[e], gate_ref[e]) + dot_nt(d_up_ref[e], up_ref[e])
        rows[e * cap_pad:e * cap_pad + cap, :] = part.astype(BF16)
    total = dot(combine_ref[...], rows[...]).astype(BF16)
    store_parts(plan, total, pl.ds(pl.multiple_of(step * tile, tile), tile), outs)


def store_halves(part, near_ref, both, keep_ref, give_ref):
    both[...] = part.astype(BF16)
    size = keep_ref.shape[1]
    keep_ref[0] = both[pl.ds(pl.multiple_of(near_ref[0] * size, 16), size), :]
    give_ref[0] = both[pl.ds(pl.multiple_of((1 - near_ref[0]) * size, 16), size), :]


def down_kernel(cap, near_ref, pick_ref, *refs):
    x_refs, c_refs, (act_ref, act_far_ref, rows_ref, keep_ref, give_ref, c_rows, acts, both) = refs[:3], refs[3:6], refs[6:]
    hidden = acts.shape[1]
    line = x_refs[1].shape[0]
    acts[:cap, :] = act_ref[0, :, :hidden]
    acts[cap:, :] = act_far_ref[0, :, :hidden]
    pair = act_far_ref[0, :, hidden:].astype(F32)
    token = pair[:, 0:1] * 128.0 + pair[:, 1:2]
    pick = pick_ref[...]
    pick_far = jnp.where(token == iota(pick.shape, 1).astype(F32), 1.0, 0.0).astype(BF16)
    for (own, far, far_pair), rows in ((x_refs, rows_ref.at[0]), (c_refs, c_rows)):
        rows[:cap, :] = dot(pick, own[...]).astype(BF16)
        rows[cap:, :] = (dot(pick_far[:, :line], far[...]) + dot(pick_far[:, line:], far_pair[...])).astype(BF16)
    store_halves(dot_tn(c_rows[...], acts[...]), near_ref, both, keep_ref, give_ref)


def both_kernel(cap, near_ref, rows_ref, d_gate_ref, gate_far_ref, d_up_ref, up_far_ref, keep_ref, give_ref, grads, both):
    hidden = d_gate_ref.shape[2]
    grads[:cap, :hidden] = d_gate_ref[0]
    grads[cap:, :hidden] = gate_far_ref[0]
    grads[:cap, hidden:] = d_up_ref[0]
    grads[cap:, hidden:] = up_far_ref[0]
    store_halves(dot_tn(rows_ref[0], grads[...]), near_ref, both, keep_ref, give_ref)


def cut_kernel(half, plan, word_ref, *refs):
    count = 1 + max(i for i, _, _, _ in plan)
    blocks, outs, sems = refs[:count], refs[count:-1], refs[-1]
    copies = []
    for i, flip, out, row in plan:
        which = 1 - word_ref[0] if flip else word_ref[0]
        here = pl.ds(pl.multiple_of(which * half, LANES), half)
        there = outs[out].at[pl.ds(row, blocks[i].shape[0]), :]
        copies.append(pltpu.make_async_copy(blocks[i].at[:, here], there, sems.at[len(copies)]))
    for copy in copies:
        copy.start()
    for copy in copies:
        copy.wait()


def swap(value, bit, count):
    return lax.ppermute(value, "dp", [(i, i ^ bit) for i in range(count)])


def exchange(value, bit, count):
    return lax.ppermute(value, "expert", [(i, i ^ bit) for i in range(count)])


def fence(*values):
    leaves, tree = jax.tree.flatten(values)
    return jax.tree.unflatten(tree, lax.optimization_barrier(tuple(leaves)))


def split3(value):
    high = lax.reduce_precision(value, 8, 7)
    rest = value - high
    middle = lax.reduce_precision(rest, 8, 7)
    return [high.astype(BF16), middle.astype(BF16), (rest - middle).astype(BF16)]


def shards(tokens, routes, probs, cotangent, w_gate, w_up, w_down):
    tok_rows, top = routes.shape
    local, width, hidden = w_gate.shape
    n_exp = lax.axis_size("expert")
    n_dp = lax.axis_size("dp")
    experts = local * n_exp
    cap = 5 * tok_rows * top // (4 * experts) * n_exp
    cap_pad = round_up(cap, LANES)
    total = n_exp * tok_rows
    levels = n_exp // 2
    line = levels * tok_rows
    wide = width + LANES
    tile = min(width, 512)
    columns = width // n_dp
    half = width // 2
    far_bit = n_dp // 2
    my_dp = lax.axis_index("dp")
    far = jnp.where((my_dp & far_bit) > 0, 1, 0)
    near = jnp.where((my_dp & 1) > 0, 1, 0)
    near_word = near.astype(jnp.int32).reshape(1)
    far_word = far.astype(jnp.int32).reshape(1)
    first = (lax.axis_index("expert") * local).astype(jnp.int32).reshape(1)
    line_blocks = list(range(0, n_exp, 2))
    sides = [k for k in line_blocks if k & 2 and k > 2]
    folds = [k ^ 2 for k in sides]
    groups = [sides, folds, [2, 0]]
    plan = [[k // 2 for k in group] for group in groups]
    upper_bits = [1 << i for i in range(2, n_exp.bit_length() - 1)]

    def send(value, bit):
        return exchange(value, bit, n_exp)

    def gather_upper(value):
        blocks = {0: value}
        for bit in reversed(upper_bits):
            blocks.update({k | bit: send(block, bit) for k, block in list(blocks.items())})
        return blocks

    any_space = pl.BlockSpec(memory_space=pl.ANY)
    smem = pl.BlockSpec(memory_space=pltpu.SMEM)
    params = pltpu.CompilerParams(dimension_semantics=("arbitrary",), vmem_limit_bytes=VMEM_LIMIT)

    def by_expert(*shape):
        return pl.BlockSpec((1,) + shape, lambda e: (e,) + (0,) * len(shape))

    def whole(*shape):
        return pl.BlockSpec(shape, lambda e: (0,) * len(shape))

    def sds(shape, dtype):
        return jax.ShapeDtypeStruct(shape, dtype)

    def cost(gflop, mbyte):
        return pl.CostEstimate(flops=gflop * 10**6, bytes_accessed=mbyte * 10**3, transcendentals=0)

    def cut_blocks(word, blocks, size, wanted, name):
        plan, rows = [], []
        for out, items in enumerate(wanted):
            rows.append(0)
            for i, flip in items:
                plan.append((i, flip, out, rows[out]))
                rows[out] += blocks[i].shape[0]
        return pl.pallas_call(
            functools.partial(cut_kernel, size, plan),
            in_specs=[smem] + [any_space] * len(blocks),
            out_specs=[pl.BlockSpec(memory_space=pltpu.VMEM)] * len(wanted),
            out_shape=[sds((n, size), BF16) for n in rows],
            scratch_shapes=[pltpu.SemaphoreType.DMA((len(plan),))],
            compiler_params=pltpu.CompilerParams(vmem_limit_bytes=VMEM_LIMIT),
            cost_estimate=cost(0, 2),
            name=name,
        )(word, *blocks)

    def cut_far(blocks, name):
        return cut_blocks(far_word, blocks, width // 2, [[(i, 1) for i in range(len(blocks))]], name)[0]

    by_columns = pl.BlockSpec((local, tile, hidden), lambda j: (0, j, 0))
    weight_spec = by_expert(width, hidden)
    parts = n_exp
    cfg = (parts, local, cap, cap_pad, top)

    totals = jnp.sum(probs, axis=1, keepdims=True)
    share = probs / totals
    meta = jnp.concatenate([routes.astype(BF16)] + split3(share), axis=1)
    meta = jnp.pad(meta, ((0, 0), (0, LANES - 4 * top)))

    x_own = jnp.concatenate([tokens, meta], axis=1)
    x_line = gather_upper(x_own)
    x_line[2] = send(x_own, 2)
    x_pair = {k: send(x_line[k], 1) for k in (0, 2)}
    x_line, x_pair[0], cot = fence(x_line, x_pair[0], cotangent)

    x_line.update({k | 2: send(x_line[k], 2) for k in folds})
    c_line = gather_upper(cot)
    x_pair.update({k: send(x_line[k], 1) for k in folds})
    x_line, c_line, x_pair = fence(x_line, c_line, x_pair)
    x_pair.update({k: send(x_line[k], 1) for k in sides})
    x_far = swap(cut_far([x_line[k] for k in line_blocks], "cut_x"), far_bit, n_dp)
    c_line[2] = send(c_line[0], 2)
    c_line.update({k | 2: send(c_line[k], 2) for k in folds})
    c_pair = {k: send(c_line[k], 1) for k in [0] + folds}
    pre, act, info, pick, combine, x_keep, x_give = pl.pallas_call(
        functools.partial(hidden_kernel, cfg),
        grid=(local,),
        in_specs=[smem] * 2 + [any_space] * parts + [weight_spec] * 2,
        out_specs=[by_expert(cap, 2 * hidden), by_expert(cap, hidden + LANES), by_expert(cap, LANES),
                   whole(local * cap, total), whole(total, local * cap_pad), whole(total, half), whole(line, half)],
        out_shape=[sds((local, cap, 2 * hidden), F32), sds((local, cap, hidden + LANES), BF16),
                   sds((local, cap, LANES), F32), sds((local * cap, total), BF16), sds((total, local * cap_pad), BF16),
                   sds((total, half), BF16), sds((line, half), BF16)],
        scratch_shapes=[
            pltpu.VMEM((total, wide), BF16),
            pltpu.VMEM((local * cap, wide), BF16),
            pltpu.SemaphoreType.DMA((parts,)),
        ],
        compiler_params=params,
        cost_estimate=cost(6, 20),
        name="hidden",
    )(first, far_word, *[x_line[k] for k in line_blocks], *[x_pair[k] for k in line_blocks], w_gate, w_up)
    act, c_line, c_pair, x_far = fence(act, c_line, c_pair, x_far)

    c_pair.update({k: send(c_line[k], 1) for k in [2] + sides})
    x_far_pair = swap(x_give, far_bit, n_dp)
    act_far = swap(act, far_bit, n_dp)
    level_rows = [line] + [len(group) * tok_rows for group in groups]
    level_specs = [whole(rows, width) for rows in level_rows]
    mixed_keep, *mixed_out, c_give = pl.pallas_call(
        functools.partial(mixed_kernel, (plan, levels, local, cap, cap_pad)),
        grid=(width // tile,),
        in_specs=[smem, whole(local, cap, hidden + LANES), whole(total, local * cap_pad), by_columns] + [any_space] * levels,
        out_specs=level_specs + [whole(line, half)],
        out_shape=[sds((rows, width), BF16) for rows in level_rows] + [sds((line, half), BF16)],
        scratch_shapes=[pltpu.VMEM((total, local * hidden), BF16), pltpu.SemaphoreType.DMA((levels,))],
        compiler_params=params,
        cost_estimate=cost(6, 10),
        name="mixed",
    )(far_word, act, combine, w_down, *[c_line[k] for k in line_blocks])
    c_pair, mixed_keep, mixed_out, c_give, x_far_pair = fence(c_pair, mixed_keep, mixed_out, c_give, x_far_pair)

    def back_rows(keep, got):
        return keep.astype(F32) + got.astype(F32)

    def pair_sums(keep, got, group):
        mine = jnp.concatenate([keep[k // 2 * tok_rows:(k // 2 + 1) * tok_rows] for k in group], axis=0)
        return back_rows(mine, got)

    def fold_upper(sums):
        blocks = {k: sums[i * tok_rows:(i + 1) * tok_rows] for i, k in enumerate(folds)}
        landed = []
        for bit in upper_bits:
            for k in [k for k in blocks if k & bit]:
                got = send(blocks.pop(k).astype(BF16), bit)
                if k == bit:
                    landed.append(got)
                else:
                    blocks[k ^ bit] = back_rows(blocks[k ^ bit], got)
        return landed

    def finish(sums, landed):
        return sum([part.astype(F32) for part in landed], sums[tok_rows:].astype(F32))

    mixed_got = [send(part, 1) for part in mixed_out[:2]]
    c_far = swap(c_give, far_bit, n_dp)
    d_gate, d_up, tail, c_keep, c_give = pl.pallas_call(
        functools.partial(grad_kernel, cfg),
        grid=(local,),
        in_specs=[smem] + [any_space] * parts + [whole(local * cap, total), whole(total, local * cap_pad), weight_spec,
                                                 by_expert(cap, 2 * hidden), by_expert(cap, LANES)],
        out_specs=[by_expert(cap, hidden)] * 2 + [whole(total, LANES), whole(total, half), whole(line, half)],
        out_shape=[sds((local, cap, hidden), BF16)] * 2 + [sds((total, LANES), BF16),
                   sds((total, half), BF16), sds((line, half), BF16)],
        scratch_shapes=[
            pltpu.VMEM((total, width), BF16),
            pltpu.VMEM((local * cap, width), BF16),
            pltpu.VMEM((local * cap_pad, LANES), BF16),
            pltpu.SemaphoreType.DMA((parts,)),
        ],
        compiler_params=params,
        cost_estimate=cost(6, 12),
        name="hidden_grads",
    )(far_word, *[c_line[k] for k in line_blocks], *[c_pair[k] for k in line_blocks], pick, combine, w_down, pre, info)
    mixed_sides, mixed_got, mixed_out, d_gate, d_up, tail, c_give, act_far = fence(
        pair_sums(mixed_keep, mixed_got[0], sides).astype(BF16), mixed_got, mixed_out, d_gate, d_up, tail, c_give, act_far)

    mixed_sides = send(mixed_sides, 2)
    mixed_got.append(send(mixed_out[2], 1))
    c_far_pair = swap(c_give, far_bit, n_dp)
    wide_specs = [whole(rows, wide) for rows in level_rows]
    input_keep, *input_out = pl.pallas_call(
        functools.partial(input_kernel, (plan, local, cap, cap_pad)),
        grid=(width // tile,),
        in_specs=[whole(local, cap, hidden)] * 2 + [whole(total, local * cap_pad), whole(total, LANES),
                                                    by_columns, by_columns],
        out_specs=wide_specs,
        out_shape=[sds((rows, wide), BF16) for rows in level_rows],
        scratch_shapes=[pltpu.VMEM((local * cap_pad, tile), BF16)],
        compiler_params=params,
        cost_estimate=cost(6, 16),
        name="input_grads",
    )(d_gate, d_up, combine, tail, w_gate, w_up)
    input_keep, input_out, mixed_sides, mixed_got, c_far, d_gate = fence(
        input_keep, input_out, mixed_sides, mixed_got, c_far, d_gate)

    input_got = [send(part, 1) for part in input_out[:2]]
    mixed_landed = fold_upper(back_rows(pair_sums(mixed_keep, mixed_got[1], folds), mixed_sides))
    gate_far = swap(d_gate, far_bit, n_dp)
    input_sides, input_out, c_far_pair, x_keep, d_up, mixed_got[2] = fence(
        pair_sums(input_keep, input_got[0], sides).astype(BF16), input_out, c_far_pair, x_keep, d_up, mixed_got[2])
    input_sides = send(input_sides, 2)
    input_got.append(send(input_out[2], 1))
    up_far = swap(d_up, far_bit, n_dp)
    mixed_ends = pair_sums(mixed_keep, mixed_got[2], [2, 0])
    partial_specs = [by_expert(columns, hidden)] * 2
    partial_shapes = [sds((local, columns, hidden), BF16)] * 2
    x_rows, down_keep, down_give = pl.pallas_call(
        functools.partial(down_kernel, cap),
        grid=(local,),
        in_specs=[smem, pl.BlockSpec((cap, total), lambda e: (e, 0))] + [whole(total, half), whole(line, half), whole(line, half)] * 2
        + [by_expert(cap, hidden + LANES)] * 2,
        out_specs=[by_expert(2 * cap, half)] + partial_specs,
        out_shape=[sds((local, 2 * cap, half), BF16)] + partial_shapes,
        scratch_shapes=[pltpu.VMEM((2 * cap, half), BF16), pltpu.VMEM((2 * cap, hidden), BF16), pltpu.VMEM((half, hidden), BF16)],
        compiler_params=params,
        cost_estimate=cost(6, 12),
        name="down_grads",
    )(near_word, pick, x_keep, x_far, x_far_pair, c_keep, c_far, c_far_pair, act, act_far)
    input_folds, mixed_landed, x_rows, down_keep, down_give = fence(
        back_rows(pair_sums(input_keep, input_got[1], folds), input_sides).astype(BF16),
        mixed_landed, x_rows, down_keep, down_give)

    input_landed = fold_upper(input_folds)
    mixed_landed.append(send(mixed_ends[:tok_rows].astype(BF16), 2))
    input_ends = pair_sums(input_keep, input_got[2], [2, 0])
    input_landed.append(send(input_ends[:tok_rows].astype(BF16), 2))
    down_got = swap(down_give, 1, n_dp)
    mixed = finish(mixed_ends, mixed_landed).astype(BF16)
    mixed, input_ends, input_landed[0], gate_far, up_far = fence(
        mixed, input_ends, input_landed[0], gate_far, up_far)
    both_specs = [by_expert(columns, 2 * hidden)] * 2
    both_keep, both_give = pl.pallas_call(
        functools.partial(both_kernel, cap),
        grid=(local,),
        in_specs=[smem, by_expert(2 * cap, half)] + [by_expert(cap, hidden)] * 4,
        out_specs=both_specs,
        out_shape=[sds((local, columns, 2 * hidden), BF16)] * 2,
        scratch_shapes=[pltpu.VMEM((2 * cap, 2 * hidden), BF16), pltpu.VMEM((half, 2 * hidden), BF16)],
        compiler_params=params,
        cost_estimate=cost(3, 10),
        name="gate_up_grads",
    )(near_word, x_rows, d_gate, gate_far, d_up, up_far)
    both_give, input_landed = fence(both_give, input_landed)
    both_got = swap(both_give, 1, n_dp)
    gate_grad = back_rows(both_keep[:, :, :hidden], both_got[:, :, :hidden]).astype(BF16)
    up_grad = back_rows(both_keep[:, :, hidden:], both_got[:, :, hidden:]).astype(BF16)
    gate_grad, up_grad, down_got = fence(gate_grad, up_grad, down_got)
    down_grad = back_rows(down_keep, down_got).astype(BF16)

    back = finish(input_ends, input_landed)
    token_grad = back[:, :width].astype(BF16)
    tail = back[:, width:]
    slot_sg = tail[:, :top] + tail[:, top:2 * top] + tail[:, 2 * top:3 * top]
    prob_grad = (slot_sg - jnp.sum(share * slot_sg, axis=1, keepdims=True)) / totals
    return mixed, token_grad, prob_grad, gate_grad, up_grad, down_grad


def solution(mesh):
    rows = P(("expert", "dp"), None)
    weight = P("expert", None, None)
    grad = P("expert", "dp", None)
    return jax.shard_map(
        shards,
        mesh=mesh,
        in_specs=(rows, rows, rows, rows, weight, weight, weight),
        out_specs=(rows, rows, rows, grad, grad, grad),
        check_vma=False,
    )
```

```python
import functools

import jax
import jax.numpy as jnp
from jax import lax
from jax.experimental import pallas as pl
from jax.experimental.pallas import tpu as pltpu
from jax.sharding import PartitionSpec as P


F32 = jnp.float32
BF16 = jnp.bfloat16
LANES = 128
VMEM_LIMIT = 60 * 1024 * 1024


def round_up(value, unit):
    return -(-value // unit) * unit


def dot(a, b):
    return jnp.dot(a, b, preferred_element_type=F32)


def dot_nt(a, b):
    return lax.dot_general(a, b, (((1,), (1,)), ((), ())), preferred_element_type=F32)


def dot_tn(a, b):
    return lax.dot_general(a, b, (((0,), (0,)), ((), ())), preferred_element_type=F32)


def iota(shape, dim):
    return lax.broadcasted_iota(jnp.int32, shape, dim)


def load_blocks(blocks, held, sems):
    copies, start = [], 0
    for i, block in enumerate(blocks):
        size = block.shape[0]
        copies.append(pltpu.make_async_copy(block, held.at[pl.ds(start, size), :], sems.at[i]))
        start += size
    for copy in copies:
        copy.start()
    for copy in copies:
        copy.wait()


def tiles(width, tile=512):
    return [(start, min(start + tile, width)) for start in range(0, width, tile)]


def half_of(which, width):
    return pl.ds(pl.multiple_of(which * (width // 2), LANES), width // 2)


def hidden_kernel(cfg, first_ref, far_ref, *refs):
    parts, local, cap, cap_pad, top = cfg
    blocks, refs = refs[:parts], refs[parts:]
    gate_ref, up_ref, pre_ref, act_ref, info_ref, pick_ref, combine_ref, keep_ref, give_ref = refs[:9]
    held, rows_ref, sems = refs[9:]
    expert = pl.program_id(0)
    tokens = held.shape[0]
    width, hidden = gate_ref.shape[1:]

    @pl.when(expert == 0)
    def _():
        load_blocks(blocks, held, sems)
        meta = held[:, width:].astype(F32).astype(jnp.int32)
        lane = iota(meta.shape, 1)
        hits = jnp.zeros(meta.shape, F32)
        for i in range(local):
            named = (meta == first_ref[0] + i) & (lane < top)
            hit = jnp.sum(jnp.where(named, 1.0, 0.0), axis=1, keepdims=True)
            hits = hits + jnp.where(lane == i, hit, 0.0)
        step = min(tokens, 256)
        below = (iota((step, step), 0) >= iota((step, step), 1)).astype(F32).astype(BF16)
        carry = jnp.zeros((1, LANES), F32)
        slots = []
        for start in range(0, tokens, step):
            part = hits[start:start + step]
            rank = dot(below, part.astype(BF16)) + carry
            carry = rank[step - 1:step]
            slots.append(jnp.where(part > 0.0, rank - 1.0, -1.0))
        slots = jnp.concatenate(slots, axis=0)
        slots_t = jnp.transpose(slots)
        places = iota((tokens, cap_pad), 1).astype(F32)
        places_t = iota((cap, tokens), 0).astype(F32)
        for i in range(local):
            hit = slots[:, i:i + 1] == places
            combine_ref[:, i * cap_pad:(i + 1) * cap_pad] = jnp.where(hit, 1.0, 0.0).astype(BF16)
            hit = slots_t[i:i + 1, :] == places_t
            pick_ref[i * cap:(i + 1) * cap, :] = jnp.where(hit, 1.0, 0.0).astype(BF16)
        for start, stop in tiles(held.shape[1]):
            rows_ref[:, start:stop] = dot(pick_ref[...], held[:, start:stop]).astype(BF16)
        keep_ref[...] = held[:, half_of(far_ref[0], width)]
        give_ref[...] = held[give_ref.shape[0]:, half_of(1 - far_ref[0], width)]

    here = pl.ds(pl.multiple_of(expert * cap, 16), cap)
    pick = pick_ref[here, :].astype(F32)
    token = jnp.sum(pick * iota(pick.shape, 1).astype(F32), axis=1, keepdims=True)
    token = jnp.where(jnp.sum(pick, axis=1, keepdims=True) > 0.0, token, -128.0).astype(jnp.int32)
    meta = rows_ref[here, width:].astype(F32)
    lane = iota(meta.shape, 1)
    named = (meta.astype(jnp.int32) == first_ref[0] + expert) & (lane < top)
    shares = sum(pltpu.roll(meta, LANES - top * (i + 1), 1) for i in range(3))
    share = jnp.sum(jnp.where(named, shares, 0.0), axis=1, keepdims=True)
    info_ref[0] = jnp.where(lane < top, jnp.where(named, 1.0, 0.0), share)

    rows = rows_ref[here, :width]
    gate_pre = dot(rows, gate_ref[0])
    up_pre = dot(rows, up_ref[0])
    pre_ref[0, :, :hidden] = gate_pre
    pre_ref[0, :, hidden:] = up_pre
    active = gate_pre * jax.nn.sigmoid(gate_pre) * up_pre
    act_ref[0, :, :hidden] = (share * active).astype(BF16)
    token_pair = jnp.where(lane == 0, token >> 7, jnp.where(lane == 1, token & 127, 0))
    act_ref[0, :, hidden:] = token_pair.astype(F32).astype(BF16)


def store_parts(plan, value, here, refs):
    refs[0][:, here] = value[:refs[0].shape[0]]
    line, size = refs[0].shape[0], refs[0].shape[0] // sum(len(items) for items in plan)
    for ref, items in zip(refs[1:], plan):
        for i, block in enumerate(items):
            start = line + block * size
            ref[i * size:(i + 1) * size, here] = value[start:start + size]


def mixed_kernel(cfg, far_ref, act_ref, combine_ref, down_ref, *refs):
    plan, levels, local, cap, cap_pad = cfg
    blocks, refs = refs[:levels], refs[levels:]
    outs, give_ref, spread, sems = refs[:-3], refs[-3], refs[-2], refs[-1]
    size = blocks[0].shape[0]
    here = half_of(1 - far_ref[0], blocks[0].shape[1])
    copies = [pltpu.make_async_copy(block.at[:, here], give_ref.at[pl.ds(i * size, size), :], sems.at[i])
              for i, block in enumerate(blocks)]
    hidden = down_ref.shape[2]
    tile = down_ref.shape[1]
    step = pl.program_id(0)

    @pl.when(step == 0)
    def _():
        for copy in copies:
            copy.start()
        for e in range(local):
            here = combine_ref[:, e * cap_pad:e * cap_pad + cap]
            spread[:, e * hidden:(e + 1) * hidden] = dot(here, act_ref[e, :, :hidden]).astype(BF16)

    total = dot_nt(spread[:, :hidden], down_ref[0])
    for e in range(1, local):
        total = total + dot_nt(spread[:, e * hidden:(e + 1) * hidden], down_ref[e])
    store_parts(plan, total.astype(BF16), pl.ds(pl.multiple_of(step * tile, tile), tile), outs)

    @pl.when(step == pl.num_programs(0) - 1)
    def _():
        for copy in copies:
            copy.wait()


def grad_kernel(cfg, far_ref, *refs):
    parts, local, cap, cap_pad, top = cfg
    blocks, refs = refs[:parts], refs[parts:]
    pick_ref, combine_ref, down_ref, pre_ref, info_ref, d_gate_ref, d_up_ref, tail_ref, keep_ref, give_ref = refs[:10]
    held, rows_ref, tails, sems = refs[10:]
    expert = pl.program_id(0)
    hidden = down_ref.shape[2]

    @pl.when(expert == 0)
    def _():
        load_blocks(blocks, held, sems)
        tails[...] = jnp.zeros(tails.shape, BF16)
        for start, stop in tiles(held.shape[1]):
            rows_ref[:, start:stop] = dot(pick_ref[...], held[:, start:stop]).astype(BF16)
        width = held.shape[1]
        keep_ref[...] = held[:, half_of(far_ref[0], width)]
        give_ref[...] = held[give_ref.shape[0]:, half_of(1 - far_ref[0], width)]

    info = info_ref[0]
    lane = iota(info.shape, 1)
    share = info[:, top:top + 1]
    gate_pre, up_pre = pre_ref[0, :, :hidden], pre_ref[0, :, hidden:]
    sig = jax.nn.sigmoid(gate_pre)
    silu = gate_pre * sig
    d_raw = dot(rows_ref[pl.ds(pl.multiple_of(expert * cap, 16), cap), :], down_ref[0])
    share_grad = jnp.sum(silu * up_pre * d_raw, axis=1, keepdims=True)
    d_active = share * d_raw
    d_gate_ref[0] = (d_active * up_pre * sig * (1.0 + gate_pre * (1.0 - sig))).astype(BF16)
    d_up_ref[0] = (d_active * silu).astype(BF16)
    placed = jnp.where((lane < top) & (info > 0.0), share_grad, 0.0)
    high = placed.astype(BF16)
    rest = placed - high.astype(F32)
    middle = rest.astype(BF16)
    low = (rest - middle.astype(F32)).astype(BF16)
    tail = high.astype(F32) + pltpu.roll(middle.astype(F32), top, 1) + pltpu.roll(low.astype(F32), 2 * top, 1)
    tails[pl.ds(pl.multiple_of(expert * cap_pad, cap_pad), cap), :] = tail.astype(BF16)

    @pl.when(expert == local - 1)
    def _():
        tail_ref[...] = dot(combine_ref[...], tails[...]).astype(BF16)


def input_kernel(cfg, d_gate_ref, d_up_ref, combine_ref, tail_ref, gate_ref, up_ref, *refs):
    plan, local, cap, cap_pad = cfg
    outs, rows = refs[:-1], refs[-1]
    tile, hidden = gate_ref.shape[1:]
    step = pl.program_id(0)

    @pl.when(step == 0)
    def _():
        rows[...] = jnp.zeros(rows.shape, BF16)
        width = outs[0].shape[1] - LANES
        store_parts(plan, tail_ref[...], slice(width, width + LANES), outs)

    for e in range(local):
        part = dot_nt(d_gate_ref[e], gate_ref[e]) + dot_nt(d_up_ref[e], up_ref[e])
        rows[e * cap_pad:e * cap_pad + cap, :] = part.astype(BF16)
    total = dot(combine_ref[...], rows[...]).astype(BF16)
    store_parts(plan, total, pl.ds(pl.multiple_of(step * tile, tile), tile), outs)


def store_halves(part, near_ref, both, keep_ref, give_ref):
    both[...] = part.astype(BF16)
    size = keep_ref.shape[1]
    keep_ref[0] = both[pl.ds(pl.multiple_of(near_ref[0] * size, 16), size), :]
    give_ref[0] = both[pl.ds(pl.multiple_of((1 - near_ref[0]) * size, 16), size), :]


def down_kernel(cap, near_ref, pick_ref, *refs):
    x_refs, c_refs, (act_ref, act_far_ref, rows_ref, keep_ref, give_ref, c_rows, acts, both) = refs[:3], refs[3:6], refs[6:]
    hidden = acts.shape[1]
    line = x_refs[1].shape[0]
    acts[:cap, :] = act_ref[0, :, :hidden]
    acts[cap:, :] = act_far_ref[0, :, :hidden]
    pair = act_far_ref[0, :, hidden:].astype(F32)
    token = pair[:, 0:1] * 128.0 + pair[:, 1:2]
    pick = pick_ref[...]
    pick_far = jnp.where(token == iota(pick.shape, 1).astype(F32), 1.0, 0.0).astype(BF16)
    for (own, far, far_pair), rows in ((x_refs, rows_ref.at[0]), (c_refs, c_rows)):
        rows[:cap, :] = dot(pick, own[...]).astype(BF16)
        rows[cap:, :] = (dot(pick_far[:, :line], far[...]) + dot(pick_far[:, line:], far_pair[...])).astype(BF16)
    store_halves(dot_tn(c_rows[...], acts[...]), near_ref, both, keep_ref, give_ref)


def both_kernel(cap, near_ref, rows_ref, d_gate_ref, gate_far_ref, d_up_ref, up_far_ref, keep_ref, give_ref, grads, both):
    hidden = d_gate_ref.shape[2]
    grads[:cap, :hidden] = d_gate_ref[0]
    grads[cap:, :hidden] = gate_far_ref[0]
    grads[:cap, hidden:] = d_up_ref[0]
    grads[cap:, hidden:] = up_far_ref[0]
    store_halves(dot_tn(rows_ref[0], grads[...]), near_ref, both, keep_ref, give_ref)


def cut_kernel(half, plan, word_ref, *refs):
    count = 1 + max(i for i, _, _, _ in plan)
    blocks, outs, sems = refs[:count], refs[count:-1], refs[-1]
    copies = []
    for i, flip, out, row in plan:
        which = 1 - word_ref[0] if flip else word_ref[0]
        here = pl.ds(pl.multiple_of(which * half, LANES), half)
        there = outs[out].at[pl.ds(row, blocks[i].shape[0]), :]
        copies.append(pltpu.make_async_copy(blocks[i].at[:, here], there, sems.at[len(copies)]))
    for copy in copies:
        copy.start()
    for copy in copies:
        copy.wait()


def swap(value, bit, count):
    return lax.ppermute(value, "dp", [(i, i ^ bit) for i in range(count)])


def exchange(value, bit, count):
    return lax.ppermute(value, "expert", [(i, i ^ bit) for i in range(count)])


def fence(*values):
    leaves, tree = jax.tree.flatten(values)
    return jax.tree.unflatten(tree, lax.optimization_barrier(tuple(leaves)))


def split3(value):
    high = lax.reduce_precision(value, 8, 7)
    rest = value - high
    middle = lax.reduce_precision(rest, 8, 7)
    return [high.astype(BF16), middle.astype(BF16), (rest - middle).astype(BF16)]


def shards(tokens, routes, probs, cotangent, w_gate, w_up, w_down):
    tok_rows, top = routes.shape
    local, width, hidden = w_gate.shape
    n_exp = lax.axis_size("expert")
    n_dp = lax.axis_size("dp")
    experts = local * n_exp
    cap = 5 * tok_rows * top // (4 * experts) * n_exp
    cap_pad = round_up(cap, LANES)
    total = n_exp * tok_rows
    levels = n_exp // 2
    line = levels * tok_rows
    wide = width + LANES
    tile = min(width, 512)
    columns = width // n_dp
    half = width // 2
    far_bit = n_dp // 2
    my_dp = lax.axis_index("dp")
    far = jnp.where((my_dp & far_bit) > 0, 1, 0)
    near = jnp.where((my_dp & 1) > 0, 1, 0)
    near_word = near.astype(jnp.int32).reshape(1)
    far_word = far.astype(jnp.int32).reshape(1)
    first = (lax.axis_index("expert") * local).astype(jnp.int32).reshape(1)
    line_blocks = list(range(0, n_exp, 2))
    sides = [k for k in line_blocks if k & 2 and k > 2]
    folds = [k ^ 2 for k in sides]
    groups = [sides, folds, [2, 0]]
    plan = [[k // 2 for k in group] for group in groups]
    upper_bits = [1 << i for i in range(2, n_exp.bit_length() - 1)]

    def send(value, bit):
        return exchange(value, bit, n_exp)

    def gather_upper(value):
        blocks = {0: value}
        for bit in reversed(upper_bits):
            blocks.update({k | bit: send(block, bit) for k, block in list(blocks.items())})
        return blocks

    any_space = pl.BlockSpec(memory_space=pl.ANY)
    smem = pl.BlockSpec(memory_space=pltpu.SMEM)
    params = pltpu.CompilerParams(dimension_semantics=("arbitrary",), vmem_limit_bytes=VMEM_LIMIT)

    def by_expert(*shape):
        return pl.BlockSpec((1,) + shape, lambda e: (e,) + (0,) * len(shape))

    def whole(*shape):
        return pl.BlockSpec(shape, lambda e: (0,) * len(shape))

    def sds(shape, dtype):
        return jax.ShapeDtypeStruct(shape, dtype)

    def cost(gflop, mbyte):
        return pl.CostEstimate(flops=gflop * 10**6, bytes_accessed=mbyte * 10**3, transcendentals=0)

    def cut_blocks(word, blocks, size, wanted, name):
        plan, rows = [], []
        for out, items in enumerate(wanted):
            rows.append(0)
            for i, flip in items:
                plan.append((i, flip, out, rows[out]))
                rows[out] += blocks[i].shape[0]
        return pl.pallas_call(
            functools.partial(cut_kernel, size, plan),
            in_specs=[smem] + [any_space] * len(blocks),
            out_specs=[pl.BlockSpec(memory_space=pltpu.VMEM)] * len(wanted),
            out_shape=[sds((n, size), BF16) for n in rows],
            scratch_shapes=[pltpu.SemaphoreType.DMA((len(plan),))],
            compiler_params=pltpu.CompilerParams(vmem_limit_bytes=VMEM_LIMIT),
            cost_estimate=cost(0, 2),
            name=name,
        )(word, *blocks)

    def cut_far(blocks, name):
        return cut_blocks(far_word, blocks, width // 2, [[(i, 1) for i in range(len(blocks))]], name)[0]

    by_columns = pl.BlockSpec((local, tile, hidden), lambda j: (0, j, 0))
    weight_spec = by_expert(width, hidden)
    parts = n_exp
    cfg = (parts, local, cap, cap_pad, top)

    totals = jnp.sum(probs, axis=1, keepdims=True)
    share = probs / totals
    meta = jnp.concatenate([routes.astype(BF16)] + split3(share), axis=1)
    meta = jnp.pad(meta, ((0, 0), (0, LANES - 4 * top)))

    x_own = jnp.concatenate([tokens, meta], axis=1)
    x_line = gather_upper(x_own)
    x_line[2] = send(x_own, 2)
    x_pair = {k: send(x_line[k], 1) for k in (0, 2)}
    x_line, x_pair[0], cot = fence(x_line, x_pair[0], cotangent)

    x_line.update({k | 2: send(x_line[k], 2) for k in folds})
    c_line = gather_upper(cot)
    x_pair.update({k: send(x_line[k], 1) for k in folds})
    x_line, c_line, x_pair = fence(x_line, c_line, x_pair)
    x_pair.update({k: send(x_line[k], 1) for k in sides})
    x_far = swap(cut_far([x_line[k] for k in line_blocks], "cut_x"), far_bit, n_dp)
    c_line[2] = send(c_line[0], 2)
    c_line.update({k | 2: send(c_line[k], 2) for k in folds})
    c_pair = {k: send(c_line[k], 1) for k in [0] + folds}
    pre, act, info, pick, combine, x_keep, x_give = pl.pallas_call(
        functools.partial(hidden_kernel, cfg),
        grid=(local,),
        in_specs=[smem] * 2 + [any_space] * parts + [weight_spec] * 2,
        out_specs=[by_expert(cap, 2 * hidden), by_expert(cap, hidden + LANES), by_expert(cap, LANES),
                   whole(local * cap, total), whole(total, local * cap_pad), whole(total, half), whole(line, half)],
        out_shape=[sds((local, cap, 2 * hidden), F32), sds((local, cap, hidden + LANES), BF16),
                   sds((local, cap, LANES), F32), sds((local * cap, total), BF16), sds((total, local * cap_pad), BF16),
                   sds((total, half), BF16), sds((line, half), BF16)],
        scratch_shapes=[
            pltpu.VMEM((total, wide), BF16),
            pltpu.VMEM((local * cap, wide), BF16),
            pltpu.SemaphoreType.DMA((parts,)),
        ],
        compiler_params=params,
        cost_estimate=cost(6, 20),
        name="hidden",
    )(first, far_word, *[x_line[k] for k in line_blocks], *[x_pair[k] for k in line_blocks], w_gate, w_up)
    act, c_line, c_pair, x_far = fence(act, c_line, c_pair, x_far)

    c_pair.update({k: send(c_line[k], 1) for k in [2] + sides})
    x_far_pair = swap(x_give, far_bit, n_dp)
    act_far = swap(act, far_bit, n_dp)
    level_rows = [line] + [len(group) * tok_rows for group in groups]
    level_specs = [whole(rows, width) for rows in level_rows]
    mixed_keep, *mixed_out, c_give = pl.pallas_call(
        functools.partial(mixed_kernel, (plan, levels, local, cap, cap_pad)),
        grid=(width // tile,),
        in_specs=[smem, whole(local, cap, hidden + LANES), whole(total, local * cap_pad), by_columns] + [any_space] * levels,
        out_specs=level_specs + [whole(line, half)],
        out_shape=[sds((rows, width), BF16) for rows in level_rows] + [sds((line, half), BF16)],
        scratch_shapes=[pltpu.VMEM((total, local * hidden), BF16), pltpu.SemaphoreType.DMA((levels,))],
        compiler_params=params,
        cost_estimate=cost(6, 10),
        name="mixed",
    )(far_word, act, combine, w_down, *[c_line[k] for k in line_blocks])
    c_pair, mixed_keep, mixed_out, c_give, x_far_pair = fence(c_pair, mixed_keep, mixed_out, c_give, x_far_pair)

    def back_rows(keep, got):
        return keep.astype(F32) + got.astype(F32)

    def pair_sums(keep, got, group):
        mine = jnp.concatenate([keep[k // 2 * tok_rows:(k // 2 + 1) * tok_rows] for k in group], axis=0)
        return back_rows(mine, got)

    def fold_upper(sums):
        blocks = {k: sums[i * tok_rows:(i + 1) * tok_rows] for i, k in enumerate(folds)}
        landed = []
        for bit in upper_bits:
            for k in [k for k in blocks if k & bit]:
                got = send(blocks.pop(k).astype(BF16), bit)
                if k == bit:
                    landed.append(got)
                else:
                    blocks[k ^ bit] = back_rows(blocks[k ^ bit], got)
        return landed

    def finish(sums, landed):
        return sum([part.astype(F32) for part in landed], sums[tok_rows:].astype(F32))

    mixed_got = [send(part, 1) for part in mixed_out[:2]]
    c_far = swap(c_give, far_bit, n_dp)
    d_gate, d_up, tail, c_keep, c_give = pl.pallas_call(
        functools.partial(grad_kernel, cfg),
        grid=(local,),
        in_specs=[smem] + [any_space] * parts + [whole(local * cap, total), whole(total, local * cap_pad), weight_spec,
                                                 by_expert(cap, 2 * hidden), by_expert(cap, LANES)],
        out_specs=[by_expert(cap, hidden)] * 2 + [whole(total, LANES), whole(total, half), whole(line, half)],
        out_shape=[sds((local, cap, hidden), BF16)] * 2 + [sds((total, LANES), BF16),
                   sds((total, half), BF16), sds((line, half), BF16)],
        scratch_shapes=[
            pltpu.VMEM((total, width), BF16),
            pltpu.VMEM((local * cap, width), BF16),
            pltpu.VMEM((local * cap_pad, LANES), BF16),
            pltpu.SemaphoreType.DMA((parts,)),
        ],
        compiler_params=params,
        cost_estimate=cost(6, 12),
        name="hidden_grads",
    )(far_word, *[c_line[k] for k in line_blocks], *[c_pair[k] for k in line_blocks], pick, combine, w_down, pre, info)
    mixed_sides, mixed_got, mixed_out, d_gate, d_up, tail, c_give, act_far = fence(
        pair_sums(mixed_keep, mixed_got[0], sides).astype(BF16), mixed_got, mixed_out, d_gate, d_up, tail, c_give, act_far)

    mixed_sides = send(mixed_sides, 2)
    mixed_got.append(send(mixed_out[2], 1))
    c_far_pair = swap(c_give, far_bit, n_dp)
    wide_specs = [whole(rows, wide) for rows in level_rows]
    input_keep, *input_out = pl.pallas_call(
        functools.partial(input_kernel, (plan, local, cap, cap_pad)),
        grid=(width // tile,),
        in_specs=[whole(local, cap, hidden)] * 2 + [whole(total, local * cap_pad), whole(total, LANES),
                                                    by_columns, by_columns],
        out_specs=wide_specs,
        out_shape=[sds((rows, wide), BF16) for rows in level_rows],
        scratch_shapes=[pltpu.VMEM((local * cap_pad, tile), BF16)],
        compiler_params=params,
        cost_estimate=cost(6, 16),
        name="input_grads",
    )(d_gate, d_up, combine, tail, w_gate, w_up)
    input_keep, input_out, mixed_sides, mixed_got, c_far, d_gate = fence(
        input_keep, input_out, mixed_sides, mixed_got, c_far, d_gate)

    input_got = [send(part, 1) for part in input_out[:2]]
    mixed_landed = fold_upper(back_rows(pair_sums(mixed_keep, mixed_got[1], folds), mixed_sides))
    gate_far = swap(d_gate, far_bit, n_dp)
    input_sides, input_out, c_far_pair, x_keep, d_up, mixed_got[2] = fence(
        pair_sums(input_keep, input_got[0], sides).astype(BF16), input_out, c_far_pair, x_keep, d_up, mixed_got[2])
    input_sides = send(input_sides, 2)
    input_got.append(send(input_out[2], 1))
    up_far = swap(d_up, far_bit, n_dp)
    mixed_ends = pair_sums(mixed_keep, mixed_got[2], [2, 0])
    partial_specs = [by_expert(columns, hidden)] * 2
    partial_shapes = [sds((local, columns, hidden), BF16)] * 2
    x_rows, down_keep, down_give = pl.pallas_call(
        functools.partial(down_kernel, cap),
        grid=(local,),
        in_specs=[smem, pl.BlockSpec((cap, total), lambda e: (e, 0))] + [whole(total, half), whole(line, half), whole(line, half)] * 2
        + [by_expert(cap, hidden + LANES)] * 2,
        out_specs=[by_expert(2 * cap, half)] + partial_specs,
        out_shape=[sds((local, 2 * cap, half), BF16)] + partial_shapes,
        scratch_shapes=[pltpu.VMEM((2 * cap, half), BF16), pltpu.VMEM((2 * cap, hidden), BF16), pltpu.VMEM((half, hidden), BF16)],
        compiler_params=params,
        cost_estimate=cost(6, 12),
        name="down_grads",
    )(near_word, pick, x_keep, x_far, x_far_pair, c_keep, c_far, c_far_pair, act, act_far)
    input_folds, mixed_landed, x_rows, down_keep, down_give = fence(
        back_rows(pair_sums(input_keep, input_got[1], folds), input_sides).astype(BF16),
        mixed_landed, x_rows, down_keep, down_give)

    input_landed = fold_upper(input_folds)
    mixed_landed.append(send(mixed_ends[:tok_rows].astype(BF16), 2))
    input_ends = pair_sums(input_keep, input_got[2], [2, 0])
    input_landed.append(send(input_ends[:tok_rows].astype(BF16), 2))
    down_got = swap(down_give, 1, n_dp)
    input_ends, input_landed[0], gate_far, up_far = fence(input_ends, input_landed[0], gate_far, up_far)
    both_specs = [by_expert(columns, 2 * hidden)] * 2
    both_keep, both_give = pl.pallas_call(
        functools.partial(both_kernel, cap),
        grid=(local,),
        in_specs=[smem, by_expert(2 * cap, half)] + [by_expert(cap, hidden)] * 4,
        out_specs=both_specs,
        out_shape=[sds((local, columns, 2 * hidden), BF16)] * 2,
        scratch_shapes=[pltpu.VMEM((2 * cap, 2 * hidden), BF16), pltpu.VMEM((half, 2 * hidden), BF16)],
        compiler_params=params,
        cost_estimate=cost(3, 10),
        name="gate_up_grads",
    )(near_word, x_rows, d_gate, gate_far, d_up, up_far)
    both_give, input_landed, mixed_landed = fence(both_give, input_landed, mixed_landed)
    mixed = finish(mixed_ends, mixed_landed).astype(BF16)
    both_got = swap(both_give, 1, n_dp)
    gate_grad = back_rows(both_keep[:, :, :hidden], both_got[:, :, :hidden]).astype(BF16)
    up_grad = back_rows(both_keep[:, :, hidden:], both_got[:, :, hidden:]).astype(BF16)
    gate_grad, up_grad, down_got = fence(gate_grad, up_grad, down_got)
    down_grad = back_rows(down_keep, down_got).astype(BF16)

    back = finish(input_ends, input_landed)
    token_grad = back[:, :width].astype(BF16)
    tail = back[:, width:]
    slot_sg = tail[:, :top] + tail[:, top:2 * top] + tail[:, 2 * top:3 * top]
    prob_grad = (slot_sg - jnp.sum(share * slot_sg, axis=1, keepdims=True)) / totals
    return mixed, token_grad, prob_grad, gate_grad, up_grad, down_grad


def solution(mesh):
    rows = P(("expert", "dp"), None)
    weight = P("expert", None, None)
    grad = P("expert", "dp", None)
    return jax.shard_map(
        shards,
        mesh=mesh,
        in_specs=(rows, rows, rows, rows, weight, weight, weight),
        out_specs=(rows, rows, rows, grad, grad, grad),
        check_vma=False,
    )
```

```python
import functools

import jax
import jax.numpy as jnp
from jax import lax
from jax.experimental import pallas as pl
from jax.experimental.pallas import tpu as pltpu
from jax.sharding import PartitionSpec as P


F32 = jnp.float32
BF16 = jnp.bfloat16
LANES = 128
VMEM_LIMIT = 60 * 1024 * 1024


def round_up(value, unit):
    return -(-value // unit) * unit


def dot(a, b):
    return jnp.dot(a, b, preferred_element_type=F32)


def dot_nt(a, b):
    return lax.dot_general(a, b, (((1,), (1,)), ((), ())), preferred_element_type=F32)


def dot_tn(a, b):
    return lax.dot_general(a, b, (((0,), (0,)), ((), ())), preferred_element_type=F32)


def iota(shape, dim):
    return lax.broadcasted_iota(jnp.int32, shape, dim)


def load_blocks(blocks, held, sems):
    copies, start = [], 0
    for i, block in enumerate(blocks):
        size = block.shape[0]
        copies.append(pltpu.make_async_copy(block, held.at[pl.ds(start, size), :], sems.at[i]))
        start += size
    for copy in copies:
        copy.start()
    for copy in copies:
        copy.wait()


def tiles(width, tile=512):
    return [(start, min(start + tile, width)) for start in range(0, width, tile)]


def half_of(which, width):
    return pl.ds(pl.multiple_of(which * (width // 2), LANES), width // 2)


def hidden_kernel(cfg, first_ref, far_ref, *refs):
    parts, local, cap, cap_pad, top = cfg
    blocks, refs = refs[:parts], refs[parts:]
    gate_ref, up_ref, pre_ref, act_ref, info_ref, pick_ref, combine_ref, keep_ref, give_ref = refs[:9]
    held, rows_ref, sems = refs[9:]
    expert = pl.program_id(0)
    tokens = held.shape[0]
    width, hidden = gate_ref.shape[1:]

    @pl.when(expert == 0)
    def _():
        load_blocks(blocks, held, sems)
        meta = held[:, width:].astype(F32).astype(jnp.int32)
        lane = iota(meta.shape, 1)
        hits = jnp.zeros(meta.shape, F32)
        for i in range(local):
            named = (meta == first_ref[0] + i) & (lane < top)
            hit = jnp.sum(jnp.where(named, 1.0, 0.0), axis=1, keepdims=True)
            hits = hits + jnp.where(lane == i, hit, 0.0)
        step = min(tokens, 256)
        below = (iota((step, step), 0) >= iota((step, step), 1)).astype(F32).astype(BF16)
        carry = jnp.zeros((1, LANES), F32)
        slots = []
        for start in range(0, tokens, step):
            part = hits[start:start + step]
            rank = dot(below, part.astype(BF16)) + carry
            carry = rank[step - 1:step]
            slots.append(jnp.where(part > 0.0, rank - 1.0, -1.0))
        slots = jnp.concatenate(slots, axis=0)
        slots_t = jnp.transpose(slots)
        places = iota((tokens, cap_pad), 1).astype(F32)
        places_t = iota((cap, tokens), 0).astype(F32)
        for i in range(local):
            hit = slots[:, i:i + 1] == places
            combine_ref[:, i * cap_pad:(i + 1) * cap_pad] = jnp.where(hit, 1.0, 0.0).astype(BF16)
            hit = slots_t[i:i + 1, :] == places_t
            pick_ref[i * cap:(i + 1) * cap, :] = jnp.where(hit, 1.0, 0.0).astype(BF16)
        for start, stop in tiles(held.shape[1]):
            rows_ref[:, start:stop] = dot(pick_ref[...], held[:, start:stop]).astype(BF16)
        keep_ref[...] = held[:, half_of(far_ref[0], width)]
        give_ref[...] = held[give_ref.shape[0]:, half_of(1 - far_ref[0], width)]

    here = pl.ds(pl.multiple_of(expert * cap, 16), cap)
    pick = pick_ref[here, :].astype(F32)
    token = jnp.sum(pick * iota(pick.shape, 1).astype(F32), axis=1, keepdims=True)
    token = jnp.where(jnp.sum(pick, axis=1, keepdims=True) > 0.0, token, -128.0).astype(jnp.int32)
    meta = rows_ref[here, width:].astype(F32)
    lane = iota(meta.shape, 1)
    named = (meta.astype(jnp.int32) == first_ref[0] + expert) & (lane < top)
    shares = sum(pltpu.roll(meta, LANES - top * (i + 1), 1) for i in range(3))
    share = jnp.sum(jnp.where(named, shares, 0.0), axis=1, keepdims=True)
    info_ref[0] = jnp.where(lane < top, jnp.where(named, 1.0, 0.0), share)

    rows = rows_ref[here, :width]
    gate_pre = dot(rows, gate_ref[0])
    up_pre = dot(rows, up_ref[0])
    pre_ref[0, :, :hidden] = gate_pre
    pre_ref[0, :, hidden:] = up_pre
    active = gate_pre * jax.nn.sigmoid(gate_pre) * up_pre
    act_ref[0, :, :hidden] = (share * active).astype(BF16)
    token_pair = jnp.where(lane == 0, token >> 7, jnp.where(lane == 1, token & 127, 0))
    act_ref[0, :, hidden:] = token_pair.astype(F32).astype(BF16)


def store_parts(plan, value, here, refs):
    refs[0][:, here] = value[:refs[0].shape[0]]
    line, size = refs[0].shape[0], refs[0].shape[0] // sum(len(items) for items in plan)
    for ref, items in zip(refs[1:], plan):
        for i, block in enumerate(items):
            start = line + block * size
            ref[i * size:(i + 1) * size, here] = value[start:start + size]


def mixed_kernel(cfg, far_ref, act_ref, combine_ref, down_ref, *refs):
    plan, levels, local, cap, cap_pad = cfg
    blocks, refs = refs[:levels], refs[levels:]
    outs, give_ref, spread, sems = refs[:-3], refs[-3], refs[-2], refs[-1]
    size = blocks[0].shape[0]
    here = half_of(1 - far_ref[0], blocks[0].shape[1])
    copies = [pltpu.make_async_copy(block.at[:, here], give_ref.at[pl.ds(i * size, size), :], sems.at[i])
              for i, block in enumerate(blocks)]
    hidden = down_ref.shape[2]
    tile = down_ref.shape[1]
    step = pl.program_id(0)

    @pl.when(step == 0)
    def _():
        for copy in copies:
            copy.start()
        for e in range(local):
            here = combine_ref[:, e * cap_pad:e * cap_pad + cap]
            spread[:, e * hidden:(e + 1) * hidden] = dot(here, act_ref[e, :, :hidden]).astype(BF16)

    total = dot_nt(spread[:, :hidden], down_ref[0])
    for e in range(1, local):
        total = total + dot_nt(spread[:, e * hidden:(e + 1) * hidden], down_ref[e])
    store_parts(plan, total.astype(BF16), pl.ds(pl.multiple_of(step * tile, tile), tile), outs)

    @pl.when(step == pl.num_programs(0) - 1)
    def _():
        for copy in copies:
            copy.wait()


def grad_kernel(cfg, far_ref, *refs):
    parts, local, cap, cap_pad, top = cfg
    blocks, refs = refs[:parts], refs[parts:]
    pick_ref, combine_ref, down_ref, pre_ref, info_ref, d_gate_ref, d_up_ref, tail_ref, keep_ref, give_ref = refs[:10]
    held, rows_ref, tails, sems = refs[10:]
    expert = pl.program_id(0)
    hidden = down_ref.shape[2]

    @pl.when(expert == 0)
    def _():
        load_blocks(blocks, held, sems)
        tails[...] = jnp.zeros(tails.shape, BF16)
        for start, stop in tiles(held.shape[1]):
            rows_ref[:, start:stop] = dot(pick_ref[...], held[:, start:stop]).astype(BF16)
        width = held.shape[1]
        keep_ref[...] = held[:, half_of(far_ref[0], width)]
        give_ref[...] = held[give_ref.shape[0]:, half_of(1 - far_ref[0], width)]

    info = info_ref[0]
    lane = iota(info.shape, 1)
    share = info[:, top:top + 1]
    gate_pre, up_pre = pre_ref[0, :, :hidden], pre_ref[0, :, hidden:]
    sig = jax.nn.sigmoid(gate_pre)
    silu = gate_pre * sig
    d_raw = dot(rows_ref[pl.ds(pl.multiple_of(expert * cap, 16), cap), :], down_ref[0])
    share_grad = jnp.sum(silu * up_pre * d_raw, axis=1, keepdims=True)
    d_active = share * d_raw
    d_gate_ref[0] = (d_active * up_pre * sig * (1.0 + gate_pre * (1.0 - sig))).astype(BF16)
    d_up_ref[0] = (d_active * silu).astype(BF16)
    placed = jnp.where((lane < top) & (info > 0.0), share_grad, 0.0)
    high = placed.astype(BF16)
    rest = placed - high.astype(F32)
    middle = rest.astype(BF16)
    low = (rest - middle.astype(F32)).astype(BF16)
    tail = high.astype(F32) + pltpu.roll(middle.astype(F32), top, 1) + pltpu.roll(low.astype(F32), 2 * top, 1)
    tails[pl.ds(pl.multiple_of(expert * cap_pad, cap_pad), cap), :] = tail.astype(BF16)

    @pl.when(expert == local - 1)
    def _():
        tail_ref[...] = dot(combine_ref[...], tails[...]).astype(BF16)


def input_kernel(cfg, d_gate_ref, d_up_ref, combine_ref, tail_ref, gate_ref, up_ref, *refs):
    plan, local, cap, cap_pad = cfg
    outs, rows = refs[:-1], refs[-1]
    tile, hidden = gate_ref.shape[1:]
    step = pl.program_id(0)

    @pl.when(step == 0)
    def _():
        rows[...] = jnp.zeros(rows.shape, BF16)
        width = outs[0].shape[1] - LANES
        store_parts(plan, tail_ref[...], slice(width, width + LANES), outs)

    for e in range(local):
        part = dot_nt(d_gate_ref[e], gate_ref[e]) + dot_nt(d_up_ref[e], up_ref[e])
        rows[e * cap_pad:e * cap_pad + cap, :] = part.astype(BF16)
    total = dot(combine_ref[...], rows[...]).astype(BF16)
    store_parts(plan, total, pl.ds(pl.multiple_of(step * tile, tile), tile), outs)


def store_halves(part, near_ref, both, keep_ref, give_ref):
    both[...] = part.astype(BF16)
    size = keep_ref.shape[1]
    keep_ref[0] = both[pl.ds(pl.multiple_of(near_ref[0] * size, 16), size), :]
    give_ref[0] = both[pl.ds(pl.multiple_of((1 - near_ref[0]) * size, 16), size), :]


def down_kernel(cap, near_ref, pick_ref, *refs):
    x_refs, c_refs, (act_ref, act_far_ref, rows_ref, keep_ref, give_ref, c_rows, acts, both) = refs[:3], refs[3:6], refs[6:]
    hidden = acts.shape[1]
    line = x_refs[1].shape[0]
    acts[:cap, :] = act_ref[0, :, :hidden]
    acts[cap:, :] = act_far_ref[0, :, :hidden]
    pair = act_far_ref[0, :, hidden:].astype(F32)
    token = pair[:, 0:1] * 128.0 + pair[:, 1:2]
    pick = pick_ref[...]
    pick_far = jnp.where(token == iota(pick.shape, 1).astype(F32), 1.0, 0.0).astype(BF16)
    for (own, far, far_pair), rows in ((x_refs, rows_ref.at[0]), (c_refs, c_rows)):
        rows[:cap, :] = dot(pick, own[...]).astype(BF16)
        rows[cap:, :] = (dot(pick_far[:, :line], far[...]) + dot(pick_far[:, line:], far_pair[...])).astype(BF16)
    store_halves(dot_tn(c_rows[...], acts[...]), near_ref, both, keep_ref, give_ref)


def both_kernel(cap, near_ref, rows_ref, d_gate_ref, gate_far_ref, d_up_ref, up_far_ref, keep_ref, give_ref, grads, both):
    hidden = d_gate_ref.shape[2]
    grads[:cap, :hidden] = d_gate_ref[0]
    grads[cap:, :hidden] = gate_far_ref[0]
    grads[:cap, hidden:] = d_up_ref[0]
    grads[cap:, hidden:] = up_far_ref[0]
    store_halves(dot_tn(rows_ref[0], grads[...]), near_ref, both, keep_ref, give_ref)


def cut_kernel(half, plan, word_ref, *refs):
    count = 1 + max(i for i, _, _, _ in plan)
    blocks, outs, sems = refs[:count], refs[count:-1], refs[-1]
    copies = []
    for i, flip, out, row in plan:
        which = 1 - word_ref[0] if flip else word_ref[0]
        here = pl.ds(pl.multiple_of(which * half, LANES), half)
        there = outs[out].at[pl.ds(row, blocks[i].shape[0]), :]
        copies.append(pltpu.make_async_copy(blocks[i].at[:, here], there, sems.at[len(copies)]))
    for copy in copies:
        copy.start()
    for copy in copies:
        copy.wait()


def swap(value, bit, count):
    return lax.ppermute(value, "dp", [(i, i ^ bit) for i in range(count)])


def exchange(value, bit, count):
    return lax.ppermute(value, "expert", [(i, i ^ bit) for i in range(count)])


def fence(*values):
    leaves, tree = jax.tree.flatten(values)
    return jax.tree.unflatten(tree, lax.optimization_barrier(tuple(leaves)))


def split3(value):
    high = lax.reduce_precision(value, 8, 7)
    rest = value - high
    middle = lax.reduce_precision(rest, 8, 7)
    return [high.astype(BF16), middle.astype(BF16), (rest - middle).astype(BF16)]


def shards(tokens, routes, probs, cotangent, w_gate, w_up, w_down):
    tok_rows, top = routes.shape
    local, width, hidden = w_gate.shape
    n_exp = lax.axis_size("expert")
    n_dp = lax.axis_size("dp")
    experts = local * n_exp
    cap = 5 * tok_rows * top // (4 * experts) * n_exp
    cap_pad = round_up(cap, LANES)
    total = n_exp * tok_rows
    levels = n_exp // 2
    line = levels * tok_rows
    wide = width + LANES
    tile = min(width, 512)
    columns = width // n_dp
    half = width // 2
    far_bit = n_dp // 2
    my_dp = lax.axis_index("dp")
    far = jnp.where((my_dp & far_bit) > 0, 1, 0)
    near = jnp.where((my_dp & 1) > 0, 1, 0)
    near_word = near.astype(jnp.int32).reshape(1)
    far_word = far.astype(jnp.int32).reshape(1)
    first = (lax.axis_index("expert") * local).astype(jnp.int32).reshape(1)
    line_blocks = list(range(0, n_exp, 2))
    sides = [k for k in line_blocks if k & 2 and k > 2]
    folds = [k ^ 2 for k in sides]
    groups = [sides, folds, [2, 0]]
    plan = [[k // 2 for k in group] for group in groups]
    upper_bits = [1 << i for i in range(2, n_exp.bit_length() - 1)]

    def send(value, bit):
        return exchange(value, bit, n_exp)

    def gather_upper(value):
        blocks = {0: value}
        for bit in reversed(upper_bits):
            blocks.update({k | bit: send(block, bit) for k, block in list(blocks.items())})
        return blocks

    any_space = pl.BlockSpec(memory_space=pl.ANY)
    smem = pl.BlockSpec(memory_space=pltpu.SMEM)
    params = pltpu.CompilerParams(dimension_semantics=("arbitrary",), vmem_limit_bytes=VMEM_LIMIT)

    def by_expert(*shape):
        return pl.BlockSpec((1,) + shape, lambda e: (e,) + (0,) * len(shape))

    def whole(*shape):
        return pl.BlockSpec(shape, lambda e: (0,) * len(shape))

    def sds(shape, dtype):
        return jax.ShapeDtypeStruct(shape, dtype)

    def cost(gflop, mbyte):
        return pl.CostEstimate(flops=gflop * 10**6, bytes_accessed=mbyte * 10**3, transcendentals=0)

    def cut_blocks(word, blocks, size, wanted, name):
        plan, rows = [], []
        for out, items in enumerate(wanted):
            rows.append(0)
            for i, flip in items:
                plan.append((i, flip, out, rows[out]))
                rows[out] += blocks[i].shape[0]
        return pl.pallas_call(
            functools.partial(cut_kernel, size, plan),
            in_specs=[smem] + [any_space] * len(blocks),
            out_specs=[pl.BlockSpec(memory_space=pltpu.VMEM)] * len(wanted),
            out_shape=[sds((n, size), BF16) for n in rows],
            scratch_shapes=[pltpu.SemaphoreType.DMA((len(plan),))],
            compiler_params=pltpu.CompilerParams(vmem_limit_bytes=VMEM_LIMIT),
            cost_estimate=cost(0, 2),
            name=name,
        )(word, *blocks)

    def cut_far(blocks, name):
        return cut_blocks(far_word, blocks, width // 2, [[(i, 1) for i in range(len(blocks))]], name)[0]

    by_columns = pl.BlockSpec((local, tile, hidden), lambda j: (0, j, 0))
    weight_spec = by_expert(width, hidden)
    parts = n_exp
    cfg = (parts, local, cap, cap_pad, top)

    totals = jnp.sum(probs, axis=1, keepdims=True)
    share = probs / totals
    meta = jnp.concatenate([routes.astype(BF16)] + split3(share), axis=1)
    meta = jnp.pad(meta, ((0, 0), (0, LANES - 4 * top)))

    x_own = jnp.concatenate([tokens, meta], axis=1)
    x_line = gather_upper(x_own)
    x_line[2] = send(x_own, 2)
    x_pair = {k: send(x_line[k], 1) for k in (0, 2)}
    x_line, x_pair[0], cot = fence(x_line, x_pair[0], cotangent)

    x_line.update({k | 2: send(x_line[k], 2) for k in folds})
    c_line = gather_upper(cot)
    x_pair.update({k: send(x_line[k], 1) for k in folds})
    x_line, c_line, x_pair = fence(x_line, c_line, x_pair)
    x_pair.update({k: send(x_line[k], 1) for k in sides})
    x_far = swap(cut_far([x_line[k] for k in line_blocks], "cut_x"), far_bit, n_dp)
    c_line[2] = send(c_line[0], 2)
    c_line.update({k | 2: send(c_line[k], 2) for k in folds})
    c_pair = {k: send(c_line[k], 1) for k in [0] + folds}
    pre, act, info, pick, combine, x_keep, x_give = pl.pallas_call(
        functools.partial(hidden_kernel, cfg),
        grid=(local,),
        in_specs=[smem] * 2 + [any_space] * parts + [weight_spec] * 2,
        out_specs=[by_expert(cap, 2 * hidden), by_expert(cap, hidden + LANES), by_expert(cap, LANES),
                   whole(local * cap, total), whole(total, local * cap_pad), whole(total, half), whole(line, half)],
        out_shape=[sds((local, cap, 2 * hidden), F32), sds((local, cap, hidden + LANES), BF16),
                   sds((local, cap, LANES), F32), sds((local * cap, total), BF16), sds((total, local * cap_pad), BF16),
                   sds((total, half), BF16), sds((line, half), BF16)],
        scratch_shapes=[
            pltpu.VMEM((total, wide), BF16),
            pltpu.VMEM((local * cap, wide), BF16),
            pltpu.SemaphoreType.DMA((parts,)),
        ],
        compiler_params=params,
        cost_estimate=cost(6, 20),
        name="hidden",
    )(first, far_word, *[x_line[k] for k in line_blocks], *[x_pair[k] for k in line_blocks], w_gate, w_up)
    act, c_line, c_pair, x_far = fence(act, c_line, c_pair, x_far)

    c_pair.update({k: send(c_line[k], 1) for k in [2] + sides})
    x_far_pair = swap(x_give, far_bit, n_dp)
    act_far = swap(act, far_bit, n_dp)
    level_rows = [line] + [len(group) * tok_rows for group in groups]
    level_specs = [whole(rows, width) for rows in level_rows]
    mixed_keep, *mixed_out, c_give = pl.pallas_call(
        functools.partial(mixed_kernel, (plan, levels, local, cap, cap_pad)),
        grid=(width // tile,),
        in_specs=[smem, whole(local, cap, hidden + LANES), whole(total, local * cap_pad), by_columns] + [any_space] * levels,
        out_specs=level_specs + [whole(line, half)],
        out_shape=[sds((rows, width), BF16) for rows in level_rows] + [sds((line, half), BF16)],
        scratch_shapes=[pltpu.VMEM((total, local * hidden), BF16), pltpu.SemaphoreType.DMA((levels,))],
        compiler_params=params,
        cost_estimate=cost(6, 10),
        name="mixed",
    )(far_word, act, combine, w_down, *[c_line[k] for k in line_blocks])
    c_pair, mixed_keep, mixed_out, c_give, x_far_pair = fence(c_pair, mixed_keep, mixed_out, c_give, x_far_pair)

    def back_rows(keep, got):
        return keep.astype(F32) + got.astype(F32)

    def pair_sums(keep, got, group):
        mine = jnp.concatenate([keep[k // 2 * tok_rows:(k // 2 + 1) * tok_rows] for k in group], axis=0)
        return back_rows(mine, got)

    def fold_upper(sums):
        blocks = {k: sums[i * tok_rows:(i + 1) * tok_rows] for i, k in enumerate(folds)}
        landed = []
        for bit in upper_bits:
            for k in [k for k in blocks if k & bit]:
                got = send(blocks.pop(k).astype(BF16), bit)
                if k == bit:
                    landed.append(got)
                else:
                    blocks[k ^ bit] = back_rows(blocks[k ^ bit], got)
        return landed

    def finish(sums, landed):
        return sum([part.astype(F32) for part in landed], sums[tok_rows:].astype(F32))

    mixed_got = [send(part, 1) for part in mixed_out[:2]]
    c_far = swap(c_give, far_bit, n_dp)
    d_gate, d_up, tail, c_keep, c_give = pl.pallas_call(
        functools.partial(grad_kernel, cfg),
        grid=(local,),
        in_specs=[smem] + [any_space] * parts + [whole(local * cap, total), whole(total, local * cap_pad), weight_spec,
                                                 by_expert(cap, 2 * hidden), by_expert(cap, LANES)],
        out_specs=[by_expert(cap, hidden)] * 2 + [whole(total, LANES), whole(total, half), whole(line, half)],
        out_shape=[sds((local, cap, hidden), BF16)] * 2 + [sds((total, LANES), BF16),
                   sds((total, half), BF16), sds((line, half), BF16)],
        scratch_shapes=[
            pltpu.VMEM((total, width), BF16),
            pltpu.VMEM((local * cap, width), BF16),
            pltpu.VMEM((local * cap_pad, LANES), BF16),
            pltpu.SemaphoreType.DMA((parts,)),
        ],
        compiler_params=params,
        cost_estimate=cost(6, 12),
        name="hidden_grads",
    )(far_word, *[c_line[k] for k in line_blocks], *[c_pair[k] for k in line_blocks], pick, combine, w_down, pre, info)
    mixed_sides, mixed_got, mixed_out, d_gate, d_up, tail, c_give = fence(
        pair_sums(mixed_keep, mixed_got[0], sides).astype(BF16), mixed_got, mixed_out, d_gate, d_up, tail, c_give)

    mixed_sides = send(mixed_sides, 2)
    mixed_got.append(send(mixed_out[2], 1))
    c_far_pair = swap(c_give, far_bit, n_dp)
    wide_specs = [whole(rows, wide) for rows in level_rows]
    input_keep, *input_out = pl.pallas_call(
        functools.partial(input_kernel, (plan, local, cap, cap_pad)),
        grid=(width // tile,),
        in_specs=[whole(local, cap, hidden)] * 2 + [whole(total, local * cap_pad), whole(total, LANES),
                                                    by_columns, by_columns],
        out_specs=wide_specs,
        out_shape=[sds((rows, wide), BF16) for rows in level_rows],
        scratch_shapes=[pltpu.VMEM((local * cap_pad, tile), BF16)],
        compiler_params=params,
        cost_estimate=cost(6, 16),
        name="input_grads",
    )(d_gate, d_up, combine, tail, w_gate, w_up)
    input_keep, input_out, mixed_sides, mixed_got, c_far, act_far, d_gate = fence(
        input_keep, input_out, mixed_sides, mixed_got, c_far, act_far, d_gate)

    input_got = [send(part, 1) for part in input_out[:2]]
    mixed_landed = fold_upper(back_rows(pair_sums(mixed_keep, mixed_got[1], folds), mixed_sides))
    gate_far = swap(d_gate, far_bit, n_dp)
    input_sides, input_out, c_far_pair, x_keep, d_up, mixed_got[2] = fence(
        pair_sums(input_keep, input_got[0], sides).astype(BF16), input_out, c_far_pair, x_keep, d_up, mixed_got[2])
    input_sides = send(input_sides, 2)
    input_got.append(send(input_out[2], 1))
    up_far = swap(d_up, far_bit, n_dp)
    mixed_ends = pair_sums(mixed_keep, mixed_got[2], [2, 0])
    partial_specs = [by_expert(columns, hidden)] * 2
    partial_shapes = [sds((local, columns, hidden), BF16)] * 2
    x_rows, down_keep, down_give = pl.pallas_call(
        functools.partial(down_kernel, cap),
        grid=(local,),
        in_specs=[smem, pl.BlockSpec((cap, total), lambda e: (e, 0))] + [whole(total, half), whole(line, half), whole(line, half)] * 2
        + [by_expert(cap, hidden + LANES)] * 2,
        out_specs=[by_expert(2 * cap, half)] + partial_specs,
        out_shape=[sds((local, 2 * cap, half), BF16)] + partial_shapes,
        scratch_shapes=[pltpu.VMEM((2 * cap, half), BF16), pltpu.VMEM((2 * cap, hidden), BF16), pltpu.VMEM((half, hidden), BF16)],
        compiler_params=params,
        cost_estimate=cost(6, 12),
        name="down_grads",
    )(near_word, pick, x_keep, x_far, x_far_pair, c_keep, c_far, c_far_pair, act, act_far)
    input_folds, mixed_landed, x_rows, down_keep, down_give = fence(
        back_rows(pair_sums(input_keep, input_got[1], folds), input_sides).astype(BF16),
        mixed_landed, x_rows, down_keep, down_give)

    input_landed = fold_upper(input_folds)
    mixed_landed.append(send(mixed_ends[:tok_rows].astype(BF16), 2))
    input_ends = pair_sums(input_keep, input_got[2], [2, 0])
    input_landed.append(send(input_ends[:tok_rows].astype(BF16), 2))
    down_got = swap(down_give, 1, n_dp)
    mixed = finish(mixed_ends, mixed_landed).astype(BF16)
    mixed, input_ends, input_landed[0], gate_far, up_far = fence(
        mixed, input_ends, input_landed[0], gate_far, up_far)
    both_specs = [by_expert(columns, 2 * hidden)] * 2
    both_keep, both_give = pl.pallas_call(
        functools.partial(both_kernel, cap),
        grid=(local,),
        in_specs=[smem, by_expert(2 * cap, half)] + [by_expert(cap, hidden)] * 4,
        out_specs=both_specs,
        out_shape=[sds((local, columns, 2 * hidden), BF16)] * 2,
        scratch_shapes=[pltpu.VMEM((2 * cap, 2 * hidden), BF16), pltpu.VMEM((half, 2 * hidden), BF16)],
        compiler_params=params,
        cost_estimate=cost(3, 10),
        name="gate_up_grads",
    )(near_word, x_rows, d_gate, gate_far, d_up, up_far)
    both_give, input_landed = fence(both_give, input_landed)
    both_got = swap(both_give, 1, n_dp)
    gate_grad = back_rows(both_keep[:, :, :hidden], both_got[:, :, :hidden]).astype(BF16)
    up_grad = back_rows(both_keep[:, :, hidden:], both_got[:, :, hidden:]).astype(BF16)
    gate_grad, up_grad, down_got = fence(gate_grad, up_grad, down_got)
    down_grad = back_rows(down_keep, down_got).astype(BF16)

    back = finish(input_ends, input_landed)
    token_grad = back[:, :width].astype(BF16)
    tail = back[:, width:]
    slot_sg = tail[:, :top] + tail[:, top:2 * top] + tail[:, 2 * top:3 * top]
    prob_grad = (slot_sg - jnp.sum(share * slot_sg, axis=1, keepdims=True)) / totals
    return mixed, token_grad, prob_grad, gate_grad, up_grad, down_grad


def solution(mesh):
    rows = P(("expert", "dp"), None)
    weight = P("expert", None, None)
    grad = P("expert", "dp", None)
    return jax.shard_map(
        shards,
        mesh=mesh,
        in_specs=(rows, rows, rows, rows, weight, weight, weight),
        out_specs=(rows, rows, rows, grad, grad, grad),
        check_vma=False,
    )
```
